256 devices in a mesh: dp: 4 (over y_lo, core), px: 8 (over x, y_hi), py: 8 (over z).
Axes of the slice: x: 4, y: 4 (y_hi: 2, y_lo: 2; y = y_hi * 2 + y_lo), z: 8, core: 2. Of those that a mesh axis runs over, the one named last changes fastest.
Arguments:
- state_field: bfloat16 [4, 64, 64, 32, 384], P('dp', 'px', 'py'), may hold values from -6 to 6
- cotangent: bfloat16 [4, 64, 64, 32, 384], P('dp', 'px', 'py'), may hold values from -6 to 6
- first_weight: float32 [2, 4, 96, 96], replicated, may hold values from -0.4375 to 0.4375
- first_bias: float32 [2, 4, 96], replicated, may hold values from -3 to 3
- second_weight: float32 [2, 4, 96, 96], replicated, may hold values from -0.4375 to 0.4375
- second_bias: float32 [2, 4, 96], replicated, may hold values from -3 to 3
Outputs:
- state_grad: bfloat16 [4, 64, 64, 32, 384], P('dp', 'px', 'py')
- first_weight_grad: float32 [2, 4, 96, 96], replicated
- first_bias_grad: float32 [2, 4, 96], replicated
- second_weight_grad: float32 [2, 4, 96, 96], replicated
- second_bias_grad: float32 [2, 4, 96], replicated
The draws below stay inside these ranges and needn't reach their ends.
All inputs are finite; a program needn't handle non-finite values.
Results may differ from the reference program's by a relative error of at most 0.001.
Values sent between devices are 32-bit elements; how exact they have to be, the bound alone decides.
No kernel may reach another device: no remote copies, remote signals or barrier semaphores. Data moves between devices by JAX's collectives and lax.ppermute only.
A program may use at most 128 MiB of HBM per device.

```python
import math
import jax
import jax.numpy as jnp
from jax import lax

NX = 64
NY = 64
NZ = 32
NB = 4
BS = 96
KZ = 16
C = 384
SAMPLES = 4


def steps_of(stream_key, shape, split, least, largest):
    def one(dim, blocks):
        heights = jax.random.uniform(jax.random.fold_in(jax.random.fold_in(stream_key, 6), dim), (blocks,), jnp.float32, least / len(split), largest / len(split))
        return jnp.repeat(jnp.exp(heights), shape[dim] // blocks).reshape((-1,) + (1,) * (len(shape) - dim - 1))

    gain = one(*split[0])
    for cut in split[1:]:
        gain = gain * one(*cut)
    return gain


def noise(key, shape, deviation, reach, pieces=(), held_as=jnp.bfloat16):
    gain = steps_of(key, shape, pieces, -0.22, 0.18) if pieces else 1.0
    entries = jax.random.normal(key, shape, jnp.float32) * deviation * gain
    return jnp.minimum(jnp.maximum(entries, -reach), reach).astype(held_as)


def setup_inputs(seed: int = 0) -> dict:
    seeds = jax.random.split(jax.random.key(seed), 7)
    state_field = noise(seeds[0], (SAMPLES, NX, NY, NZ, C), 1.0, 6.0, ((0, 4), (1, 8), (2, 8)))
    cotangent = noise(seeds[1], (SAMPLES, NX, NY, NZ, C), 1.0, 6.0, ((0, 4), (1, 8), (2, 8)))
    first_weight = noise(seeds[2], (2, NB, BS, BS), (2 * BS) ** -0.5, 0.4375, (), jnp.float32)
    first_bias = noise(seeds[3], (2, NB, BS), 0.5, 3.0, (), jnp.float32)
    second_weight = noise(seeds[4], (2, NB, BS, BS), (2 * BS) ** -0.5, 0.4375, (), jnp.float32)
    second_bias = noise(seeds[5], (2, NB, BS), 0.5, 3.0, (), jnp.float32)
    return {"state_field": state_field, "cotangent": cotangent, "first_weight": first_weight, "first_bias": first_bias, "second_weight": second_weight, "second_bias": second_bias}


shrink_level = 0.25
highest = lax.Precision.HIGHEST

def pair_table(weight):
    real_part = weight[0]
    imag_part = weight[1]
    upper_half = jnp.stack([real_part, imag_part], axis=2)
    lower_half = jnp.stack([-imag_part, real_part], axis=2)
    return jnp.stack([upper_half, lower_half], axis=0)

def fold_pairs(pair_grads):
    return jnp.stack([pair_grads[0, :, :, 0] + pair_grads[1, :, :, 1], pair_grads[0, :, :, 1] - pair_grads[1, :, :, 0]])

def contract(pattern, left_side, right_side):
    return jnp.einsum(pattern, left_side, right_side, precision=highest, preferred_element_type=jnp.float32)

def spectrum_of(field_values):
    full_spectrum = jnp.fft.rfftn(field_values, axes=(0, 1, 2), norm='ortho')[:, :, :KZ, :]
    return jnp.stack([jnp.real(full_spectrum), jnp.imag(full_spectrum)])

def field_of(spectral):
    kz_ids = jnp.arange(KZ, dtype=jnp.int32)
    halving = jnp.where(kz_ids == 0, 1.0, 0.5).astype(spectral.dtype)[:, None]
    values = lax.complex(spectral[0] * halving, spectral[1] * halving)
    padding = jnp.zeros((NX, NY, NZ // 2 + 1 - KZ, NB * BS), values.dtype)
    padded = jnp.concatenate([values, padding], axis=2)
    return jnp.fft.irfftn(padded, s=(NX, NY, NZ), axes=(0, 1, 2), norm='ortho')

def reference(state_field, cotangent, first_weight, first_bias, second_weight, second_bias):
    first_table = pair_table(first_weight)
    second_table = pair_table(second_weight)
    kz_ids = jnp.arange(KZ, dtype=jnp.int32)
    doubling = jnp.where(kz_ids == 0, 1.0, 2.0).astype(jnp.float32)[:, None]

    def one_sample(totals, inputs):
        sample_field, sample_cotangent = inputs
        spectral_full = spectrum_of(sample_field.astype(jnp.float32))
        shape_full = spectral_full.shape
        spectral_in = spectral_full.reshape(2, -1, NB, BS)
        gradient_in = (spectrum_of(sample_cotangent.astype(jnp.float32)) * doubling).reshape(2, -1, NB, BS)
        pre_one = contract('rfbi,rbiqo->qfbo', spectral_in, first_table) + first_bias[:, None]
        outer_one, gelu_back = jax.vjp(jax.nn.gelu, pre_one)
        pre_two = contract('rfbi,rbiqo->qfbo', outer_one, second_table) + second_bias[:, None]
        grad_two = gradient_in * jnp.tanh(pre_two / shrink_level) ** 2
        table_two = contract('rfbi,qfbo->rbiqo', outer_one, grad_two)
        grad_outer = contract('qfbo,rbiqo->rfbi', grad_two, second_table)
        grad_one = gelu_back(grad_outer)[0]
        table_one = contract('rfbi,qfbo->rbiqo', spectral_in, grad_one)
        grad_spec = contract('qfbo,rbiqo->rfbi', grad_one, first_table)
        spatial = field_of(grad_spec.reshape(shape_full))
        state_grad = (sample_cotangent.astype(jnp.float32) + spatial).astype(jnp.bfloat16)
        totals = (totals[0] + fold_pairs(table_one), totals[1] + lax.optimization_barrier(jnp.sum(grad_one, axis=1)), totals[2] + fold_pairs(table_two), totals[3] + lax.optimization_barrier(jnp.sum(grad_two, axis=1)))
        return (totals, state_grad)
    zeros_weight = jnp.zeros((2, NB, BS, BS), jnp.float32)
    zeros_bias = jnp.zeros((2, NB, BS), jnp.float32)
    totals, state_grad = lax.scan(one_sample, (zeros_weight, zeros_bias, zeros_weight, zeros_bias), (state_field, cotangent))
    norm_factor = 1.0 / math.sqrt(SAMPLES * NX * NY * KZ)
    return (state_grad, totals[0] * norm_factor, totals[1] * norm_factor, totals[2] * norm_factor, totals[3] * norm_factor)
```

```python
import math

import jax
import jax.numpy as jnp
import ml_dtypes
import numpy as np
from jax import lax
from jax.experimental import pallas as pl
from jax.experimental.pallas import tpu as pltpu
from jax.sharding import PartitionSpec as P

NX = 64
NY = 64
NZ = 32
NB = 4
BS = 96
KZ = 16
C = 384
HALF = BS // 2
CELLS = 64
GROUPS = 16
WIDE = 256
PIECE = 640
SHRINK = 0.25
f32 = jnp.float32
bf16 = jnp.bfloat16
BIG = pltpu.CompilerParams(vmem_limit_bytes=56 * 1024 * 1024)
SPECTRAL = jax.ShapeDtypeStruct((64, 2, HALF, 128), f32)
GROUPED = jax.ShapeDtypeStruct((GROUPS, 2 * BS, WIDE), f32)


def np_split(table):
    high = table.astype(np.float32).astype(ml_dtypes.bfloat16)
    low = (table - high.astype(np.float64)).astype(np.float32).astype(ml_dtypes.bfloat16)
    return high, low


def depth_tables():
    k = np.arange(KZ)[:, None]
    z = np.arange(NZ)[None, :]
    angle = 2.0 * np.pi * (k * z % NZ) / NZ
    scale = 1.0 / math.sqrt(NX * NY * NZ)
    pair = np.stack([np.cos(angle), -np.sin(angle)], axis=1) * scale
    eye = np.eye(8)
    forward = np.einsum("kqz,ab->kqabz", pair, eye).reshape(256, 256)
    return np_split(forward), np_split(forward.T.copy())


def plane_tables():
    j = np.arange(8)
    eight = np.exp(-2j * np.pi * np.outer(j, j) / 8.0)
    both = np.einsum("xk,yl->xykl", eight, eight).reshape(64, 64)
    real = np.zeros((2, 64, 2, 64))
    real[0, :, 0] = both.real
    real[0, :, 1] = both.imag
    real[1, :, 0] = -both.imag
    real[1, :, 1] = both.real
    eye = np.eye(2)
    forward = np.einsum("qxpf,kl,cd->kqcxpdlf", real, eye, eye).reshape(512, 512)
    return np_split(forward), np_split(forward.T.copy())


def twiddle_table():
    k2 = np.arange(8)
    j = np.arange(8)
    one = np.exp(-2j * np.pi * np.outer(k2, j) / 64.0)
    both = np.einsum("kx,ly->klxy", one, one).reshape(64, 64)
    both = np.tile(both, (1, 2))
    return np.stack([both.real, both.imag], axis=1).astype(np.float32)


def split(value):
    high = value.astype(bf16)
    low = (value - high.astype(f32)).astype(bf16)
    return high, low


def dot(left, right, dims=((1,), (0,))):
    return lax.dot_general(left, right, (dims, ((), ())), preferred_element_type=f32)


def dot3(left, right, dims=((1,), (0,))):
    return (
        dot(left[0], right[0], dims) + dot(left[0], right[1], dims) + dot(left[1], right[0], dims)
    )


def fft(re, im, sign):
    n = len(re)
    if n == 1:
        return re, im
    even_re, even_im = fft(re[0::2], im[0::2], sign)
    odd_re, odd_im = fft(re[1::2], im[1::2], sign)
    out_re = [None] * n
    out_im = [None] * n
    root = math.sqrt(0.5)
    for k in range(n // 2):
        a, b = odd_re[k], odd_im[k]
        turn = k * (8 // n)
        if turn == 1:
            a, b = (a - sign * b) * root, (b + sign * a) * root
        elif turn == 2:
            a, b = -sign * b, sign * a
        elif turn == 3:
            a, b = (-a - sign * b) * root, (-b + sign * a) * root
        out_re[k], out_im[k] = even_re[k] + a, even_im[k] + b
        out_re[k + n // 2], out_im[k + n // 2] = even_re[k] - a, even_im[k] - b
    return out_re, out_im


def plane_stage_one(src_ref, dst_ref, sign):
    def body(p, carry):
        for tile in range(HALF // 8):
            rows = slice(tile * 8, tile * 8 + 8)
            re = [src_ref[p * 8 + n, 0, rows, :] for n in range(8)]
            im = [src_ref[p * 8 + n, 1, rows, :] for n in range(8)]
            re, im = fft(re, im, sign)
            for n in range(8):
                dst_ref[p * 8 + n, 0, rows, :] = re[n]
                dst_ref[p * 8 + n, 1, rows, :] = im[n]
        return carry

    lax.fori_loop(0, 8, body, 0)


def plane_forward(src_ref, work_ref, twiddle_ref):
    plane_stage_one(src_ref, work_ref, -1.0)

    def body(p, carry):
        for tile in range(HALF // 8):
            rows = slice(tile * 8, tile * 8 + 8)
            re = [work_ref[n * 8 + p, 0, rows, :] for n in range(8)]
            im = [work_ref[n * 8 + p, 1, rows, :] for n in range(8)]
            re, im = fft(re, im, -1.0)
            for n in range(8):
                c = twiddle_ref[n * 8 + p, 0:1, :]
                s = twiddle_ref[n * 8 + p, 1:2, :]
                work_ref[n * 8 + p, 0, rows, :] = re[n] * c - im[n] * s
                work_ref[n * 8 + p, 1, rows, :] = re[n] * s + im[n] * c
        return carry

    lax.fori_loop(0, 8, body, 0)


def plane_backward(work_ref, out_ref, twiddle_ref):
    def body(p, carry):
        for tile in range(HALF // 8):
            rows = slice(tile * 8, tile * 8 + 8)
            re = []
            im = []
            for n in range(8):
                c = twiddle_ref[n * 8 + p, 0:1, :]
                s = twiddle_ref[n * 8 + p, 1:2, :]
                a = work_ref[n * 8 + p, 0, rows, :]
                b = work_ref[n * 8 + p, 1, rows, :]
                re.append(a * c + b * s)
                im.append(b * c - a * s)
            re, im = fft(re, im, 1.0)
            for n in range(8):
                work_ref[n * 8 + p, 0, rows, :] = re[n]
                work_ref[n * 8 + p, 1, rows, :] = im[n]
        return carry

    lax.fori_loop(0, 8, body, 0)
    plane_stage_one(work_ref, out_ref, 1.0)


def load_group(work_ref, group, high_ref, low_ref):
    rows = []
    for pair in range(2):
        rows.append(
            jnp.concatenate(
                [work_ref[group * 4 + pair * 2 + n // 2, n % 2] for n in range(4)], axis=1
            )
        )
    values = dot3(split(jnp.concatenate(rows, axis=0)), (high_ref[...], low_ref[...]))
    halves = []
    for pair in range(2):
        part = values[pair * HALF : (pair + 1) * HALF]
        halves.append(
            jnp.concatenate([part[:, n * 128 : (n + 1) * 128] for n in range(4)], axis=0)
        )
    return jnp.concatenate(halves, axis=1)


def store_group(work_ref, group, spectral, high_ref, low_ref):
    rows = []
    for pair in range(2):
        part = spectral[:, pair * 128 : (pair + 1) * 128]
        rows.append(
            jnp.concatenate([part[n * HALF : (n + 1) * HALF] for n in range(4)], axis=1)
        )
    values = dot3(split(jnp.concatenate(rows, axis=0)), (high_ref[...], low_ref[...]))
    for pair in range(2):
        for n in range(4):
            work_ref[group * 4 + pair * 2 + n // 2, n % 2] = values[
                pair * HALF : (pair + 1) * HALF, n * 128 : (n + 1) * 128
            ]


def depth_kernel(field_ref, high_ref, low_ref, out_ref, work_ref):
    for g in range(8):
        rows = field_ref[g * 256 : (g + 1) * 256, :]
        values = dot(high_ref[...], rows) + dot(low_ref[...], rows)
        work_ref[:, g * 8 : (g + 1) * 8, :] = values.reshape(2 * KZ, 8, C)

    def body(k, carry):
        values = work_ref[pl.ds(2 * k, 2)].reshape(2 * CELLS, C).T
        lane = lax.broadcasted_iota(jnp.int32, (HALF, 128), 1)
        for b in range(NB):
            upper = values[b * BS : b * BS + HALF]
            lower = values[b * BS + HALF : (b + 1) * BS]
            out_ref[b * KZ + k, 0] = jnp.where(lane < 64, upper, pltpu.roll(lower, 64, 1))
            out_ref[b * KZ + k, 1] = jnp.where(lane < 64, pltpu.roll(upper, 64, 1), lower)
        return carry

    lax.fori_loop(0, KZ, body, 0)


def forward_kernel(
    doubling_ref, src_ref, twiddle_ref, th_ref, tl_ref, w1h, w1l, b1, w2h, w2l, b2,
    spec_ref, outer_ref, slope_ref, square_ref, work_ref,
):
    plane_forward(src_ref, work_ref, twiddle_ref)
    root = math.sqrt(2.0 / math.pi)

    def body(g, carry):
        spectral = load_group(work_ref, g, th_ref, tl_ref)
        spec_ref[g] = spectral
        pre = dot3((w1h[...], w1l[...]), split(spectral)) + b1[...]
        pre_sq = pre * pre
        t = jnp.tanh(root * (pre + 0.044715 * (pre * pre_sq)))
        outer = 0.5 * pre * (1.0 + t)
        outer_ref[g] = outer
        slope_ref[g] = 0.5 * (1.0 + t) + 0.5 * pre * (1.0 - t * t) * (
            root * (1.0 + 3.0 * 0.044715 * pre_sq)
        )
        pre_two = dot3((w2h[...], w2l[...]), split(outer)) + b2[...]
        t2 = jnp.tanh(pre_two * (1.0 / SHRINK))
        square_ref[g] = t2 * t2 * doubling_ref[0, 0]
        return carry

    lax.fori_loop(0, GROUPS, body, 0)


def backward_kernel(
    src_ref, twiddle_ref, th_ref, tl_ref, bh_ref, bl_ref, w1h, w1l, w2h, w2l, slope_ref, square_ref,
    two_ref, one_ref, out_ref, work_ref,
):
    plane_forward(src_ref, work_ref, twiddle_ref)

    def body(g, carry):
        grad_two = load_group(work_ref, g, th_ref, tl_ref) * square_ref[g]
        two_ref[g] = grad_two
        grad_one = dot3((w2h[...], w2l[...]), split(grad_two)) * slope_ref[g]
        one_ref[g] = grad_one
        grad_spec = dot3((w1h[...], w1l[...]), split(grad_one))
        store_group(work_ref, g, grad_spec, bh_ref, bl_ref)
        return carry

    lax.fori_loop(0, GROUPS, body, 0)
    plane_backward(work_ref, out_ref, twiddle_ref)


def table_kernel(spec_ref, outer_ref, one_ref, two_ref, t1_ref, b1_ref, t2_ref, b2_ref):
    lanes = ((1,), (1,))
    shape = (2 * BS, 2 * BS)

    def body(g, carry):
        t1, s1, t2, s2 = carry
        one = one_ref[g]
        two = two_ref[g]
        t1 = t1 + dot3(split(spec_ref[g]), split(one), lanes)
        t2 = t2 + dot3(split(outer_ref[g]), split(two), lanes)
        return t1, s1 + one, t2, s2 + two

    zero = jnp.zeros(shape, f32)
    wide = jnp.zeros((2 * BS, WIDE), f32)
    t1, s1, t2, s2 = lax.fori_loop(0, GROUPS, body, (zero, wide, zero, wide))
    t1_ref[...] = t1
    t2_ref[...] = t2
    b1_ref[...] = jnp.sum(s1, axis=1, keepdims=True)
    b2_ref[...] = jnp.sum(s2, axis=1, keepdims=True)


def field_kernel(src_ref, cotangent_ref, high_ref, low_ref, out_ref, work_ref):
    def body(k, carry):
        lane = lax.broadcasted_iota(jnp.int32, (HALF, 128), 1)
        parts = []
        for b in range(NB):
            re = src_ref[b * KZ + k, 0]
            im = src_ref[b * KZ + k, 1]
            parts.append(jnp.where(lane < 64, re, pltpu.roll(im, 64, 1)))
            parts.append(jnp.where(lane < 64, pltpu.roll(re, 64, 1), im))
        values = jnp.concatenate(parts, axis=0).T
        work_ref[pl.ds(2 * k, 2)] = values.reshape(2, CELLS, C)
        return carry

    lax.fori_loop(0, KZ, body, 0)
    for g in range(8):
        rows = work_ref[:, g * 8 : (g + 1) * 8, :].reshape(256, C)
        values = dot3((high_ref[...], low_ref[...]), split(rows))
        span = slice(g * 256, (g + 1) * 256)
        out_ref[span, :] = (cotangent_ref[span, :].astype(f32) + values).astype(bf16)


def vmem(n):
    return [pl.BlockSpec(memory_space=pltpu.VMEM)] * n


def call(kernel, out_shape, args, scratch, flops, moved):
    outs = len(out_shape) if isinstance(out_shape, tuple) else 1
    return pl.pallas_call(
        kernel,
        out_shape=out_shape,
        in_specs=vmem(len(args)),
        out_specs=tuple(vmem(outs)) if isinstance(out_shape, tuple) else vmem(1)[0],
        scratch_shapes=scratch,
        compiler_params=BIG,
        cost_estimate=pl.CostEstimate(flops=flops, bytes_accessed=moved, transcendentals=0),
    )(*args)


def depth_forward(field, tables):
    return call(
        depth_kernel,
        SPECTRAL,
        (field.reshape(2048, C), *tables),
        [pltpu.VMEM((2 * KZ, CELLS, C), f32)],
        800_000_000,
        5_000_000,
    )


def mixing(weight):
    real = weight[0].T
    imag = weight[1].T
    return jnp.concatenate(
        [jnp.concatenate([real, -imag], axis=1), jnp.concatenate([imag, real], axis=1)], axis=0
    )


def jax_split(value):
    high = lax.reduce_precision(value, 8, 7)
    return high.astype(bf16), (value - high).astype(bf16)


def fold(table):
    return jnp.stack(
        [table[:BS, :BS] + table[BS:, BS:], table[:BS, BS:] - table[BS:, :BS]]
    )


def exchange(value):
    return lax.all_to_all(value, ("px", "py"), split_axis=0, concat_axis=0, tiled=True)


def shards(state_field, cotangent, first_weight, first_bias, second_weight, second_bias):
    depth_fwd, depth_bwd = depth_tables()
    plane_fwd, plane_bwd = plane_tables()
    twiddle = twiddle_table()
    owner = lax.axis_index("px") * 8 + lax.axis_index("py")
    block = owner // KZ
    doubling = jnp.where(owner % KZ == 0, 1.0, 2.0).astype(f32).reshape(1, 1)

    first = mixing(lax.dynamic_index_in_dim(first_weight, block, 1, keepdims=False))
    second = mixing(lax.dynamic_index_in_dim(second_weight, block, 1, keepdims=False))
    bias_one = lax.dynamic_index_in_dim(first_bias, block, 1, keepdims=False).reshape(2 * BS, 1)
    bias_two = lax.dynamic_index_in_dim(second_bias, block, 1, keepdims=False).reshape(2 * BS, 1)

    state_spec = exchange(depth_forward(state_field, depth_fwd))
    cot_spec = exchange(depth_forward(cotangent, depth_fwd))
    spec, outer, slope, square = pl.pallas_call(
        forward_kernel,
        out_shape=(GROUPED,) * 4,
        in_specs=[pl.BlockSpec(memory_space=pltpu.SMEM)] + vmem(10),
        out_specs=tuple(vmem(4)),
        scratch_shapes=[pltpu.VMEM((64, 2, HALF, 128), f32)],
        compiler_params=BIG,
        cost_estimate=pl.CostEstimate(
            flops=8_000_000_000, bytes_accessed=16_000_000, transcendentals=1_500_000
        ),
    )(doubling, state_spec, twiddle, *plane_fwd, *jax_split(first), bias_one, *jax_split(second), bias_two)

    grad_two, grad_one, grad_plane = call(
        backward_kernel,
        (GROUPED, GROUPED, SPECTRAL),
        (cot_spec, twiddle, *plane_fwd, *plane_bwd, *jax_split(first.T), *jax_split(second.T), slope, square),
        [pltpu.VMEM((64, 2, HALF, 128), f32)],
        10_000_000_000,
        20_000_000,
    )
    grad_cells = exchange(grad_plane)

    t1, s1, t2, s2 = call(
        table_kernel,
        (
            jax.ShapeDtypeStruct((2 * BS, 2 * BS), f32),
            jax.ShapeDtypeStruct((2 * BS, 1), f32),
        )
        * 2,
        (spec, outer, grad_one, grad_two),
        [],
        4_000_000_000,
        13_000_000,
    )
    norm = 1.0 / math.sqrt(4 * NX * NY * KZ)
    wide = 2 * BS * BS
    flat = jnp.concatenate(
        [fold(t1).reshape(-1), fold(t2).reshape(-1), s1.reshape(-1), s2.reshape(-1)]
    )
    flat = jnp.pad(flat * norm, (0, 64 * PIECE - flat.shape[0])).reshape(64, 5, 128)
    flat = exchange(flat).reshape(NB, KZ, 5, 128).sum(axis=1)
    flat = lax.all_to_all(flat, "dp", split_axis=0, concat_axis=0, tiled=True).sum(axis=0)
    for axis, size in (("py", 8), ("px", 8), ("dp", 4)):
        flat = jnp.broadcast_to(flat.reshape(1, -1, 128), (size, flat.size // 128, 128))
        flat = lax.all_to_all(flat, axis, split_axis=0, concat_axis=0, tiled=True)
    flat = flat.reshape(NB, 64 * PIECE)
    grads_one = flat[:, :wide].reshape(NB, 2, BS, BS).transpose(1, 0, 2, 3)
    grads_two = flat[:, wide : 2 * wide].reshape(NB, 2, BS, BS).transpose(1, 0, 2, 3)
    biases = flat[:, 2 * wide : 2 * wide + 4 * BS].reshape(NB, 2, 2, BS)

    state_grad = call(
        field_kernel,
        jax.ShapeDtypeStruct((2048, C), bf16),
        (grad_cells, cotangent.reshape(2048, C), *depth_bwd),
        [pltpu.VMEM((2 * KZ, CELLS, C), f32)],
        1_200_000_000,
        7_000_000,
    ).reshape(1, 8, 8, NZ, C)
    return (
        state_grad,
        grads_one,
        biases[:, 0].transpose(1, 0, 2),
        grads_two,
        biases[:, 1].transpose(1, 0, 2),
    )


def solution(mesh):
    in_specs = (
        P("dp", "px", "py", None, None),
        P("dp", "px", "py", None, None),
        P(),
        P(),
        P(),
        P(),
    )
    out_specs = (P("dp", "px", "py", None, None), P(), P(), P(), P())
    return jax.shard_map(shards, mesh=mesh, in_specs=in_specs, out_specs=out_specs, check_vma=False)
```

```python
import math

import jax
import jax.numpy as jnp
import ml_dtypes
import numpy as np
from jax import lax
from jax.experimental import pallas as pl
from jax.experimental.pallas import tpu as pltpu
from jax.sharding import PartitionSpec as P

NX = 64
NY = 64
NZ = 32
NB = 4
BS = 96
KZ = 16
C = 384
HALF = BS // 2
CELLS = 64
STEP = 8
GROUPS = 64 // STEP
WIDE = STEP * 64
ROWS = 512
SHRINK = 0.25
f32 = jnp.float32
bf16 = jnp.bfloat16
BIG = pltpu.CompilerParams(vmem_limit_bytes=26 * 1024 * 1024)
SPECTRAL = jax.ShapeDtypeStruct((64, 2, HALF, 128), f32)
GROUPED = jax.ShapeDtypeStruct((GROUPS, 2 * BS, WIDE), f32)


def np_split(table):
    high = table.astype(np.float32).astype(ml_dtypes.bfloat16)
    low = (table - high.astype(np.float64)).astype(np.float32).astype(ml_dtypes.bfloat16)
    return high, low


def depth_tables():
    k = np.arange(KZ)[:, None]
    z = np.arange(NZ)[None, :]
    angle = 2.0 * np.pi * (k * z % NZ) / NZ
    scale = 1.0 / math.sqrt(NX * NY * NZ)
    pair = np.stack([np.cos(angle), -np.sin(angle)], axis=1) * scale
    eye = np.eye(8)
    forward = np.einsum("kqz,ab->kqabz", pair, eye).reshape(256, 256)
    return np_split(forward), np_split(forward.T.copy())


def plane_tables():
    j = np.arange(8)
    eight = np.exp(-2j * np.pi * np.outer(j, j) / 8.0)
    both = np.einsum("xk,yl->xykl", eight, eight).reshape(64, 64)
    real = np.zeros((2, 64, 2, 64))
    real[0, :, 0] = both.real
    real[0, :, 1] = both.imag
    real[1, :, 0] = -both.imag
    real[1, :, 1] = both.real
    forward = np.einsum("qxpf,cd->qcxpdf", real, np.eye(2)).reshape(256, 256)
    return np_split(forward), np_split(forward.T.copy())


def twiddle_table():
    k2 = np.arange(8)
    j = np.arange(8)
    one = np.exp(-2j * np.pi * np.outer(k2, j) / 64.0)
    both = np.einsum("kx,ly->klxy", one, one).reshape(64, 64)
    both = np.tile(both, (1, 2))
    return np.stack([both.real, both.imag], axis=1).astype(np.float32)


def split(value):
    high = value.astype(bf16)
    low = (value - high.astype(f32)).astype(bf16)
    return high, low


def dot(left, right, dims=((1,), (0,))):
    return lax.dot_general(left, right, (dims, ((), ())), preferred_element_type=f32)


def dot3(left, right, dims=((1,), (0,))):
    high, low = left
    rows = high.shape[0]
    both = dot(jnp.concatenate([high, low], axis=0), right[0], dims)
    return both[:rows] + both[rows:] + dot(high, right[1], dims)


def product(weight_ref, value):
    rows = weight_ref.shape[0] // 2
    high, low = split(value)
    both = dot(weight_ref[...], high)
    return both[:rows] + both[rows:] + dot(weight_ref[:rows], low)


def swap(upper, lower):
    lane = lax.broadcasted_iota(jnp.int32, upper.shape, 1)
    first = jnp.where(lane < 64, upper, pltpu.roll(lower, 64, 1))
    second = jnp.where(lane < 64, pltpu.roll(upper, 64, 1), lower)
    return first, second


def fft(re, im, sign):
    n = len(re)
    if n == 1:
        return re, im
    even_re, even_im = fft(re[0::2], im[0::2], sign)
    odd_re, odd_im = fft(re[1::2], im[1::2], sign)
    out_re = [None] * n
    out_im = [None] * n
    root = math.sqrt(0.5)
    for k in range(n // 2):
        a, b = odd_re[k], odd_im[k]
        turn = k * (8 // n)
        if turn == 1:
            a, b = (a - sign * b) * root, (b + sign * a) * root
        elif turn == 2:
            a, b = -sign * b, sign * a
        elif turn == 3:
            a, b = (-a - sign * b) * root, (-b + sign * a) * root
        out_re[k], out_im[k] = even_re[k] + a, even_im[k] + b
        out_re[k + n // 2], out_im[k + n // 2] = even_re[k] - a, even_im[k] - b
    return out_re, out_im


def plane_stage_one(src_ref, dst_ref, sign):
    def body(p, carry):
        for tile in range(HALF // 8):
            rows = slice(tile * 8, tile * 8 + 8)
            re = [src_ref[p * 8 + n, 0, rows, :] for n in range(8)]
            im = [src_ref[p * 8 + n, 1, rows, :] for n in range(8)]
            re, im = fft(re, im, sign)
            for n in range(8):
                dst_ref[p * 8 + n, 0, rows, :] = re[n]
                dst_ref[p * 8 + n, 1, rows, :] = im[n]
        return carry

    lax.fori_loop(0, 8, body, 0)


def plane_forward(src_ref, work_ref, twiddle_ref):
    plane_stage_one(src_ref, work_ref, -1.0)

    def body(p, carry):
        for tile in range(HALF // 8):
            rows = slice(tile * 8, tile * 8 + 8)
            re = [work_ref[n * 8 + p, 0, rows, :] for n in range(8)]
            im = [work_ref[n * 8 + p, 1, rows, :] for n in range(8)]
            re, im = fft(re, im, -1.0)
            for n in range(8):
                c = twiddle_ref[n * 8 + p, 0:1, :]
                s = twiddle_ref[n * 8 + p, 1:2, :]
                work_ref[n * 8 + p, 0, rows, :] = re[n] * c - im[n] * s
                work_ref[n * 8 + p, 1, rows, :] = re[n] * s + im[n] * c
        return carry

    lax.fori_loop(0, 8, body, 0)


def plane_backward(work_ref, out_ref, twiddle_ref):
    def body(p, carry):
        for tile in range(HALF // 8):
            rows = slice(tile * 8, tile * 8 + 8)
            re = []
            im = []
            for n in range(8):
                c = twiddle_ref[n * 8 + p, 0:1, :]
                s = twiddle_ref[n * 8 + p, 1:2, :]
                a = work_ref[n * 8 + p, 0, rows, :]
                b = work_ref[n * 8 + p, 1, rows, :]
                re.append(a * c + b * s)
                im.append(b * c - a * s)
            re, im = fft(re, im, 1.0)
            for n in range(8):
                work_ref[n * 8 + p, 0, rows, :] = re[n]
                work_ref[n * 8 + p, 1, rows, :] = im[n]
        return carry

    lax.fori_loop(0, 8, body, 0)
    plane_stage_one(work_ref, out_ref, 1.0)


def load_group(work_ref, group, high_ref, low_ref):
    rows = [
        jnp.concatenate([work_ref[group * STEP + n, 0], work_ref[group * STEP + n, 1]], axis=1)
        for n in range(STEP)
    ]
    values = dot3(split(jnp.concatenate(rows, axis=0)), (high_ref[...], low_ref[...]))
    pairs = []
    for pair in range(STEP // 2):
        part = []
        for q in range(2):
            lanes = slice(q * 128, (q + 1) * 128)
            upper = values[2 * pair * HALF : (2 * pair + 1) * HALF, lanes]
            lower = values[(2 * pair + 1) * HALF : (2 * pair + 2) * HALF, lanes]
            part.extend(swap(upper, lower))
        pairs.append(jnp.concatenate(part, axis=0))
    return jnp.concatenate(pairs, axis=1)


def store_group(work_ref, group, spectral, high_ref, low_ref):
    rows = []
    for pair in range(STEP // 2):
        part = spectral[:, pair * 128 : (pair + 1) * 128]
        parts = [
            swap(part[q * BS : q * BS + HALF], part[q * BS + HALF : (q + 1) * BS])
            for q in range(2)
        ]
        for n in range(2):
            rows.append(jnp.concatenate([parts[0][n], parts[1][n]], axis=1))
    values = dot3(split(jnp.concatenate(rows, axis=0)), (high_ref[...], low_ref[...]))
    for n in range(STEP):
        for q in range(2):
            work_ref[group * STEP + n, q] = values[
                n * HALF : (n + 1) * HALF, q * 128 : (q + 1) * 128
            ]


def depth_kernel(field_ref, both_ref, out_ref, work_ref):
    for g in range(8):
        values = dot(both_ref[...], field_ref[g * 256 : (g + 1) * 256, :])
        values = values[:256] + values[256:]
        work_ref[:, g * 8 : (g + 1) * 8, :] = values.reshape(2 * KZ, 8, C)
    for k in range(KZ):
        values = work_ref[2 * k : 2 * k + 2].reshape(2 * CELLS, C).T
        for b in range(NB):
            upper = values[b * BS : b * BS + HALF]
            lower = values[b * BS + HALF : (b + 1) * BS]
            out_ref[b * KZ + k, 0], out_ref[b * KZ + k, 1] = swap(upper, lower)


def forward_kernel(
    doubling_ref, src_ref, twiddle_ref, th_ref, tl_ref, w1, b1, w2, b2,
    spec_ref, outer_ref, slope_ref, square_ref, work_ref,
):
    plane_forward(src_ref, work_ref, twiddle_ref)
    root = math.sqrt(2.0 / math.pi)

    def body(g, carry):
        spectral = load_group(work_ref, g, th_ref, tl_ref)
        spec_ref[g] = spectral
        pre = product(w1, spectral) + b1[...]
        pre_sq = pre * pre
        t = jnp.tanh(root * (pre + 0.044715 * (pre * pre_sq)))
        outer = 0.5 * pre * (1.0 + t)
        outer_ref[g] = outer
        slope_ref[g] = 0.5 * (1.0 + t) + 0.5 * pre * (1.0 - t * t) * (
            root * (1.0 + 3.0 * 0.044715 * pre_sq)
        )
        pre_two = product(w2, outer) + b2[...]
        t2 = jnp.tanh(pre_two * (1.0 / SHRINK))
        square_ref[g] = t2 * t2 * doubling_ref[0, 0]
        return carry

    lax.fori_loop(0, GROUPS, body, 0)


def backward_kernel(
    src_ref, twiddle_ref, th_ref, tl_ref, bh_ref, bl_ref, w1, w2, slope_ref, square_ref,
    two_ref, one_ref, out_ref, work_ref,
):
    plane_forward(src_ref, work_ref, twiddle_ref)

    def body(g, carry):
        grad_two = load_group(work_ref, g, th_ref, tl_ref) * square_ref[g]
        two_ref[g] = grad_two
        grad_one = product(w2, grad_two) * slope_ref[g]
        one_ref[g] = grad_one
        grad_spec = product(w1, grad_one)
        store_group(work_ref, g, grad_spec, bh_ref, bl_ref)
        return carry

    lax.fori_loop(0, GROUPS, body, 0)
    plane_backward(work_ref, out_ref, twiddle_ref)


def spread(value):
    gap = jnp.zeros((128 - BS, value.shape[1]), value.dtype)
    return jnp.concatenate([value[:BS], gap, value[BS:], gap], axis=0)


def table_kernel(spec_ref, outer_ref, one_ref, two_ref, out_ref):
    lanes = ((1,), (1,))

    def body(g, carry):
        t1, s1, t2, s2 = carry
        one = spread(one_ref[g])
        two = spread(two_ref[g])
        t1 = t1 + dot3(split(spec_ref[g]), split(one), lanes)
        t2 = t2 + dot3(split(outer_ref[g]), split(two), lanes)
        return t1, s1 + one, t2, s2 + two

    zero = jnp.zeros((2 * BS, 256), f32)
    wide = jnp.zeros((256, WIDE), f32)
    t1, s1, t2, s2 = lax.fori_loop(0, GROUPS, body, (zero, wide, zero, wide))
    norm = 1.0 / math.sqrt(4 * NX * NY * KZ)
    ones = jnp.ones((8, WIDE), bf16)
    row = lax.broadcasted_iota(jnp.int32, (8, 128), 0)
    out_ref[4 * BS :] = jnp.zeros((ROWS - 4 * BS, 128), f32)
    biases = jnp.zeros((8, 128), f32)
    for n, (table, total) in enumerate(((t1, s1), (t2, s2))):
        real = table[:BS, :128] + table[BS:, 128:]
        imag = table[:BS, 128:] - table[BS:, :128]
        out_ref[2 * n * BS : (2 * n + 1) * BS] = real * norm
        out_ref[(2 * n + 1) * BS : (2 * n + 2) * BS] = imag * norm
        high, low = split(total)
        sums = dot(ones, high, lanes) + dot(ones, low, lanes)
        for q in range(2):
            biases = jnp.where(row == 2 * n + q, sums[:, q * 128 : (q + 1) * 128], biases)
    out_ref[4 * BS : 4 * BS + 8] = biases * norm


def field_kernel(src_ref, cotangent_ref, high_ref, low_ref, out_ref, work_ref):
    for k in range(KZ):
        parts = []
        for b in range(NB):
            parts.extend(swap(src_ref[b * KZ + k, 0], src_ref[b * KZ + k, 1]))
        values = jnp.concatenate(parts, axis=0).T
        work_ref[2 * k : 2 * k + 2] = values.reshape(2, CELLS, C)
    both = jnp.concatenate([high_ref[...], low_ref[...]], axis=0)
    for g in range(8):
        high, low = split(work_ref[:, g * 8 : (g + 1) * 8, :].reshape(256, C))
        values = dot(both, high)
        values = values[:256] + values[256:] + dot(high_ref[...], low)
        span = slice(g * 256, (g + 1) * 256)
        out_ref[span, :] = (cotangent_ref[span, :].astype(f32) + values).astype(bf16)


def vmem(n):
    return [pl.BlockSpec(memory_space=pltpu.VMEM)] * n


def call(kernel, out_shape, args, scratch, flops, moved):
    outs = len(out_shape) if isinstance(out_shape, tuple) else 1
    return pl.pallas_call(
        kernel,
        out_shape=out_shape,
        in_specs=vmem(len(args)),
        out_specs=tuple(vmem(outs)) if isinstance(out_shape, tuple) else vmem(1)[0],
        scratch_shapes=scratch,
        compiler_params=BIG,
        cost_estimate=pl.CostEstimate(flops=flops, bytes_accessed=moved, transcendentals=0),
    )(*args)


def depth_forward(field, tables):
    return call(
        depth_kernel,
        SPECTRAL,
        (field.reshape(2048, C), np.concatenate(tables, axis=0)),
        [pltpu.VMEM((2 * KZ, CELLS, C), f32)],
        800_000_000,
        5_000_000,
    )


def mixing(weight):
    real = weight[0].T
    imag = weight[1].T
    return jnp.concatenate(
        [jnp.concatenate([real, -imag], axis=1), jnp.concatenate([imag, real], axis=1)], axis=0
    )


def stacked(value):
    high = lax.reduce_precision(value, 8, 7)
    return jnp.concatenate([high.astype(bf16), (value - high).astype(bf16)], axis=0)


def keep_half(value, axis, flip, bit):
    half = value.shape[0] // 2
    size = lax.axis_size(axis)
    mine = lax.dynamic_slice_in_dim(value, bit * half, half, 0)
    other = lax.dynamic_slice_in_dim(value, (1 - bit) * half, half, 0)
    return mine + lax.ppermute(other, axis, [(n, n ^ flip) for n in range(size)])


def join_half(value, axis, flip, bit):
    size = lax.axis_size(axis)
    other = lax.ppermute(value, axis, [(n, n ^ flip) for n in range(size)])
    return jnp.where(bit == 0, jnp.stack([value, other]), jnp.stack([other, value]))


def total_rows(rows, grad_cells):
    dp = lax.axis_index("dp")
    px = lax.axis_index("px")
    py = lax.axis_index("py")
    core = dp % 2
    low = dp // 2
    rows = keep_half(rows, "dp", 1, core)
    rows = keep_half(rows, "dp", 2, low)
    rows = keep_half(rows, "px", 1, px % 2)
    pieces = rows.reshape(8, -1, 128)
    total = lax.dynamic_index_in_dim(pieces, py, 0, keepdims=False)
    for offset in range(1, 8):
        piece = lax.dynamic_index_in_dim(pieces, (py + offset) % 8, 0, keepdims=False)
        total = total + lax.ppermute(piece, "py", [(n, (n + offset) % 8) for n in range(8)])
    total, grad_cells = lax.optimization_barrier((total, grad_cells))
    total = exchange(jnp.broadcast_to(total[None], (64, *total.shape)))
    total = join_half(total, "dp", 2, low)
    total = join_half(total, "dp", 1, core)
    total = total.reshape(2, 2, NB, 2, 8, ROWS // 64, 128)
    return total.transpose(2, 0, 1, 3, 4, 5, 6).reshape(NB, ROWS, 128), grad_cells


def exchange(value):
    return lax.all_to_all(value, ("px", "py"), split_axis=0, concat_axis=0, tiled=True)


def shards(state_field, cotangent, first_weight, first_bias, second_weight, second_bias):
    depth_fwd, depth_bwd = depth_tables()
    plane_fwd, plane_bwd = plane_tables()
    twiddle = twiddle_table()
    owner = lax.axis_index("px") * 8 + lax.axis_index("py")
    block = owner // KZ
    doubling = jnp.where(owner % KZ == 0, 1.0, 2.0).astype(f32).reshape(1, 1)

    first = mixing(lax.dynamic_index_in_dim(first_weight, block, 1, keepdims=False))
    second = mixing(lax.dynamic_index_in_dim(second_weight, block, 1, keepdims=False))
    bias_one = lax.dynamic_index_in_dim(first_bias, block, 1, keepdims=False).reshape(2 * BS, 1)
    bias_two = lax.dynamic_index_in_dim(second_bias, block, 1, keepdims=False).reshape(2 * BS, 1)

    state_spec = exchange(depth_forward(state_field, depth_fwd))
    cot_spec = exchange(depth_forward(cotangent, depth_fwd))
    spec, outer, slope, square = pl.pallas_call(
        forward_kernel,
        out_shape=(GROUPED,) * 4,
        in_specs=[pl.BlockSpec(memory_space=pltpu.SMEM)] + vmem(8),
        out_specs=tuple(vmem(4)),
        scratch_shapes=[pltpu.VMEM((64, 2, HALF, 128), f32)],
        compiler_params=BIG,
        cost_estimate=pl.CostEstimate(
            flops=8_000_000_000, bytes_accessed=16_000_000, transcendentals=1_500_000
        ),
    )(doubling, state_spec, twiddle, *plane_fwd, stacked(first), bias_one, stacked(second), bias_two)

    grad_two, grad_one, grad_plane = call(
        backward_kernel,
        (GROUPED, GROUPED, SPECTRAL),
        (cot_spec, twiddle, *plane_fwd, *plane_bwd, stacked(first.T), stacked(second.T), slope, square),
        [pltpu.VMEM((64, 2, HALF, 128), f32)],
        10_000_000_000,
        20_000_000,
    )
    grad_cells = exchange(grad_plane)

    rows = call(
        table_kernel,
        jax.ShapeDtypeStruct((ROWS, 128), f32),
        (spec, outer, grad_one, grad_two),
        [],
        4_000_000_000,
        13_000_000,
    )
    rows, grad_cells = total_rows(rows, grad_cells)
    grads_one = rows[:, : 2 * BS, :BS].reshape(NB, 2, BS, BS).transpose(1, 0, 2, 3)
    grads_two = rows[:, 2 * BS : 4 * BS, :BS].reshape(NB, 2, BS, BS).transpose(1, 0, 2, 3)
    biases = rows[:, 4 * BS : 4 * BS + 4, :BS].reshape(NB, 2, 2, BS)

    state_grad = call(
        field_kernel,
        jax.ShapeDtypeStruct((2048, C), bf16),
        (grad_cells, cotangent.reshape(2048, C), *depth_bwd),
        [pltpu.VMEM((2 * KZ, CELLS, C), f32)],
        1_200_000_000,
        7_000_000,
    ).reshape(1, 8, 8, NZ, C)
    return (
        state_grad,
        grads_one,
        biases[:, 0].transpose(1, 0, 2),
        grads_two,
        biases[:, 1].transpose(1, 0, 2),
    )


def solution(mesh):
    in_specs = (
        P("dp", "px", "py", None, None),
        P("dp", "px", "py", None, None),
        P(),
        P(),
        P(),
        P(),
    )
    out_specs = (P("dp", "px", "py", None, None), P(), P(), P(), P())
    return jax.shard_map(shards, mesh=mesh, in_specs=in_specs, out_specs=out_specs, check_vma=False)
```

```python
import math

import jax
import jax.numpy as jnp
import ml_dtypes
import numpy as np
from jax import lax
from jax.experimental import pallas as pl
from jax.experimental.pallas import tpu as pltpu
from jax.sharding import PartitionSpec as P

NX = 64
NY = 64
NZ = 32
NB = 4
BS = 96
KZ = 16
C = 384
HALF = BS // 2
PART = HALF // 2
CELLS = 64
STEP = 8
GROUPS = 64 // STEP
WIDE = STEP * 64
ROWS = 512
SHRINK = 0.25
f32 = jnp.float32
bf16 = jnp.bfloat16
BIG = pltpu.CompilerParams(vmem_limit_bytes=62 * 1024 * 1024)
SPECTRAL = (64, 2 * HALF, 128)
PARTIAL = (64, 2 * PART, 128)
GROUPED = jax.ShapeDtypeStruct((GROUPS, 2 * BS, WIDE), f32)


def np_split(table):
    high = table.astype(np.float32).astype(ml_dtypes.bfloat16)
    low = (table - high.astype(np.float64)).astype(np.float32).astype(ml_dtypes.bfloat16)
    return high, low


def depth_tables():
    k = np.arange(KZ)[:, None]
    z = np.arange(NZ)[None, :]
    angle = 2.0 * np.pi * (k * z % NZ) / NZ
    scale = 1.0 / math.sqrt(NX * NY * NZ)
    pair = np.stack([np.cos(angle), -np.sin(angle)], axis=1) * scale
    eye = np.eye(8)
    forward = np.einsum("kqz,ab->kqabz", pair, eye).reshape(256, 256)
    return np_split(forward), np_split(forward.T.copy())


def plane_tables():
    j = np.arange(8)
    eight = np.exp(-2j * np.pi * np.outer(j, j) / 8.0)
    both = np.einsum("xk,yl->xykl", eight, eight).reshape(64, 64)
    real = np.zeros((2, 64, 2, 64))
    real[0, :, 0] = both.real
    real[0, :, 1] = both.imag
    real[1, :, 0] = -both.imag
    real[1, :, 1] = both.real
    forward = np.einsum("qxpf,cd->qcxpdf", real, np.eye(2)).reshape(256, 256)
    return np_split(forward), np_split(forward.T.copy())


def twiddle_table():
    k2 = np.arange(8)
    j = np.arange(8)
    one = np.exp(-2j * np.pi * np.outer(k2, j) / 64.0)
    both = np.einsum("kx,ly->klxy", one, one).reshape(64, 64)
    both = np.tile(both, (1, 2))
    return np.stack([both.real, both.imag], axis=1).astype(np.float32)


def split(value):
    high = value.astype(bf16)
    low = (value - high.astype(f32)).astype(bf16)
    return high, low


def dot(left, right, dims=((1,), (0,))):
    return lax.dot_general(left, right, (dims, ((), ())), preferred_element_type=f32)


def dot3(left, right, dims=((1,), (0,))):
    high, low = left
    rows = high.shape[0]
    both = dot(jnp.concatenate([high, low], axis=0), right[0], dims)
    return both[:rows] + both[rows:] + dot(high, right[1], dims)


def product(weight_ref, value):
    rows = weight_ref.shape[0] // 2
    high, low = split(value)
    both = dot(weight_ref[...], high)
    return both[:rows] + both[rows:] + dot(weight_ref[:rows], low)


def swap(upper, lower):
    lane = lax.broadcasted_iota(jnp.int32, upper.shape, 1)
    first = jnp.where(lane < 64, upper, pltpu.roll(lower, 64, 1))
    second = jnp.where(lane < 64, pltpu.roll(upper, 64, 1), lower)
    return first, second


def fft(re, im, sign):
    n = len(re)
    if n == 1:
        return re, im
    even_re, even_im = fft(re[0::2], im[0::2], sign)
    odd_re, odd_im = fft(re[1::2], im[1::2], sign)
    out_re = [None] * n
    out_im = [None] * n
    root = math.sqrt(0.5)
    for k in range(n // 2):
        a, b = odd_re[k], odd_im[k]
        turn = k * (8 // n)
        if turn == 1:
            a, b = (a - sign * b) * root, (b + sign * a) * root
        elif turn == 2:
            a, b = -sign * b, sign * a
        elif turn == 3:
            a, b = (-a - sign * b) * root, (-b + sign * a) * root
        out_re[k], out_im[k] = even_re[k] + a, even_im[k] + b
        out_re[k + n // 2], out_im[k + n // 2] = even_re[k] - a, even_im[k] - b
    return out_re, out_im


def read(ref, index, tile):
    half = ref.shape[1] // 2
    rows = slice(tile * 8, tile * 8 + 8), slice(half + tile * 8, half + tile * 8 + 8)
    return ref[index, rows[0], :], ref[index, rows[1], :]


def write(ref, index, tile, re, im):
    half = ref.shape[1] // 2
    ref[index, tile * 8 : tile * 8 + 8, :] = re
    ref[index, half + tile * 8 : half + tile * 8 + 8, :] = im


def senders(src_ref, dst_ref, sign, before, after):
    def body(p, carry):
        before(p)
        for tile in range(src_ref.shape[1] // 16):
            re, im = zip(*[read(src_ref, p * 8 + n, tile) for n in range(8)])
            re, im = fft(re, im, sign)
            for n in range(8):
                write(dst_ref, p * 8 + n, tile, re[n], im[n])
        after(p)
        return carry

    lax.fori_loop(0, 8, body, 0)


def turned(a, b, twiddle_ref, index, sign):
    c = twiddle_ref[index, 0:1, :]
    s = twiddle_ref[index, 1:2, :] * sign
    return a * c - b * s, a * s + b * c


def plane_forward(src_ref, work_ref, twiddle_ref, before):
    senders(src_ref, work_ref, -1.0, before, lambda p: None)

    def body(p, carry):
        for tile in range(HALF // 8):
            re, im = zip(*[read(work_ref, n * 8 + p, tile) for n in range(8)])
            re, im = fft(re, im, -1.0)
            for n in range(8):
                write(work_ref, n * 8 + p, tile, *turned(re[n], im[n], twiddle_ref, n * 8 + p, 1.0))
        return carry

    lax.fori_loop(0, 8, body, 0)


def plane_backward(work_ref, out_ref, twiddle_ref, after):
    def body(p, carry):
        for tile in range(PART // 8):
            pairs = [
                turned(*read(work_ref, n * 8 + p, tile), twiddle_ref, n * 8 + p, -1.0)
                for n in range(8)
            ]
            re, im = fft(*zip(*pairs), 1.0)
            for n in range(8):
                write(work_ref, n * 8 + p, tile, re[n], im[n])
        return carry

    lax.fori_loop(0, 8, body, 0)
    senders(work_ref, out_ref, 1.0, lambda p: None, after)


def load_group(work_ref, group, high_ref, low_ref):
    rows = [
        jnp.concatenate(
            [work_ref[group * STEP + n, :HALF], work_ref[group * STEP + n, HALF:]], axis=1
        )
        for n in range(STEP)
    ]
    values = dot3(split(jnp.concatenate(rows, axis=0)), (high_ref[...], low_ref[...]))
    pairs = []
    for pair in range(STEP // 2):
        part = []
        for q in range(2):
            lanes = slice(q * 128, (q + 1) * 128)
            upper = values[2 * pair * HALF : (2 * pair + 1) * HALF, lanes]
            lower = values[(2 * pair + 1) * HALF : (2 * pair + 2) * HALF, lanes]
            part.extend(swap(upper, lower))
        pairs.append(jnp.concatenate(part, axis=0))
    return jnp.concatenate(pairs, axis=1)


def store_group(work_ref, group, spectral, high_ref, low_ref):
    rows = []
    for pair in range(STEP // 2):
        part = spectral[:, pair * 128 : (pair + 1) * 128]
        parts = [
            swap(
                part[2 * q * PART : (2 * q + 1) * PART],
                part[(2 * q + 1) * PART : (2 * q + 2) * PART],
            )
            for q in range(2)
        ]
        for n in range(2):
            rows.append(jnp.concatenate([parts[0][n], parts[1][n]], axis=1))
    values = dot3(split(jnp.concatenate(rows, axis=0)), (high_ref[...], low_ref[...]))
    for n in range(STEP):
        for q in range(2):
            work_ref[group * STEP + n, q * PART : (q + 1) * PART] = values[
                n * PART : (n + 1) * PART, q * 128 : (q + 1) * 128
            ]


def depth_kernel(field_hbm, both_hbm, out_hbm, field_ref, both_ref, out_ref, work_ref, sems, out_sems):
    table = pltpu.make_async_copy(both_hbm, both_ref, sems.at[8])
    table.start()
    copies = []
    for g in range(8):
        span = pl.ds(g * 256, 256)
        copies.append(pltpu.make_async_copy(field_hbm.at[span], field_ref.at[span], sems.at[g]))
        copies[-1].start()
    table.wait()
    for g in range(8):
        copies[g].wait()
        values = dot(both_ref[...], field_ref[g * 256 : (g + 1) * 256, :])
        values = values[:256] + values[256:]
        work_ref[:, g * 8 : (g + 1) * 8, :] = values.reshape(2 * KZ, 8, C)
    sends = []
    for k in range(KZ):
        values = work_ref[2 * k : 2 * k + 2].reshape(2 * CELLS, C).T
        for b in range(NB):
            upper = values[b * BS : b * BS + HALF]
            lower = values[b * BS + HALF : (b + 1) * BS]
            out_ref[b, k, :HALF], out_ref[b, k, HALF:] = swap(upper, lower)
        sends.append(pltpu.make_async_copy(out_ref.at[:, k], out_hbm.at[:, k], out_sems.at[k]))
        sends[-1].start()
    for send in sends:
        send.wait()


def forward_kernel(
    doubling_ref, src_ref, twiddle_ref, th_ref, tl_ref, w1, b1, w2, b2,
    spec_ref, outer_ref, slope_ref, square_ref, work_ref,
):
    plane_forward(src_ref, work_ref, twiddle_ref, lambda p: None)
    root = math.sqrt(2.0 / math.pi)

    def body(g, carry):
        spectral = load_group(work_ref, g, th_ref, tl_ref)
        spec_ref[g] = spectral
        pre = product(w1, spectral) + b1[...]
        pre_sq = pre * pre
        t = jnp.tanh(root * (pre + 0.044715 * (pre * pre_sq)))
        outer = 0.5 * pre * (1.0 + t)
        outer_ref[g] = outer
        slope_ref[g] = 0.5 * (1.0 + t) + 0.5 * pre * (1.0 - t * t) * (
            root * (1.0 + 3.0 * 0.044715 * pre_sq)
        )
        pre_two = product(w2, outer) + b2[...]
        t2 = jnp.tanh(pre_two * (1.0 / SHRINK))
        square_ref[g] = t2 * t2 * doubling_ref[0, 0]
        return carry

    lax.fori_loop(0, GROUPS, body, 0)


def block_of(hbm, ref, sems, p):
    span = pl.ds(p * 8, 8)
    return pltpu.make_async_copy(hbm.at[span], ref.at[span], sems.at[p])


def backward_kernel(
    src_hbm, twiddle_hbm, th_hbm, tl_hbm, bh_hbm, bl_hbm, w1_hbm, w2_hbm, slope_hbm, square_hbm,
    two_hbm, one_hbm, out_hbm,
    src_ref, twiddle_ref, th_ref, tl_ref, bh_ref, bl_ref, w1, w2, slope_ref, square_ref,
    two_ref, one_ref, out_ref, work_ref, part_ref, src_sems, sems, two_sems, one_sems, out_sems,
):
    for p in range(8):
        block_of(src_hbm, src_ref, src_sems, p).start()
    pairs = (
        (twiddle_hbm, twiddle_ref), (th_hbm, th_ref), (tl_hbm, tl_ref), (square_hbm, square_ref),
        (w2_hbm, w2), (slope_hbm, slope_ref), (w1_hbm, w1), (bh_hbm, bh_ref), (bl_hbm, bl_ref),
    )
    loads = [pltpu.make_async_copy(a, b, sems.at[n]) for n, (a, b) in enumerate(pairs)]
    for load in loads:
        load.start()
    loads[0].wait()
    plane_forward(
        src_ref, work_ref, twiddle_ref, lambda p: block_of(src_hbm, src_ref, src_sems, p).wait()
    )
    for load in loads[1:]:
        load.wait()

    def body(g, carry):
        grad_two = load_group(work_ref, g, th_ref, tl_ref) * square_ref[g]
        two_ref[g] = grad_two
        pltpu.make_async_copy(two_ref.at[g], two_hbm.at[g], two_sems.at[g]).start()
        grad_one = product(w2, grad_two) * slope_ref[g]
        one_ref[g] = grad_one
        pltpu.make_async_copy(one_ref.at[g], one_hbm.at[g], one_sems.at[g]).start()
        store_group(part_ref, g, product(w1, grad_one), bh_ref, bl_ref)
        return carry

    lax.fori_loop(0, GROUPS, body, 0)
    plane_backward(
        part_ref, out_ref, twiddle_ref, lambda p: block_of(out_ref, out_hbm, out_sems, p).start()
    )
    for g in range(GROUPS):
        pltpu.make_async_copy(two_ref.at[g], two_hbm.at[g], two_sems.at[g]).wait()
        pltpu.make_async_copy(one_ref.at[g], one_hbm.at[g], one_sems.at[g]).wait()
    for p in range(8):
        block_of(out_ref, out_hbm, out_sems, p).wait()


def rest_kernel(one_ref, twiddle_ref, bh_ref, bl_ref, w1, out_ref, part_ref, plane_ref):
    def body(g, carry):
        store_group(part_ref, g, product(w1, one_ref[g]), bh_ref, bl_ref)
        return carry

    lax.fori_loop(0, GROUPS, body, 0)
    plane_backward(part_ref, plane_ref, twiddle_ref, lambda p: None)
    out_ref[:, : 2 * PART, :] = plane_ref[...]
    out_ref[:, 2 * PART :, :] = jnp.zeros((64, 8, 128), f32)


def spread(value):
    gap = jnp.zeros((128 - BS, value.shape[1]), value.dtype)
    return jnp.concatenate([value[:BS], gap, value[BS:], gap], axis=0)


def table_kernel(spec_ref, outer_ref, one_ref, two_ref, out_ref):
    lanes = ((1,), (1,))

    def body(g, carry):
        t1, s1, t2, s2 = carry
        one = spread(one_ref[g])
        two = spread(two_ref[g])
        t1 = t1 + dot3(split(spec_ref[g]), split(one), lanes)
        t2 = t2 + dot3(split(outer_ref[g]), split(two), lanes)
        return t1, s1 + one, t2, s2 + two

    zero = jnp.zeros((2 * BS, 256), f32)
    wide = jnp.zeros((256, WIDE), f32)
    t1, s1, t2, s2 = lax.fori_loop(0, GROUPS, body, (zero, wide, zero, wide))
    norm = 1.0 / math.sqrt(4 * NX * NY * KZ)
    ones = jnp.ones((8, WIDE), bf16)
    row = lax.broadcasted_iota(jnp.int32, (8, 128), 0)
    out_ref[4 * BS :] = jnp.zeros((ROWS - 4 * BS, 128), f32)
    biases = jnp.zeros((8, 128), f32)
    for n, (table, total) in enumerate(((t1, s1), (t2, s2))):
        real = table[:BS, :128] + table[BS:, 128:]
        imag = table[:BS, 128:] - table[BS:, :128]
        out_ref[2 * n * BS : (2 * n + 1) * BS] = real * norm
        out_ref[(2 * n + 1) * BS : (2 * n + 2) * BS] = imag * norm
        high, low = split(total)
        sums = dot(ones, high, lanes) + dot(ones, low, lanes)
        for q in range(2):
            biases = jnp.where(row == 2 * n + q, sums[:, q * 128 : (q + 1) * 128], biases)
    out_ref[4 * BS : 4 * BS + 8] = biases * norm


def field_kernel(
    first_hbm, second_hbm, cotangent_hbm, high_hbm, low_hbm, out_hbm,
    first_ref, second_ref, cotangent_ref, high_ref, low_ref, out_ref, work_ref,
    first_sems, second_sems, sems, out_sems,
):
    loads = []
    for k in range(KZ):
        span = pl.ds(0, 2 * PART)
        loads.append(
            (
                pltpu.make_async_copy(first_hbm.at[:, k], first_ref.at[:, k], first_sems.at[k]),
                pltpu.make_async_copy(
                    second_hbm.at[:, k, span], second_ref.at[:, k], second_sems.at[k]
                ),
            )
        )
    pairs = ((high_hbm, high_ref), (low_hbm, low_ref), (cotangent_hbm, cotangent_ref))
    others = [pltpu.make_async_copy(a, b, sems.at[n]) for n, (a, b) in enumerate(pairs)]
    for load in loads:
        load[0].start()
        load[1].start()
    for load in others:
        load.start()
    for k in range(KZ):
        loads[k][0].wait()
        loads[k][1].wait()
        parts = []
        for b in range(NB):
            left = swap(first_ref[b, k, :PART], first_ref[b, k, PART:])
            right = swap(second_ref[b, k, :PART], second_ref[b, k, PART:])
            parts.extend([left[0], right[0], left[1], right[1]])
        values = jnp.concatenate(parts, axis=0).T
        work_ref[2 * k : 2 * k + 2] = values.reshape(2, CELLS, C)
    for load in others:
        load.wait()
    both = jnp.concatenate([high_ref[...], low_ref[...]], axis=0)
    sends = []
    for g in range(8):
        high, low = split(work_ref[:, g * 8 : (g + 1) * 8, :].reshape(256, C))
        values = dot(both, high)
        values = values[:256] + values[256:] + dot(high_ref[...], low)
        span = slice(g * 256, (g + 1) * 256)
        out_ref[span, :] = (cotangent_ref[span, :].astype(f32) + values).astype(bf16)
        rows = pl.ds(g * 256, 256)
        sends.append(pltpu.make_async_copy(out_ref.at[rows], out_hbm.at[rows], out_sems.at[g]))
        sends[-1].start()
    for send in sends:
        send.wait()


def vmem(n):
    return [pl.BlockSpec(memory_space=pltpu.VMEM)] * n


def free(n):
    return [pl.BlockSpec(memory_space=pl.ANY)] * n


def held(*values):
    return [pltpu.VMEM(v.shape, v.dtype) for v in values]


def sems(*counts):
    return [pltpu.SemaphoreType.DMA((n,)) for n in counts]


def call(kernel, out_shape, args, scratch, flops, moved, place=vmem):
    outs = len(out_shape) if isinstance(out_shape, tuple) else 1
    return pl.pallas_call(
        kernel,
        out_shape=out_shape,
        in_specs=place(len(args)),
        out_specs=tuple(place(outs)) if isinstance(out_shape, tuple) else place(1)[0],
        scratch_shapes=scratch,
        compiler_params=BIG,
        cost_estimate=pl.CostEstimate(flops=flops, bytes_accessed=moved, transcendentals=0),
    )(*args)


def depth_forward(field, tables):
    args = (field.reshape(2048, C), np.concatenate(tables, axis=0))
    out = jax.ShapeDtypeStruct((NB, KZ, 2 * HALF, 128), f32)
    scratch = [*held(*args, out), pltpu.VMEM((2 * KZ, CELLS, C), f32), *sems(9, KZ)]
    return call(depth_kernel, out, args, scratch, 800_000_000, 5_000_000, free).reshape(SPECTRAL)


def backward(cot_spec, twiddle, plane_fwd, plane_bwd, first, second, slope, square):
    args = (cot_spec, twiddle, *plane_fwd, *plane_bwd, first, second, slope, square)
    outs = (GROUPED, GROUPED, jax.ShapeDtypeStruct(PARTIAL, f32))
    scratch = [
        *held(*args, *outs),
        pltpu.VMEM(SPECTRAL, f32),
        pltpu.VMEM(PARTIAL, f32),
        *sems(8, 9, GROUPS, GROUPS, 8),
    ]
    return call(backward_kernel, outs, args, scratch, 10_000_000_000, 20_000_000, free)


def rest(grad_one, twiddle, plane_bwd, first):
    return call(
        rest_kernel,
        jax.ShapeDtypeStruct((64, 2 * PART + 8, 128), f32),
        (grad_one, twiddle, *plane_bwd, first),
        [pltpu.VMEM(PARTIAL, f32), pltpu.VMEM(PARTIAL, f32)],
        3_000_000_000,
        5_000_000,
    )


def field(first, second, cotangent, tables):
    args = (
        first.reshape(NB, KZ, 2 * PART, 128),
        second.reshape(NB, KZ, 2 * PART + 8, 128),
        cotangent.reshape(2048, C),
        *tables,
    )
    out = jax.ShapeDtypeStruct((2048, C), bf16)
    scratch = [
        *held(args[0], args[0], *args[2:], out),
        pltpu.VMEM((2 * KZ, CELLS, C), f32),
        *sems(KZ, KZ, 3, 8),
    ]
    return call(field_kernel, out, args, scratch, 1_200_000_000, 7_000_000, free)


def rows_of(weight, part):
    return weight.reshape(4, 2, PART, 2 * BS)[:, part].reshape(BS, 2 * BS)


def mixing(weight):
    real = weight[0].T
    imag = weight[1].T
    return jnp.concatenate(
        [jnp.concatenate([real, -imag], axis=1), jnp.concatenate([imag, real], axis=1)], axis=0
    )


def stacked(value):
    high = lax.reduce_precision(value, 8, 7)
    return jnp.concatenate([high.astype(bf16), (value - high).astype(bf16)], axis=0)


def keep_half(value, axis, flip, bit):
    half = value.shape[0] // 2
    size = lax.axis_size(axis)
    mine = lax.dynamic_slice_in_dim(value, bit * half, half, 0)
    other = lax.dynamic_slice_in_dim(value, (1 - bit) * half, half, 0)
    return mine + lax.ppermute(other, axis, [(n, n ^ flip) for n in range(size)])


def join_half(value, axis, flip, bit):
    size = lax.axis_size(axis)
    other = lax.ppermute(value, axis, [(n, n ^ flip) for n in range(size)])
    return jnp.where(bit == 0, jnp.stack([value, other]), jnp.stack([other, value]))


def owned_rows(rows):
    dp = lax.axis_index("dp")
    px = lax.axis_index("px")
    py = lax.axis_index("py")
    rows = keep_half(rows, "dp", 1, dp % 2)
    rows = keep_half(rows, "dp", 2, dp // 2)
    rows = keep_half(rows, "px", 1, px % 2)
    pieces = rows.reshape(8, -1, 128)
    total = lax.dynamic_index_in_dim(pieces, py, 0, keepdims=False)
    for offset in range(1, 8):
        piece = lax.dynamic_index_in_dim(pieces, (py + offset) % 8, 0, keepdims=False)
        total = total + lax.ppermute(piece, "py", [(n, (n + offset) % 8) for n in range(8)])
    return total


def every_row(total):
    dp = lax.axis_index("dp")
    total = join_half(total, "dp", 2, dp // 2)
    total = join_half(total, "dp", 1, dp % 2)
    total = total.reshape(2, 2, NB, 2, 8, ROWS // 64, 128)
    return total.transpose(2, 0, 1, 3, 4, 5, 6).reshape(NB, ROWS, 128)


def exchange(value):
    return lax.all_to_all(value, ("px", "py"), split_axis=0, concat_axis=0, tiled=True)


def shards(state_field, cotangent, first_weight, first_bias, second_weight, second_bias):
    depth_fwd, depth_bwd = depth_tables()
    plane_fwd, plane_bwd = plane_tables()
    twiddle = twiddle_table()
    owner = lax.axis_index("px") * 8 + lax.axis_index("py")
    block = owner // KZ
    doubling = jnp.where(owner % KZ == 0, 1.0, 2.0).astype(f32).reshape(1, 1)

    first = mixing(lax.dynamic_index_in_dim(first_weight, block, 1, keepdims=False))
    second = mixing(lax.dynamic_index_in_dim(second_weight, block, 1, keepdims=False))
    bias_one = lax.dynamic_index_in_dim(first_bias, block, 1, keepdims=False).reshape(2 * BS, 1)
    bias_two = lax.dynamic_index_in_dim(second_bias, block, 1, keepdims=False).reshape(2 * BS, 1)

    state_spec = exchange(depth_forward(state_field, depth_fwd))
    cot_spec = exchange(depth_forward(cotangent, depth_fwd))
    spec, outer, slope, square = pl.pallas_call(
        forward_kernel,
        out_shape=(GROUPED,) * 4,
        in_specs=[pl.BlockSpec(memory_space=pltpu.SMEM)] + vmem(8),
        out_specs=tuple(vmem(4)),
        scratch_shapes=[pltpu.VMEM(SPECTRAL, f32)],
        compiler_params=BIG,
        cost_estimate=pl.CostEstimate(
            flops=8_000_000_000, bytes_accessed=16_000_000, transcendentals=1_500_000
        ),
    )(doubling, state_spec, twiddle, *plane_fwd, stacked(first), bias_one, stacked(second), bias_two)

    grad_two, grad_one, plane = backward(
        cot_spec,
        twiddle,
        plane_fwd,
        plane_bwd,
        stacked(rows_of(first.T, 0)),
        stacked(second.T),
        slope,
        square,
    )
    first_part = exchange(plane)
    rows = call(
        table_kernel,
        jax.ShapeDtypeStruct((ROWS, 128), f32),
        (spec, outer, grad_one, grad_two),
        [],
        4_000_000_000,
        13_000_000,
    )
    rows = owned_rows(rows)
    plane = rest(grad_one, twiddle, plane_bwd, stacked(rows_of(first.T, 1)))
    plane = lax.dynamic_update_slice(
        plane, jnp.broadcast_to(rows[None], (64, *rows.shape)), (0, 2 * PART, 0)
    )
    first_part, plane = lax.optimization_barrier((first_part, plane))
    second_part = exchange(plane)
    rows = every_row(second_part[:, 2 * PART :])
    grads_one = rows[:, : 2 * BS, :BS].reshape(NB, 2, BS, BS).transpose(1, 0, 2, 3)
    grads_two = rows[:, 2 * BS : 4 * BS, :BS].reshape(NB, 2, BS, BS).transpose(1, 0, 2, 3)
    biases = rows[:, 4 * BS : 4 * BS + 4, :BS].reshape(NB, 2, 2, BS)

    state_grad = field(first_part, second_part, cotangent, depth_bwd).reshape(1, 8, 8, NZ, C)
    return (
        state_grad,
        grads_one,
        biases[:, 0].transpose(1, 0, 2),
        grads_two,
        biases[:, 1].transpose(1, 0, 2),
    )


def solution(mesh):
    in_specs = (
        P("dp", "px", "py", None, None),
        P("dp", "px", "py", None, None),
        P(),
        P(),
        P(),
        P(),
    )
    out_specs = (P("dp", "px", "py", None, None), P(), P(), P(), P())
    return jax.shard_map(shards, mesh=mesh, in_specs=in_specs, out_specs=out_specs, check_vma=False)
```

```python
import math

import jax
import jax.numpy as jnp
import ml_dtypes
import numpy as np
from jax import lax
from jax.experimental import pallas as pl
from jax.experimental.pallas import tpu as pltpu
from jax.sharding import PartitionSpec as P

NX = 64
NY = 64
NZ = 32
NB = 4
BS = 96
KZ = 16
C = 384
HALF = BS // 2
PART = HALF // 2
CELLS = 64
STEP = 8
GROUPS = 64 // STEP
WIDE = STEP * 64
ROWS = 512
SHRINK = 0.25
f32 = jnp.float32
bf16 = jnp.bfloat16
BIG = pltpu.CompilerParams(vmem_limit_bytes=62 * 1024 * 1024)
SPECTRAL = (64, 2 * HALF, 128)
PARTIAL = (64, 2 * PART, 128)
GROUPED = jax.ShapeDtypeStruct((GROUPS, 2 * BS, WIDE), f32)


def np_split(table):
    high = table.astype(np.float32).astype(ml_dtypes.bfloat16)
    low = (table - high.astype(np.float64)).astype(np.float32).astype(ml_dtypes.bfloat16)
    return high, low


def depth_tables():
    k = np.arange(KZ)[:, None]
    z = np.arange(NZ)[None, :]
    angle = 2.0 * np.pi * (k * z % NZ) / NZ
    scale = 1.0 / math.sqrt(NX * NY * NZ)
    pair = np.stack([np.cos(angle), -np.sin(angle)], axis=1) * scale
    eye = np.eye(8)
    forward = np.einsum("kqz,ab->kqabz", pair, eye).reshape(256, 256)
    return np_split(forward), np_split(forward.T.copy())


def plane_tables():
    j = np.arange(8)
    eight = np.exp(-2j * np.pi * np.outer(j, j) / 8.0)
    both = np.einsum("xk,yl->xykl", eight, eight).reshape(64, 64)
    real = np.zeros((2, 64, 2, 64))
    real[0, :, 0] = both.real
    real[0, :, 1] = both.imag
    real[1, :, 0] = -both.imag
    real[1, :, 1] = both.real
    forward = np.einsum("qxpf,cd->qcxpdf", real, np.eye(2)).reshape(256, 256)
    return np_split(forward), np_split(forward.T.copy())


def twiddle_table():
    k2 = np.arange(8)
    j = np.arange(8)
    one = np.exp(-2j * np.pi * np.outer(k2, j) / 64.0)
    both = np.einsum("kx,ly->klxy", one, one).reshape(64, 64)
    both = np.tile(both, (1, 2))
    return np.stack([both.real, both.imag], axis=1).astype(np.float32)


def split(value):
    high = value.astype(bf16)
    low = (value - high.astype(f32)).astype(bf16)
    return high, low


def dot(left, right, dims=((1,), (0,))):
    return lax.dot_general(left, right, (dims, ((), ())), preferred_element_type=f32)


def dot3(left, right, dims=((1,), (0,))):
    high, low = left
    rows = high.shape[0]
    both = dot(jnp.concatenate([high, low], axis=0), right[0], dims)
    return both[:rows] + both[rows:] + dot(high, right[1], dims)


def product(weight_ref, value):
    rows = weight_ref.shape[0] // 2
    high, low = split(value)
    both = dot(weight_ref[...], high)
    return both[:rows] + both[rows:] + dot(weight_ref[:rows], low)


def swap(upper, lower):
    lane = lax.broadcasted_iota(jnp.int32, upper.shape, 1)
    first = jnp.where(lane < 64, upper, pltpu.roll(lower, 64, 1))
    second = jnp.where(lane < 64, pltpu.roll(upper, 64, 1), lower)
    return first, second


def fft(re, im, sign):
    n = len(re)
    if n == 1:
        return re, im
    even_re, even_im = fft(re[0::2], im[0::2], sign)
    odd_re, odd_im = fft(re[1::2], im[1::2], sign)
    out_re = [None] * n
    out_im = [None] * n
    root = math.sqrt(0.5)
    for k in range(n // 2):
        a, b = odd_re[k], odd_im[k]
        turn = k * (8 // n)
        if turn == 1:
            a, b = (a - sign * b) * root, (b + sign * a) * root
        elif turn == 2:
            a, b = -sign * b, sign * a
        elif turn == 3:
            a, b = (-a - sign * b) * root, (-b + sign * a) * root
        out_re[k], out_im[k] = even_re[k] + a, even_im[k] + b
        out_re[k + n // 2], out_im[k + n // 2] = even_re[k] - a, even_im[k] - b
    return out_re, out_im


def read(ref, index, tile):
    half = ref.shape[1] // 2
    rows = slice(tile * 8, tile * 8 + 8), slice(half + tile * 8, half + tile * 8 + 8)
    return ref[index, rows[0], :], ref[index, rows[1], :]


def write(ref, index, tile, re, im):
    half = ref.shape[1] // 2
    ref[index, tile * 8 : tile * 8 + 8, :] = re
    ref[index, half + tile * 8 : half + tile * 8 + 8, :] = im


def senders(src_ref, dst_ref, sign, before, after):
    def body(p, carry):
        before(p)
        for tile in range(src_ref.shape[1] // 16):
            re, im = zip(*[read(src_ref, p * 8 + n, tile) for n in range(8)])
            re, im = fft(re, im, sign)
            for n in range(8):
                write(dst_ref, p * 8 + n, tile, re[n], im[n])
        after(p)
        return carry

    lax.fori_loop(0, 8, body, 0)


def turned(a, b, twiddle_ref, index, sign):
    c = twiddle_ref[index, 0:1, :]
    s = twiddle_ref[index, 1:2, :] * sign
    return a * c - b * s, a * s + b * c


def plane_forward(src_ref, work_ref, twiddle_ref, before):
    senders(src_ref, work_ref, -1.0, before, lambda p: None)

    def body(p, carry):
        for tile in range(HALF // 8):
            re, im = zip(*[read(work_ref, n * 8 + p, tile) for n in range(8)])
            re, im = fft(re, im, -1.0)
            for n in range(8):
                write(work_ref, n * 8 + p, tile, *turned(re[n], im[n], twiddle_ref, n * 8 + p, 1.0))
        return carry

    lax.fori_loop(0, 8, body, 0)


def plane_backward(work_ref, out_ref, twiddle_ref, after):
    def body(p, carry):
        for tile in range(PART // 8):
            pairs = [
                turned(*read(work_ref, n * 8 + p, tile), twiddle_ref, n * 8 + p, -1.0)
                for n in range(8)
            ]
            re, im = fft(*zip(*pairs), 1.0)
            for n in range(8):
                write(work_ref, n * 8 + p, tile, re[n], im[n])
        return carry

    lax.fori_loop(0, 8, body, 0)
    senders(work_ref, out_ref, 1.0, lambda p: None, after)


def load_group(work_ref, group, high_ref, low_ref):
    rows = [
        jnp.concatenate(
            [work_ref[group * STEP + n, :HALF], work_ref[group * STEP + n, HALF:]], axis=1
        )
        for n in range(STEP)
    ]
    values = dot3(split(jnp.concatenate(rows, axis=0)), (high_ref[...], low_ref[...]))
    pairs = []
    for pair in range(STEP // 2):
        part = []
        for q in range(2):
            lanes = slice(q * 128, (q + 1) * 128)
            upper = values[2 * pair * HALF : (2 * pair + 1) * HALF, lanes]
            lower = values[(2 * pair + 1) * HALF : (2 * pair + 2) * HALF, lanes]
            part.extend(swap(upper, lower))
        pairs.append(jnp.concatenate(part, axis=0))
    return jnp.concatenate(pairs, axis=1)


def store_group(work_ref, group, spectral, high_ref, low_ref):
    rows = []
    for pair in range(STEP // 2):
        part = spectral[:, pair * 128 : (pair + 1) * 128]
        parts = [
            swap(
                part[2 * q * PART : (2 * q + 1) * PART],
                part[(2 * q + 1) * PART : (2 * q + 2) * PART],
            )
            for q in range(2)
        ]
        for n in range(2):
            rows.append(jnp.concatenate([parts[0][n], parts[1][n]], axis=1))
    values = dot3(split(jnp.concatenate(rows, axis=0)), (high_ref[...], low_ref[...]))
    for n in range(STEP):
        for q in range(2):
            work_ref[group * STEP + n, q * PART : (q + 1) * PART] = values[
                n * PART : (n + 1) * PART, q * 128 : (q + 1) * 128
            ]


def depth_kernel(field_hbm, both_hbm, out_hbm, field_ref, both_ref, out_ref, work_ref, sems, out_sems):
    table = pltpu.make_async_copy(both_hbm, both_ref, sems.at[8])
    table.start()
    copies = []
    for g in range(8):
        span = pl.ds(g * 256, 256)
        copies.append(pltpu.make_async_copy(field_hbm.at[span], field_ref.at[span], sems.at[g]))
        copies[-1].start()
    table.wait()
    for g in range(8):
        copies[g].wait()
        values = dot(both_ref[...], field_ref[g * 256 : (g + 1) * 256, :])
        values = values[:256] + values[256:]
        work_ref[:, g * 8 : (g + 1) * 8, :] = values.reshape(2 * KZ, 8, C)
    sends = []
    for k in range(KZ):
        values = work_ref[2 * k : 2 * k + 2].reshape(2 * CELLS, C).T
        for b in range(NB):
            upper = values[b * BS : b * BS + HALF]
            lower = values[b * BS + HALF : (b + 1) * BS]
            out_ref[b, k, :HALF], out_ref[b, k, HALF:] = swap(upper, lower)
        sends.append(pltpu.make_async_copy(out_ref.at[:, k], out_hbm.at[:, k], out_sems.at[k]))
        sends[-1].start()
    for send in sends:
        send.wait()


def forward_kernel(
    doubling_ref, src_ref, twiddle_ref, th_ref, tl_ref, w1, b1, w2, b2,
    spec_ref, outer_ref, slope_ref, square_ref, work_ref,
):
    plane_forward(src_ref, work_ref, twiddle_ref, lambda p: None)
    root = math.sqrt(2.0 / math.pi)

    def body(g, carry):
        spectral = load_group(work_ref, g, th_ref, tl_ref)
        spec_ref[g] = spectral
        pre = product(w1, spectral) + b1[...]
        pre_sq = pre * pre
        t = jnp.tanh(root * (pre + 0.044715 * (pre * pre_sq)))
        outer = 0.5 * pre * (1.0 + t)
        outer_ref[g] = outer
        slope_ref[g] = 0.5 * (1.0 + t) + 0.5 * pre * (1.0 - t * t) * (
            root * (1.0 + 3.0 * 0.044715 * pre_sq)
        )
        pre_two = product(w2, outer) + b2[...]
        t2 = jnp.tanh(pre_two * (1.0 / SHRINK))
        square_ref[g] = t2 * t2 * doubling_ref[0, 0]
        return carry

    lax.fori_loop(0, GROUPS, body, 0)


def block_of(hbm, ref, sems, p):
    span = pl.ds(p * 8, 8)
    return pltpu.make_async_copy(hbm.at[span], ref.at[span], sems.at[p])


def backward_kernel(
    src_hbm, twiddle_hbm, th_hbm, tl_hbm, bh_hbm, bl_hbm, w1_hbm, w2_hbm, slope_hbm, square_hbm,
    two_hbm, out_hbm,
    src_ref, twiddle_ref, th_ref, tl_ref, bh_ref, bl_ref, w1, w2, slope_ref, square_ref,
    two_ref, out_ref, work_ref, part_ref, src_sems, sems, square_sems, slope_sems,
    two_sems, out_sems,
):
    for p in range(8):
        block_of(src_hbm, src_ref, src_sems, p).start()
    pairs = (
        (twiddle_hbm, twiddle_ref), (th_hbm, th_ref), (tl_hbm, tl_ref), (w2_hbm, w2),
        (w1_hbm, w1), (bh_hbm, bh_ref), (bl_hbm, bl_ref),
    )
    loads = [pltpu.make_async_copy(a, b, sems.at[n]) for n, (a, b) in enumerate(pairs)]
    for load in loads:
        load.start()
    loads[0].wait()

    def before(p):
        block_of(src_hbm, src_ref, src_sems, p).wait()
        pltpu.make_async_copy(square_hbm.at[p], square_ref.at[p], square_sems.at[p]).start()
        pltpu.make_async_copy(slope_hbm.at[p], slope_ref.at[p], slope_sems.at[p]).start()

    plane_forward(src_ref, work_ref, twiddle_ref, before)
    for load in loads[1:]:
        load.wait()

    sends = []
    spectral = load_group(work_ref, 0, th_ref, tl_ref)
    for g in range(GROUPS):
        following = load_group(work_ref, g + 1, th_ref, tl_ref) if g + 1 < GROUPS else None
        pltpu.make_async_copy(square_hbm.at[g], square_ref.at[g], square_sems.at[g]).wait()
        grad_two = spectral * square_ref[g]
        two_ref[g] = grad_two
        sends.append(pltpu.make_async_copy(two_ref.at[g], two_hbm.at[g], two_sems.at[g]))
        sends[-1].start()
        pltpu.make_async_copy(slope_hbm.at[g], slope_ref.at[g], slope_sems.at[g]).wait()
        grad_one = product(w2, grad_two) * slope_ref[g]
        store_group(part_ref, g, product(w1, grad_one), bh_ref, bl_ref)
        spectral = following
    plane_backward(
        part_ref, out_ref, twiddle_ref, lambda p: block_of(out_ref, out_hbm, out_sems, p).start()
    )
    for send in sends:
        send.wait()
    for p in range(8):
        block_of(out_ref, out_hbm, out_sems, p).wait()


def spread(value):
    gap = jnp.zeros((128 - BS, value.shape[1]), value.dtype)
    return jnp.concatenate([value[:BS], gap, value[BS:], gap], axis=0)


def rest_kernel(
    spec_ref, outer_ref, two_ref, slope_ref, w2, w1, twiddle_ref, bh_ref, bl_ref,
    out_ref, plane_hbm,
    t1_ref, s1_ref, t2_ref, s2_ref, part_ref, plane_ref, sends,
):
    lanes = ((1,), (1,))
    g = pl.program_id(0)

    @pl.when(g == 0)
    def _():
        for ref in (t1_ref, s1_ref, t2_ref, s2_ref):
            ref[...] = jnp.zeros(ref.shape, f32)

    grad_two = two_ref[0]
    two = spread(grad_two)
    t2_ref[...] += dot3(split(outer_ref[0]), split(two), lanes)
    s2_ref[...] += two
    grad_one = product(w2, grad_two) * slope_ref[0]
    one = spread(grad_one)
    t1_ref[...] += dot3(split(spec_ref[0]), split(one), lanes)
    s1_ref[...] += one
    store_group(part_ref, g, product(w1, grad_one), bh_ref, bl_ref)

    def send(p):
        span = pl.ds(p * 8, 8)
        rows = pl.ds(0, 2 * PART)
        return pltpu.make_async_copy(plane_ref.at[span], plane_hbm.at[span, rows], sends.at[p])

    @pl.when(g == GROUPS - 1)
    def _():
        plane_backward(part_ref, plane_ref, twiddle_ref, lambda p: send(p).start())
        norm = 1.0 / math.sqrt(4 * NX * NY * KZ)
        ones = jnp.ones((8, WIDE), bf16)
        row = lax.broadcasted_iota(jnp.int32, (8, 128), 0)
        out_ref[4 * BS :] = jnp.zeros((ROWS - 4 * BS, 128), f32)
        biases = jnp.zeros((8, 128), f32)
        for n, (table_ref, total_ref) in enumerate(((t1_ref, s1_ref), (t2_ref, s2_ref))):
            table = table_ref[...]
            real = table[:BS, :128] + table[BS:, 128:]
            imag = table[:BS, 128:] - table[BS:, :128]
            out_ref[2 * n * BS : (2 * n + 1) * BS] = real * norm
            out_ref[(2 * n + 1) * BS : (2 * n + 2) * BS] = imag * norm
            high, low = split(total_ref[...])
            sums = dot(ones, high, lanes) + dot(ones, low, lanes)
            for q in range(2):
                biases = jnp.where(row == 2 * n + q, sums[:, q * 128 : (q + 1) * 128], biases)
        out_ref[4 * BS : 4 * BS + 8] = biases * norm
        for p in range(8):
            send(p).wait()


def field_kernel(
    first_hbm, second_hbm, cotangent_hbm, high_hbm, low_hbm, out_hbm,
    first_ref, second_ref, cotangent_ref, high_ref, low_ref, out_ref, work_ref,
    first_sems, second_sems, sems, out_sems,
):
    loads = []
    for k in range(KZ):
        span = pl.ds(0, 2 * PART)
        loads.append(
            (
                pltpu.make_async_copy(first_hbm.at[:, k], first_ref.at[:, k], first_sems.at[k]),
                pltpu.make_async_copy(
                    second_hbm.at[:, k, span], second_ref.at[:, k], second_sems.at[k]
                ),
            )
        )
    pairs = ((high_hbm, high_ref), (low_hbm, low_ref), (cotangent_hbm, cotangent_ref))
    others = [pltpu.make_async_copy(a, b, sems.at[n]) for n, (a, b) in enumerate(pairs)]
    for load in loads:
        load[0].start()
        load[1].start()
    for load in others:
        load.start()
    for k in range(KZ):
        loads[k][0].wait()
        loads[k][1].wait()
        parts = []
        for b in range(NB):
            left = swap(first_ref[b, k, :PART], first_ref[b, k, PART:])
            right = swap(second_ref[b, k, :PART], second_ref[b, k, PART:])
            parts.extend([left[0], right[0], left[1], right[1]])
        values = jnp.concatenate(parts, axis=0).T
        work_ref[2 * k : 2 * k + 2] = values.reshape(2, CELLS, C)
    for load in others:
        load.wait()
    both = jnp.concatenate([high_ref[...], low_ref[...]], axis=0)
    sends = []
    for g in range(8):
        high, low = split(work_ref[:, g * 8 : (g + 1) * 8, :].reshape(256, C))
        values = dot(both, high)
        values = values[:256] + values[256:] + dot(high_ref[...], low)
        span = slice(g * 256, (g + 1) * 256)
        out_ref[span, :] = (cotangent_ref[span, :].astype(f32) + values).astype(bf16)
        rows = pl.ds(g * 256, 256)
        sends.append(pltpu.make_async_copy(out_ref.at[rows], out_hbm.at[rows], out_sems.at[g]))
        sends[-1].start()
    for send in sends:
        send.wait()


def vmem(n):
    return [pl.BlockSpec(memory_space=pltpu.VMEM)] * n


def free(n):
    return [pl.BlockSpec(memory_space=pl.ANY)] * n


def held(*values):
    return [pltpu.VMEM(v.shape, v.dtype) for v in values]


def sems(*counts):
    return [pltpu.SemaphoreType.DMA((n,)) for n in counts]


def call(kernel, out_shape, args, scratch, flops, moved, place=vmem):
    outs = len(out_shape) if isinstance(out_shape, tuple) else 1
    return pl.pallas_call(
        kernel,
        out_shape=out_shape,
        in_specs=place(len(args)),
        out_specs=tuple(place(outs)) if isinstance(out_shape, tuple) else place(1)[0],
        scratch_shapes=scratch,
        compiler_params=BIG,
        cost_estimate=pl.CostEstimate(flops=flops, bytes_accessed=moved, transcendentals=0),
    )(*args)


def depth_forward(field, tables):
    args = (field.reshape(2048, C), np.concatenate(tables, axis=0))
    out = jax.ShapeDtypeStruct((NB, KZ, 2 * HALF, 128), f32)
    scratch = [*held(*args, out), pltpu.VMEM((2 * KZ, CELLS, C), f32), *sems(9, KZ)]
    return call(depth_kernel, out, args, scratch, 800_000_000, 5_000_000, free).reshape(SPECTRAL)


def backward(cot_spec, twiddle, plane_fwd, plane_bwd, first, second, slope, square):
    args = (cot_spec, twiddle, *plane_fwd, *plane_bwd, first, second, slope, square)
    outs = (GROUPED, jax.ShapeDtypeStruct(PARTIAL, f32))
    scratch = [
        *held(*args, *outs),
        pltpu.VMEM(SPECTRAL, f32),
        pltpu.VMEM(PARTIAL, f32),
        *sems(8, 7, *[GROUPS] * 3, 8),
    ]
    return call(backward_kernel, outs, args, scratch, 10_000_000_000, 20_000_000, free)


def by_group(n):
    return [pl.BlockSpec((1, 2 * BS, WIDE), lambda g: (g, 0, 0))] * n


def rest(spec, outer, grad_two, slope, second, first, twiddle, plane_bwd):
    return pl.pallas_call(
        rest_kernel,
        grid=(GROUPS,),
        out_shape=(
            jax.ShapeDtypeStruct((ROWS, 128), f32),
            jax.ShapeDtypeStruct((64, 2 * PART + 8, 128), f32),
        ),
        in_specs=by_group(4) + vmem(5),
        out_specs=(pl.BlockSpec((ROWS, 128), lambda g: (0, 0)), *free(1)),
        scratch_shapes=[
            *[pltpu.VMEM((2 * BS, 256), f32), pltpu.VMEM((256, WIDE), f32)] * 2,
            *[pltpu.VMEM(PARTIAL, f32)] * 2,
            *sems(8),
        ],
        compiler_params=BIG,
        cost_estimate=pl.CostEstimate(
            flops=8_000_000_000, bytes_accessed=16_000_000, transcendentals=0
        ),
    )(spec, outer, grad_two, slope, second, first, twiddle, *plane_bwd)


def field(first, second, cotangent, tables):
    args = (
        first.reshape(NB, KZ, 2 * PART, 128),
        second.reshape(NB, KZ, 2 * PART + 8, 128),
        cotangent.reshape(2048, C),
        *tables,
    )
    out = jax.ShapeDtypeStruct((2048, C), bf16)
    scratch = [
        *held(args[0], args[0], *args[2:], out),
        pltpu.VMEM((2 * KZ, CELLS, C), f32),
        *sems(KZ, KZ, 3, 8),
    ]
    return call(field_kernel, out, args, scratch, 1_200_000_000, 7_000_000, free)


def rows_of(weight, part):
    return weight.reshape(4, 2, PART, 2 * BS)[:, part].reshape(BS, 2 * BS)


def mixing(weight):
    real = weight[0].T
    imag = weight[1].T
    return jnp.concatenate(
        [jnp.concatenate([real, -imag], axis=1), jnp.concatenate([imag, real], axis=1)], axis=0
    )


def stacked(value):
    high = lax.reduce_precision(value, 8, 7)
    return jnp.concatenate([high.astype(bf16), (value - high).astype(bf16)], axis=0)


def keep_half(value, axis, flip, bit):
    half = value.shape[0] // 2
    size = lax.axis_size(axis)
    mine = lax.dynamic_slice_in_dim(value, bit * half, half, 0)
    other = lax.dynamic_slice_in_dim(value, (1 - bit) * half, half, 0)
    return mine + lax.ppermute(other, axis, [(n, n ^ flip) for n in range(size)])


def join_half(value, axis, flip, bit):
    size = lax.axis_size(axis)
    other = lax.ppermute(value, axis, [(n, n ^ flip) for n in range(size)])
    return jnp.where(bit == 0, jnp.stack([value, other]), jnp.stack([other, value]))


def owned_rows(rows):
    dp = lax.axis_index("dp")
    px = lax.axis_index("px")
    py = lax.axis_index("py")
    rows = keep_half(rows, "dp", 1, dp % 2)
    rows = keep_half(rows, "dp", 2, dp // 2)
    rows = keep_half(rows, "px", 1, px % 2)
    pieces = rows.reshape(8, -1, 128)
    total = lax.dynamic_index_in_dim(pieces, py, 0, keepdims=False)
    for offset in range(1, 8):
        piece = lax.dynamic_index_in_dim(pieces, (py + offset) % 8, 0, keepdims=False)
        total = total + lax.ppermute(piece, "py", [(n, (n + offset) % 8) for n in range(8)])
    return total


def every_row(total):
    total = join_half(total, "dp", 1, lax.axis_index("dp") % 2)
    total = total.reshape(2, 2, NB, 2, 8, ROWS // 64, 128)
    return total.transpose(2, 0, 1, 3, 4, 5, 6).reshape(NB, ROWS, 128)


def exchange(value):
    return lax.all_to_all(value, ("px", "py"), split_axis=0, concat_axis=0, tiled=True)


def shards(state_field, cotangent, first_weight, first_bias, second_weight, second_bias):
    depth_fwd, depth_bwd = depth_tables()
    plane_fwd, plane_bwd = plane_tables()
    twiddle = twiddle_table()
    owner = lax.axis_index("px") * 8 + lax.axis_index("py")
    block = owner // KZ
    doubling = jnp.where(owner % KZ == 0, 1.0, 2.0).astype(f32).reshape(1, 1)

    first = mixing(lax.dynamic_index_in_dim(first_weight, block, 1, keepdims=False))
    second = mixing(lax.dynamic_index_in_dim(second_weight, block, 1, keepdims=False))
    bias_one = lax.dynamic_index_in_dim(first_bias, block, 1, keepdims=False).reshape(2 * BS, 1)
    bias_two = lax.dynamic_index_in_dim(second_bias, block, 1, keepdims=False).reshape(2 * BS, 1)

    state_spec = exchange(depth_forward(state_field, depth_fwd))
    cot_spec = exchange(depth_forward(cotangent, depth_fwd))
    spec, outer, slope, square = pl.pallas_call(
        forward_kernel,
        out_shape=(GROUPED,) * 4,
        in_specs=[pl.BlockSpec(memory_space=pltpu.SMEM)] + vmem(8),
        out_specs=tuple(vmem(4)),
        scratch_shapes=[pltpu.VMEM(SPECTRAL, f32)],
        compiler_params=BIG,
        cost_estimate=pl.CostEstimate(
            flops=8_000_000_000, bytes_accessed=16_000_000, transcendentals=1_500_000
        ),
    )(doubling, state_spec, twiddle, *plane_fwd, stacked(first), bias_one, stacked(second), bias_two)

    second_back = stacked(second.T)
    grad_two, plane = backward(
        cot_spec,
        twiddle,
        plane_fwd,
        plane_bwd,
        stacked(rows_of(first.T, 0)),
        second_back,
        slope,
        square,
    )
    first_part = exchange(plane)
    rows, plane = rest(
        spec, outer, grad_two, slope, second_back, stacked(rows_of(first.T, 1)), twiddle, plane_bwd
    )
    rows = owned_rows(rows)
    plane = lax.dynamic_update_slice(
        plane, jnp.broadcast_to(rows[None], (64, *rows.shape)), (0, 2 * PART, 0)
    )
    first_part, plane = lax.optimization_barrier((first_part, plane))
    second_part = exchange(plane)
    rows = join_half(second_part[:, 2 * PART :], "dp", 2, lax.axis_index("dp") // 2)
    state_grad = field(first_part, second_part, cotangent, depth_bwd).reshape(1, 8, 8, NZ, C)
    state_grad, rows = lax.optimization_barrier((state_grad, rows))
    rows = every_row(rows)
    grads_one = rows[:, : 2 * BS, :BS].reshape(NB, 2, BS, BS).transpose(1, 0, 2, 3)
    grads_two = rows[:, 2 * BS : 4 * BS, :BS].reshape(NB, 2, BS, BS).transpose(1, 0, 2, 3)
    biases = rows[:, 4 * BS : 4 * BS + 4, :BS].reshape(NB, 2, 2, BS)

    return (
        state_grad,
        grads_one,
        biases[:, 0].transpose(1, 0, 2),
        grads_two,
        biases[:, 1].transpose(1, 0, 2),
    )


def solution(mesh):
    in_specs = (
        P("dp", "px", "py", None, None),
        P("dp", "px", "py", None, None),
        P(),
        P(),
        P(),
        P(),
    )
    out_specs = (P("dp", "px", "py", None, None), P(), P(), P(), P())
    return jax.shard_map(shards, mesh=mesh, in_specs=in_specs, out_specs=out_specs, check_vma=False)
```

```python
import math

import jax
import jax.numpy as jnp
import ml_dtypes
import numpy as np
from jax import lax
from jax.experimental import pallas as pl
from jax.experimental.pallas import tpu as pltpu
from jax.sharding import PartitionSpec as P

NX = 64
NY = 64
NZ = 32
NB = 4
BS = 96
KZ = 16
C = 384
HALF = BS // 2
FIRST = 32
SECOND = HALF - FIRST
CELLS = 64
STEP = 8
GROUPS = 64 // STEP
WIDE = STEP * 64
ROWS = 512
SHRINK = 0.25
f32 = jnp.float32
bf16 = jnp.bfloat16
BIG = pltpu.CompilerParams(vmem_limit_bytes=62 * 1024 * 1024)
SPECTRAL = (64, 2 * HALF, 128)
GROUPED = jax.ShapeDtypeStruct((GROUPS, 2 * BS, WIDE), f32)


def np_split(table):
    high = table.astype(np.float32).astype(ml_dtypes.bfloat16)
    low = (table - high.astype(np.float64)).astype(np.float32).astype(ml_dtypes.bfloat16)
    return high, low


def depth_tables():
    k = np.arange(KZ)[:, None]
    z = np.arange(NZ)[None, :]
    angle = 2.0 * np.pi * (k * z % NZ) / NZ
    scale = 1.0 / math.sqrt(NX * NY * NZ)
    pair = np.stack([np.cos(angle), -np.sin(angle)], axis=1) * scale
    eye = np.eye(8)
    forward = np.einsum("kqz,ab->kqabz", pair, eye).reshape(256, 256)
    scheme = ((0, 1), (0, 1, 0))
    return [
        np.concatenate([np_split(table)[n] for n in order], axis=1)
        for table, order in zip((forward, forward.T.copy()), scheme)
    ]


def plane_tables():
    j = np.arange(8)
    eight = np.exp(-2j * np.pi * np.outer(j, j) / 8.0)
    both = np.einsum("xk,yl->xykl", eight, eight).reshape(64, 64)
    real = np.zeros((2, 64, 2, 64))
    real[0, :, 0] = both.real
    real[0, :, 1] = both.imag
    real[1, :, 0] = -both.imag
    real[1, :, 1] = both.real
    forward = np.einsum("qxpf,cd->qcxpdf", real, np.eye(2)).reshape(256, 256)
    tables = np_split(forward), np_split(forward.T.copy())
    return [np.concatenate([high, high, low], axis=0) for high, low in tables]


def twiddle_table():
    k2 = np.arange(8)
    j = np.arange(8)
    one = np.exp(-2j * np.pi * np.outer(k2, j) / 64.0)
    both = np.einsum("kx,ly->klxy", one, one).reshape(64, 64)
    both = np.tile(both, (1, 2))
    return np.stack([both.real, both.imag], axis=1).astype(np.float32)


def split(value):
    high = value.astype(bf16)
    low = (value - high.astype(f32)).astype(bf16)
    return high, low


def dot(left, right, dims=((1,), (0,))):
    return lax.dot_general(left, right, (dims, ((), ())), preferred_element_type=f32)


def thrice(pair, axis):
    high, low = pair
    return jnp.concatenate([high, low, high], axis=axis)


def paired(pair, axis):
    high, low = pair
    return jnp.concatenate([high, high, low], axis=axis)


def dot3(left, right, dims=((1,), (0,))):
    return dot(thrice(left, 1), paired(right, dims[1][0]), dims)


def product(weight_ref, value):
    return dot(weight_ref[...], paired(split(value), 0))


def swap(upper, lower):
    lane = lax.broadcasted_iota(jnp.int32, upper.shape, 1)
    first = jnp.where(lane < 64, upper, pltpu.roll(lower, 64, 1))
    second = jnp.where(lane < 64, pltpu.roll(upper, 64, 1), lower)
    return first, second


def fft(re, im, sign):
    n = len(re)
    if n == 1:
        return re, im
    even_re, even_im = fft(re[0::2], im[0::2], sign)
    odd_re, odd_im = fft(re[1::2], im[1::2], sign)
    out_re = [None] * n
    out_im = [None] * n
    root = math.sqrt(0.5)
    for k in range(n // 2):
        a, b = odd_re[k], odd_im[k]
        turn = k * (8 // n)
        if turn == 1:
            a, b = (a - sign * b) * root, (b + sign * a) * root
        elif turn == 2:
            a, b = -sign * b, sign * a
        elif turn == 3:
            a, b = (-a - sign * b) * root, (-b + sign * a) * root
        out_re[k], out_im[k] = even_re[k] + a, even_im[k] + b
        out_re[k + n // 2], out_im[k + n // 2] = even_re[k] - a, even_im[k] - b
    return out_re, out_im


def read(ref, index, tile):
    half = ref.shape[1] // 2
    rows = slice(tile * 8, tile * 8 + 8), slice(half + tile * 8, half + tile * 8 + 8)
    return ref[index, rows[0], :], ref[index, rows[1], :]


def write(ref, index, tile, re, im):
    half = ref.shape[1] // 2
    ref[index, tile * 8 : tile * 8 + 8, :] = re
    ref[index, half + tile * 8 : half + tile * 8 + 8, :] = im


def senders(src_ref, dst_ref, sign, before, after):
    def body(p, carry):
        before(p)
        for tile in range(src_ref.shape[1] // 16):
            re, im = zip(*[read(src_ref, p * 8 + n, tile) for n in range(8)])
            re, im = fft(re, im, sign)
            for n in range(8):
                write(dst_ref, p * 8 + n, tile, re[n], im[n])
        after(p)
        return carry

    lax.fori_loop(0, 8, body, 0)


def turned(a, b, twiddle_ref, index, sign):
    c = twiddle_ref[index, 0:1, :]
    s = twiddle_ref[index, 1:2, :] * sign
    return a * c - b * s, a * s + b * c


def plane_forward(src_ref, work_ref, twiddle_ref, before):
    senders(src_ref, work_ref, -1.0, before, lambda p: None)

    def body(p, carry):
        for tile in range(HALF // 8):
            re, im = zip(*[read(work_ref, n * 8 + p, tile) for n in range(8)])
            re, im = fft(re, im, -1.0)
            for n in range(8):
                write(work_ref, n * 8 + p, tile, *turned(re[n], im[n], twiddle_ref, n * 8 + p, 1.0))
        return carry

    lax.fori_loop(0, 8, body, 0)


def plane_backward(work_ref, out_ref, twiddle_ref, after):
    def body(p, carry):
        for tile in range(work_ref.shape[1] // 16):
            pairs = [
                turned(*read(work_ref, n * 8 + p, tile), twiddle_ref, n * 8 + p, -1.0)
                for n in range(8)
            ]
            re, im = fft(*zip(*pairs), 1.0)
            for n in range(8):
                write(work_ref, n * 8 + p, tile, re[n], im[n])
        return carry

    lax.fori_loop(0, 8, body, 0)
    senders(work_ref, out_ref, 1.0, lambda p: None, after)


def load_group(work_ref, group, table_ref):
    rows = [
        jnp.concatenate(
            [work_ref[group * STEP + n, :HALF], work_ref[group * STEP + n, HALF:]], axis=1
        )
        for n in range(STEP)
    ]
    values = dot(thrice(split(jnp.concatenate(rows, axis=0)), 1), table_ref[...])
    pairs = []
    for pair in range(STEP // 2):
        part = []
        for q in range(2):
            lanes = slice(q * 128, (q + 1) * 128)
            upper = values[2 * pair * HALF : (2 * pair + 1) * HALF, lanes]
            lower = values[(2 * pair + 1) * HALF : (2 * pair + 2) * HALF, lanes]
            part.extend(swap(upper, lower))
        pairs.append(jnp.concatenate(part, axis=0))
    return jnp.concatenate(pairs, axis=1)


def store_group(work_ref, group, spectral, table_ref):
    count = spectral.shape[0] // 4
    rows = []
    for pair in range(STEP // 2):
        part = spectral[:, pair * 128 : (pair + 1) * 128]
        parts = [
            swap(
                part[2 * q * count : (2 * q + 1) * count],
                part[(2 * q + 1) * count : (2 * q + 2) * count],
            )
            for q in range(2)
        ]
        for n in range(2):
            rows.append(jnp.concatenate([parts[0][n], parts[1][n]], axis=1))
    values = dot(thrice(split(jnp.concatenate(rows, axis=0)), 1), table_ref[...])
    for n in range(STEP):
        for q in range(2):
            work_ref[group * STEP + n, q * count : (q + 1) * count] = values[
                n * count : (n + 1) * count, q * 128 : (q + 1) * 128
            ]


def depth_kernel(field_hbm, both_hbm, out_hbm, field_ref, both_ref, out_ref, work_ref, sems, out_sems):
    table = pltpu.make_async_copy(both_hbm, both_ref, sems.at[8])
    table.start()
    copies = []
    for g in range(8):
        span = pl.ds(g * 256, 256)
        copies.append(pltpu.make_async_copy(field_hbm.at[span], field_ref.at[span], sems.at[g]))
        copies[-1].start()
    table.wait()
    for g in range(8):
        copies[g].wait()
        rows = field_ref[g * 256 : (g + 1) * 256, :]
        values = dot(both_ref[...], jnp.concatenate([rows, rows], axis=0))
        work_ref[:, g * 8 : (g + 1) * 8, :] = values.reshape(2 * KZ, 8, C)
    sends = []
    for k in range(KZ):
        values = work_ref[2 * k : 2 * k + 2].reshape(2 * CELLS, C).T
        for b in range(NB):
            upper = values[b * BS : b * BS + HALF]
            lower = values[b * BS + HALF : (b + 1) * BS]
            out_ref[b, k, :HALF], out_ref[b, k, HALF:] = swap(upper, lower)
        sends.append(pltpu.make_async_copy(out_ref.at[:, k], out_hbm.at[:, k], out_sems.at[k]))
        sends[-1].start()
    for send in sends:
        send.wait()


def forward_kernel(
    doubling_ref, src_ref, twiddle_ref, t_ref, w1, b1, w2, b2,
    spec_ref, outer_ref, slope_ref, square_ref, work_ref,
):
    plane_forward(src_ref, work_ref, twiddle_ref, lambda p: None)
    root = math.sqrt(2.0 / math.pi)

    def body(g, carry):
        spectral = load_group(work_ref, g, t_ref)
        spec_ref[g] = spectral
        pre = product(w1, spectral) + b1[...]
        pre_sq = pre * pre
        t = jnp.tanh(root * (pre + 0.044715 * (pre * pre_sq)))
        outer = 0.5 * pre * (1.0 + t)
        outer_ref[g] = outer
        slope_ref[g] = 0.5 * (1.0 + t) + 0.5 * pre * (1.0 - t * t) * (
            root * (1.0 + 3.0 * 0.044715 * pre_sq)
        )
        pre_two = product(w2, outer) + b2[...]
        t2 = jnp.tanh(pre_two * (1.0 / SHRINK))
        square_ref[g] = t2 * t2 * doubling_ref[0, 0]
        return carry

    lax.fori_loop(0, GROUPS, body, 0)


def block_of(hbm, ref, sems, p):
    span = pl.ds(p * 8, 8)
    return pltpu.make_async_copy(hbm.at[span], ref.at[span], sems.at[p])


def backward_kernel(
    src_hbm, twiddle_hbm, t_hbm, back_hbm, w1_hbm, w2_hbm, slope_hbm, square_hbm,
    two_hbm, out_hbm,
    src_ref, twiddle_ref, t_ref, back_ref, w1, w2, slope_ref, square_ref,
    two_ref, out_ref, work_ref, part_ref, src_sems, sems, square_sems, slope_sems,
    two_sems, out_sems,
):
    for p in range(8):
        block_of(src_hbm, src_ref, src_sems, p).start()
    pairs = (
        (twiddle_hbm, twiddle_ref), (t_hbm, t_ref), (w2_hbm, w2),
        (w1_hbm, w1), (back_hbm, back_ref),
    )
    loads = [pltpu.make_async_copy(a, b, sems.at[n]) for n, (a, b) in enumerate(pairs)]
    for load in loads:
        load.start()
    loads[0].wait()

    def before(p):
        block_of(src_hbm, src_ref, src_sems, p).wait()
        pltpu.make_async_copy(square_hbm.at[p], square_ref.at[p], square_sems.at[p]).start()
        pltpu.make_async_copy(slope_hbm.at[p], slope_ref.at[p], slope_sems.at[p]).start()

    plane_forward(src_ref, work_ref, twiddle_ref, before)
    for load in loads[1:]:
        load.wait()

    sends = []
    spectral = load_group(work_ref, 0, t_ref)
    for g in range(GROUPS):
        following = load_group(work_ref, g + 1, t_ref) if g + 1 < GROUPS else None
        pltpu.make_async_copy(square_hbm.at[g], square_ref.at[g], square_sems.at[g]).wait()
        grad_two = spectral * square_ref[g]
        two_ref[g] = grad_two
        sends.append(pltpu.make_async_copy(two_ref.at[g], two_hbm.at[g], two_sems.at[g]))
        sends[-1].start()
        pltpu.make_async_copy(slope_hbm.at[g], slope_ref.at[g], slope_sems.at[g]).wait()
        grad_one = product(w2, grad_two) * slope_ref[g]
        store_group(part_ref, g, product(w1, grad_one), back_ref)
        spectral = following
    plane_backward(
        part_ref, out_ref, twiddle_ref, lambda p: block_of(out_ref, out_hbm, out_sems, p).start()
    )
    for send in sends:
        send.wait()
    for p in range(8):
        block_of(out_ref, out_hbm, out_sems, p).wait()


def spread(value):
    gap = jnp.zeros((128 - BS, value.shape[1]), value.dtype)
    return jnp.concatenate([value[:BS], gap, value[BS:], gap], axis=0)


def rest_kernel(
    spec_ref, outer_ref, two_ref, slope_ref, w2, w1, twiddle_ref, back_ref,
    out_ref, plane_hbm,
    t1_ref, s1_ref, t2_ref, s2_ref, part_ref, plane_ref, sends,
):
    lanes = ((1,), (1,))
    g = pl.program_id(0)

    @pl.when(g == 0)
    def _():
        for ref in (t1_ref, s1_ref, t2_ref, s2_ref):
            ref[...] = jnp.zeros(ref.shape, f32)

    grad_two = two_ref[0]
    two = spread(grad_two)
    t2_ref[...] += dot3(split(outer_ref[0]), split(two), lanes)
    s2_ref[...] += two
    grad_one = product(w2, grad_two) * slope_ref[0]
    one = spread(grad_one)
    t1_ref[...] += dot3(split(spec_ref[0]), split(one), lanes)
    s1_ref[...] += one
    store_group(part_ref, g, product(w1, grad_one), back_ref)

    def send(p):
        span = pl.ds(p * 8, 8)
        rows = pl.ds(0, 2 * SECOND)
        return pltpu.make_async_copy(plane_ref.at[span], plane_hbm.at[span, rows], sends.at[p])

    @pl.when(g == GROUPS - 1)
    def _():
        plane_backward(part_ref, plane_ref, twiddle_ref, lambda p: send(p).start())
        norm = 1.0 / math.sqrt(4 * NX * NY * KZ)
        ones = jnp.ones((8, WIDE), bf16)
        row = lax.broadcasted_iota(jnp.int32, (8, 128), 0)
        out_ref[4 * BS :] = jnp.zeros((ROWS - 4 * BS, 128), f32)
        biases = jnp.zeros((8, 128), f32)
        for n, (table_ref, total_ref) in enumerate(((t1_ref, s1_ref), (t2_ref, s2_ref))):
            table = table_ref[...]
            real = table[:BS, :128] + table[BS:, 128:]
            imag = table[:BS, 128:] - table[BS:, :128]
            out_ref[2 * n * BS : (2 * n + 1) * BS] = real * norm
            out_ref[(2 * n + 1) * BS : (2 * n + 2) * BS] = imag * norm
            high, low = split(total_ref[...])
            sums = dot(ones, high, lanes) + dot(ones, low, lanes)
            for q in range(2):
                biases = jnp.where(row == 2 * n + q, sums[:, q * 128 : (q + 1) * 128], biases)
        out_ref[4 * BS : 4 * BS + 8] = biases * norm
        for p in range(8):
            send(p).wait()


def field_kernel(
    first_hbm, second_hbm, cotangent_hbm, table_hbm, out_hbm,
    first_ref, second_ref, cotangent_ref, table_ref, out_ref, work_ref,
    first_sems, second_sems, sems, out_sems,
):
    loads = []
    for k in range(KZ):
        span = pl.ds(0, 2 * SECOND)
        loads.append(
            (
                pltpu.make_async_copy(first_hbm.at[:, k], first_ref.at[:, k], first_sems.at[k]),
                pltpu.make_async_copy(
                    second_hbm.at[:, k, span], second_ref.at[:, k], second_sems.at[k]
                ),
            )
        )
    pairs = ((table_hbm, table_ref), (cotangent_hbm, cotangent_ref))
    others = [pltpu.make_async_copy(a, b, sems.at[n]) for n, (a, b) in enumerate(pairs)]
    for load in loads:
        load[0].start()
        load[1].start()
    for load in others:
        load.start()
    for k in range(KZ):
        loads[k][0].wait()
        loads[k][1].wait()
        parts = []
        for b in range(NB):
            left = swap(first_ref[b, k, :FIRST], first_ref[b, k, FIRST:])
            right = swap(second_ref[b, k, :SECOND], second_ref[b, k, SECOND:])
            parts.extend([left[0], right[0], left[1], right[1]])
        values = jnp.concatenate(parts, axis=0).T
        work_ref[2 * k : 2 * k + 2] = values.reshape(2, CELLS, C)
    for load in others:
        load.wait()
    sends = []
    for g in range(8):
        values = product(table_ref, work_ref[:, g * 8 : (g + 1) * 8, :].reshape(256, C))
        span = slice(g * 256, (g + 1) * 256)
        out_ref[span, :] = (cotangent_ref[span, :].astype(f32) + values).astype(bf16)
        rows = pl.ds(g * 256, 256)
        sends.append(pltpu.make_async_copy(out_ref.at[rows], out_hbm.at[rows], out_sems.at[g]))
        sends[-1].start()
    for send in sends:
        send.wait()


def vmem(n):
    return [pl.BlockSpec(memory_space=pltpu.VMEM)] * n


def free(n):
    return [pl.BlockSpec(memory_space=pl.ANY)] * n


def held(*values):
    return [pltpu.VMEM(v.shape, v.dtype) for v in values]


def sems(*counts):
    return [pltpu.SemaphoreType.DMA((n,)) for n in counts]


def call(kernel, out_shape, args, scratch, flops, moved, place=vmem):
    outs = len(out_shape) if isinstance(out_shape, tuple) else 1
    return pl.pallas_call(
        kernel,
        out_shape=out_shape,
        in_specs=place(len(args)),
        out_specs=tuple(place(outs)) if isinstance(out_shape, tuple) else place(1)[0],
        scratch_shapes=scratch,
        compiler_params=BIG,
        cost_estimate=pl.CostEstimate(flops=flops, bytes_accessed=moved, transcendentals=0),
    )(*args)


def depth_forward(field, tables):
    args = (field.reshape(2048, C), tables)
    out = jax.ShapeDtypeStruct((NB, KZ, 2 * HALF, 128), f32)
    scratch = [*held(*args, out), pltpu.VMEM((2 * KZ, CELLS, C), f32), *sems(9, KZ)]
    return call(depth_kernel, out, args, scratch, 800_000_000, 5_000_000, free).reshape(SPECTRAL)


def backward(cot_spec, twiddle, plane_fwd, plane_bwd, first, second, slope, square):
    args = (cot_spec, twiddle, plane_fwd, plane_bwd, first, second, slope, square)
    outs = (GROUPED, jax.ShapeDtypeStruct((64, 2 * FIRST, 128), f32))
    scratch = [
        *held(*args, *outs),
        pltpu.VMEM(SPECTRAL, f32),
        pltpu.VMEM((64, 2 * FIRST, 128), f32),
        *sems(8, 5, *[GROUPS] * 3, 8),
    ]
    return call(backward_kernel, outs, args, scratch, 10_000_000_000, 20_000_000, free)


def by_group(n):
    return [pl.BlockSpec((1, 2 * BS, WIDE), lambda g: (g, 0, 0))] * n


def rest(spec, outer, grad_two, slope, second, first, twiddle, plane_bwd):
    return pl.pallas_call(
        rest_kernel,
        grid=(GROUPS,),
        out_shape=(
            jax.ShapeDtypeStruct((ROWS, 128), f32),
            jax.ShapeDtypeStruct((64, 2 * SECOND + 8, 128), f32),
        ),
        in_specs=by_group(4) + vmem(4),
        out_specs=(pl.BlockSpec((ROWS, 128), lambda g: (0, 0)), *free(1)),
        scratch_shapes=[
            *[pltpu.VMEM((2 * BS, 256), f32), pltpu.VMEM((256, WIDE), f32)] * 2,
            *[pltpu.VMEM((64, 2 * SECOND, 128), f32)] * 2,
            *sems(8),
        ],
        compiler_params=BIG,
        cost_estimate=pl.CostEstimate(
            flops=8_000_000_000, bytes_accessed=16_000_000, transcendentals=0
        ),
    )(spec, outer, grad_two, slope, second, first, twiddle, plane_bwd)


def field(first, second, cotangent, tables):
    args = (
        first.reshape(NB, KZ, 2 * FIRST, 128),
        second.reshape(NB, KZ, 2 * SECOND + 8, 128),
        cotangent.reshape(2048, C),
        tables,
    )
    out = jax.ShapeDtypeStruct((2048, C), bf16)
    scratch = [
        *held(args[0], jax.ShapeDtypeStruct((NB, KZ, 2 * SECOND, 128), f32), *args[2:], out),
        pltpu.VMEM((2 * KZ, CELLS, C), f32),
        *sems(KZ, KZ, 2, 8),
    ]
    return call(field_kernel, out, args, scratch, 1_200_000_000, 7_000_000, free)


def rows_of(weight, start, stop):
    return weight.reshape(4, HALF, 2 * BS)[:, start:stop].reshape(-1, 2 * BS)


def mixing(weight):
    real = weight[0].T
    imag = weight[1].T
    return jnp.concatenate(
        [jnp.concatenate([real, -imag], axis=1), jnp.concatenate([imag, real], axis=1)], axis=0
    )


def stacked(value):
    high = lax.reduce_precision(value, 8, 7)
    return thrice((high.astype(bf16), (value - high).astype(bf16)), 1)


def keep_half(value, axis, flip, bit):
    half = value.shape[0] // 2
    size = lax.axis_size(axis)
    mine = lax.dynamic_slice_in_dim(value, bit * half, half, 0)
    other = lax.dynamic_slice_in_dim(value, (1 - bit) * half, half, 0)
    return mine + lax.ppermute(other, axis, [(n, n ^ flip) for n in range(size)])


def join_half(value, axis, flip, bit):
    size = lax.axis_size(axis)
    other = lax.ppermute(value, axis, [(n, n ^ flip) for n in range(size)])
    return jnp.where(bit == 0, jnp.stack([value, other]), jnp.stack([other, value]))


def owned_rows(rows):
    dp = lax.axis_index("dp")
    px = lax.axis_index("px")
    py = lax.axis_index("py")
    rows = keep_half(rows, "dp", 1, dp % 2)
    rows = keep_half(rows, "dp", 2, dp // 2)
    rows = keep_half(rows, "px", 1, px % 2)
    pieces = rows.reshape(8, -1, 128)
    total = lax.dynamic_index_in_dim(pieces, py, 0, keepdims=False)
    for offset in range(1, 8):
        piece = lax.dynamic_index_in_dim(pieces, (py + offset) % 8, 0, keepdims=False)
        total = total + lax.ppermute(piece, "py", [(n, (n + offset) % 8) for n in range(8)])
    return total


def every_row(total):
    total = join_half(total, "dp", 1, lax.axis_index("dp") % 2)
    total = total.reshape(2, 2, NB, 2, 8, ROWS // 64, 128)
    return total.transpose(2, 0, 1, 3, 4, 5, 6).reshape(NB, ROWS, 128)


def exchange(value):
    return lax.all_to_all(value, ("px", "py"), split_axis=0, concat_axis=0, tiled=True)


def shards(state_field, cotangent, first_weight, first_bias, second_weight, second_bias):
    depth_fwd, depth_bwd = depth_tables()
    plane_fwd, plane_bwd = plane_tables()
    twiddle = twiddle_table()
    owner = lax.axis_index("px") * 8 + lax.axis_index("py")
    block = owner // KZ
    doubling = jnp.where(owner % KZ == 0, 1.0, 2.0).astype(f32).reshape(1, 1)

    first = mixing(lax.dynamic_index_in_dim(first_weight, block, 1, keepdims=False))
    second = mixing(lax.dynamic_index_in_dim(second_weight, block, 1, keepdims=False))
    bias_one = lax.dynamic_index_in_dim(first_bias, block, 1, keepdims=False).reshape(2 * BS, 1)
    bias_two = lax.dynamic_index_in_dim(second_bias, block, 1, keepdims=False).reshape(2 * BS, 1)

    state_spec = exchange(depth_forward(state_field, depth_fwd))
    cot_spec = exchange(depth_forward(cotangent, depth_fwd))
    spec, outer, slope, square = pl.pallas_call(
        forward_kernel,
        out_shape=(GROUPED,) * 4,
        in_specs=[pl.BlockSpec(memory_space=pltpu.SMEM)] + vmem(7),
        out_specs=tuple(vmem(4)),
        scratch_shapes=[pltpu.VMEM(SPECTRAL, f32)],
        compiler_params=BIG,
        cost_estimate=pl.CostEstimate(
            flops=8_000_000_000, bytes_accessed=16_000_000, transcendentals=1_500_000
        ),
    )(doubling, state_spec, twiddle, plane_fwd, stacked(first), bias_one, stacked(second), bias_two)

    second_back = stacked(second.T)
    grad_two, plane = backward(
        cot_spec,
        twiddle,
        plane_fwd,
        plane_bwd,
        stacked(rows_of(first.T, 0, FIRST)),
        second_back,
        slope,
        square,
    )
    first_part = exchange(plane)
    rows, plane = rest(
        spec, outer, grad_two, slope, second_back, stacked(rows_of(first.T, FIRST, HALF)), twiddle, plane_bwd
    )
    rows = owned_rows(rows)
    plane = lax.dynamic_update_slice(
        plane, jnp.broadcast_to(rows[None], (64, *rows.shape)), (0, 2 * SECOND, 0)
    )
    first_part, plane = lax.optimization_barrier((first_part, plane))
    second_part = exchange(plane)
    rows = join_half(second_part[:, 2 * SECOND :], "dp", 2, lax.axis_index("dp") // 2)
    state_grad = field(first_part, second_part, cotangent, depth_bwd).reshape(1, 8, 8, NZ, C)
    state_grad, rows = lax.optimization_barrier((state_grad, rows))
    rows = every_row(rows)
    grads_one = rows[:, : 2 * BS, :BS].reshape(NB, 2, BS, BS).transpose(1, 0, 2, 3)
    grads_two = rows[:, 2 * BS : 4 * BS, :BS].reshape(NB, 2, BS, BS).transpose(1, 0, 2, 3)
    biases = rows[:, 4 * BS : 4 * BS + 4, :BS].reshape(NB, 2, 2, BS)

    return (
        state_grad,
        grads_one,
        biases[:, 0].transpose(1, 0, 2),
        grads_two,
        biases[:, 1].transpose(1, 0, 2),
    )


def solution(mesh):
    in_specs = (
        P("dp", "px", "py", None, None),
        P("dp", "px", "py", None, None),
        P(),
        P(),
        P(),
        P(),
    )
    out_specs = (P("dp", "px", "py", None, None), P(), P(), P(), P())
    return jax.shard_map(shards, mesh=mesh, in_specs=in_specs, out_specs=out_specs, check_vma=False)
```

```python
import math

import jax
import jax.numpy as jnp
import ml_dtypes
import numpy as np
from jax import lax
from jax.experimental import pallas as pl
from jax.experimental.pallas import tpu as pltpu
from jax.sharding import PartitionSpec as P

NX = 64
NY = 64
NZ = 32
NB = 4
BS = 96
KZ = 16
C = 384
HALF = BS // 2
FIRST = 40
SECOND = HALF - FIRST
CELLS = 64
STEP = 8
GROUPS = 64 // STEP
WIDE = STEP * 64
ROWS = 512
SHRINK = 0.25
f32 = jnp.float32
bf16 = jnp.bfloat16
BIG = pltpu.CompilerParams(vmem_limit_bytes=62 * 1024 * 1024)
SPECTRAL = (64, 2 * HALF, 128)
GROUPED = jax.ShapeDtypeStruct((GROUPS, 2 * BS, WIDE), f32)


def np_split(table):
    high = table.astype(np.float32).astype(ml_dtypes.bfloat16)
    low = (table - high.astype(np.float64)).astype(np.float32).astype(ml_dtypes.bfloat16)
    return high, low


def depth_tables():
    k = np.arange(KZ)[:, None]
    z = np.arange(NZ)[None, :]
    angle = 2.0 * np.pi * (k * z % NZ) / NZ
    scale = 1.0 / math.sqrt(NX * NY * NZ)
    pair = np.stack([np.cos(angle), -np.sin(angle)], axis=1) * scale
    eye = np.eye(8)
    forward = np.einsum("kqz,ab->kqabz", pair, eye).reshape(256, 256)
    scheme = ((0, 1), (0, 1, 0))
    return [
        np.concatenate([np_split(table)[n] for n in order], axis=1)
        for table, order in zip((forward, forward.T.copy()), scheme)
    ]


def plane_tables():
    j = np.arange(8)
    eight = np.exp(-2j * np.pi * np.outer(j, j) / 8.0)
    both = np.einsum("xk,yl->xykl", eight, eight).reshape(64, 64)
    real = np.zeros((2, 64, 2, 64))
    real[0, :, 0] = both.real
    real[0, :, 1] = both.imag
    real[1, :, 0] = -both.imag
    real[1, :, 1] = both.real
    forward = np.einsum("qxpf,cd->qcxpdf", real, np.eye(2)).reshape(256, 256)
    tables = np_split(forward), np_split(forward.T.copy())
    return [np.concatenate([high, high, low], axis=0) for high, low in tables]


def twiddle_table():
    k2 = np.arange(8)
    j = np.arange(8)
    one = np.exp(-2j * np.pi * np.outer(k2, j) / 64.0)
    both = np.einsum("kx,ly->klxy", one, one).reshape(64, 64)
    both = np.tile(both, (1, 2))
    return np.stack([both.real, both.imag], axis=1).astype(np.float32)


def split(value):
    high = value.astype(bf16)
    low = (value - high.astype(f32)).astype(bf16)
    return high, low


def dot(left, right, dims=((1,), (0,))):
    return lax.dot_general(left, right, (dims, ((), ())), preferred_element_type=f32)


def thrice(pair, axis):
    high, low = pair
    return jnp.concatenate([high, low, high], axis=axis)


def paired(pair, axis):
    high, low = pair
    return jnp.concatenate([high, high, low], axis=axis)


def dot3(left, right, dims=((1,), (0,))):
    return dot(thrice(left, 1), paired(right, dims[1][0]), dims)


def product(weight_ref, value):
    return dot(weight_ref[...], paired(split(value), 0))


def swap(upper, lower):
    lane = lax.broadcasted_iota(jnp.int32, upper.shape, 1)
    first = jnp.where(lane < 64, upper, pltpu.roll(lower, 64, 1))
    second = jnp.where(lane < 64, pltpu.roll(upper, 64, 1), lower)
    return first, second


def fft(re, im, sign):
    n = len(re)
    if n == 1:
        return re, im
    even_re, even_im = fft(re[0::2], im[0::2], sign)
    odd_re, odd_im = fft(re[1::2], im[1::2], sign)
    out_re = [None] * n
    out_im = [None] * n
    root = math.sqrt(0.5)
    for k in range(n // 2):
        a, b = odd_re[k], odd_im[k]
        turn = k * (8 // n)
        if turn == 1:
            a, b = (a - sign * b) * root, (b + sign * a) * root
        elif turn == 2:
            a, b = -sign * b, sign * a
        elif turn == 3:
            a, b = (-a - sign * b) * root, (-b + sign * a) * root
        out_re[k], out_im[k] = even_re[k] + a, even_im[k] + b
        out_re[k + n // 2], out_im[k + n // 2] = even_re[k] - a, even_im[k] - b
    return out_re, out_im


def read(ref, index, tile):
    half = ref.shape[1] // 2
    rows = slice(tile * 8, tile * 8 + 8), slice(half + tile * 8, half + tile * 8 + 8)
    return ref[index, rows[0], :], ref[index, rows[1], :]


def write(ref, index, tile, re, im):
    half = ref.shape[1] // 2
    ref[index, tile * 8 : tile * 8 + 8, :] = re
    ref[index, half + tile * 8 : half + tile * 8 + 8, :] = im


def senders(src_ref, dst_ref, sign, before, after):
    def body(p, carry):
        before(p)
        for tile in range(src_ref.shape[1] // 16):
            re, im = zip(*[read(src_ref, p * 8 + n, tile) for n in range(8)])
            re, im = fft(re, im, sign)
            for n in range(8):
                write(dst_ref, p * 8 + n, tile, re[n], im[n])
        after(p)
        return carry

    lax.fori_loop(0, 8, body, 0)


def turned(a, b, twiddle_ref, index, sign):
    c = twiddle_ref[index, 0:1, :]
    s = twiddle_ref[index, 1:2, :] * sign
    return a * c - b * s, a * s + b * c


def plane_forward(src_ref, work_ref, twiddle_ref, before):
    senders(src_ref, work_ref, -1.0, before, lambda p: None)

    def body(p, carry):
        for tile in range(HALF // 8):
            re, im = zip(*[read(work_ref, n * 8 + p, tile) for n in range(8)])
            re, im = fft(re, im, -1.0)
            for n in range(8):
                write(work_ref, n * 8 + p, tile, *turned(re[n], im[n], twiddle_ref, n * 8 + p, 1.0))
        return carry

    lax.fori_loop(0, 8, body, 0)


def plane_backward(work_ref, out_ref, twiddle_ref, after):
    def body(p, carry):
        for tile in range(work_ref.shape[1] // 16):
            pairs = [
                turned(*read(work_ref, n * 8 + p, tile), twiddle_ref, n * 8 + p, -1.0)
                for n in range(8)
            ]
            re, im = fft(*zip(*pairs), 1.0)
            for n in range(8):
                write(work_ref, n * 8 + p, tile, re[n], im[n])
        return carry

    lax.fori_loop(0, 8, body, 0)
    senders(work_ref, out_ref, 1.0, lambda p: None, after)


def load_group(work_ref, group, table_ref):
    rows = [
        jnp.concatenate(
            [work_ref[group * STEP + n, :HALF], work_ref[group * STEP + n, HALF:]], axis=1
        )
        for n in range(STEP)
    ]
    values = dot(thrice(split(jnp.concatenate(rows, axis=0)), 1), table_ref[...])
    pairs = []
    for pair in range(STEP // 2):
        part = []
        for q in range(2):
            lanes = slice(q * 128, (q + 1) * 128)
            upper = values[2 * pair * HALF : (2 * pair + 1) * HALF, lanes]
            lower = values[(2 * pair + 1) * HALF : (2 * pair + 2) * HALF, lanes]
            part.extend(swap(upper, lower))
        pairs.append(jnp.concatenate(part, axis=0))
    return jnp.concatenate(pairs, axis=1)


def store_group(work_ref, group, spectral, table_ref):
    count = spectral.shape[0] // 4
    rows = []
    for pair in range(STEP // 2):
        part = spectral[:, pair * 128 : (pair + 1) * 128]
        parts = [
            swap(
                part[2 * q * count : (2 * q + 1) * count],
                part[(2 * q + 1) * count : (2 * q + 2) * count],
            )
            for q in range(2)
        ]
        for n in range(2):
            rows.append(jnp.concatenate([parts[0][n], parts[1][n]], axis=1))
    values = dot(thrice(split(jnp.concatenate(rows, axis=0)), 1), table_ref[...])
    for n in range(STEP):
        for q in range(2):
            work_ref[group * STEP + n, q * count : (q + 1) * count] = values[
                n * count : (n + 1) * count, q * 128 : (q + 1) * 128
            ]


def depth_kernel(field_hbm, both_hbm, out_hbm, field_ref, both_ref, out_ref, work_ref, sems, out_sems):
    table = pltpu.make_async_copy(both_hbm, both_ref, sems.at[8])
    table.start()
    copies = []
    for g in range(8):
        span = pl.ds(g * 256, 256)
        copies.append(pltpu.make_async_copy(field_hbm.at[span], field_ref.at[span], sems.at[g]))
        copies[-1].start()
    table.wait()
    for g in range(8):
        copies[g].wait()
        rows = field_ref[g * 256 : (g + 1) * 256, :]
        values = dot(both_ref[...], jnp.concatenate([rows, rows], axis=0))
        work_ref[:, g * 8 : (g + 1) * 8, :] = values.reshape(2 * KZ, 8, C)
    sends = []
    for k in range(KZ):
        values = work_ref[2 * k : 2 * k + 2].reshape(2 * CELLS, C).T
        for b in range(NB):
            upper = values[b * BS : b * BS + HALF]
            lower = values[b * BS + HALF : (b + 1) * BS]
            out_ref[b, k, :HALF], out_ref[b, k, HALF:] = swap(upper, lower)
        sends.append(pltpu.make_async_copy(out_ref.at[:, k], out_hbm.at[:, k], out_sems.at[k]))
        sends[-1].start()
    for send in sends:
        send.wait()


def forward_kernel(
    doubling_ref, src_ref, twiddle_ref, t_ref, w1, b1, w2, b2,
    spec_ref, outer_ref, slope_ref, square_ref, work_ref,
):
    plane_forward(src_ref, work_ref, twiddle_ref, lambda p: None)
    root = math.sqrt(2.0 / math.pi)

    def body(g, carry):
        spectral = load_group(work_ref, g, t_ref)
        spec_ref[g] = spectral
        pre = product(w1, spectral) + b1[...]
        pre_sq = pre * pre
        t = jnp.tanh(root * (pre + 0.044715 * (pre * pre_sq)))
        outer = 0.5 * pre * (1.0 + t)
        outer_ref[g] = outer
        slope_ref[g] = 0.5 * (1.0 + t) + 0.5 * pre * (1.0 - t * t) * (
            root * (1.0 + 3.0 * 0.044715 * pre_sq)
        )
        pre_two = product(w2, outer) + b2[...]
        t2 = jnp.tanh(pre_two * (1.0 / SHRINK))
        square_ref[g] = t2 * t2 * doubling_ref[0, 0]
        return carry

    lax.fori_loop(0, GROUPS, body, 0)


def block_of(hbm, ref, sems, p):
    span = pl.ds(p * 8, 8)
    return pltpu.make_async_copy(hbm.at[span], ref.at[span], sems.at[p])


def backward_kernel(
    src_hbm, twiddle_hbm, t_hbm, back_hbm, w1_hbm, w2_hbm, slope_hbm, square_hbm,
    two_hbm, out_hbm,
    src_ref, twiddle_ref, t_ref, back_ref, w1, w2, slope_ref, square_ref,
    two_ref, out_ref, work_ref, part_ref, src_sems, sems, square_sems, slope_sems,
    two_sems, out_sems,
):
    for p in range(8):
        block_of(src_hbm, src_ref, src_sems, p).start()
    pairs = (
        (twiddle_hbm, twiddle_ref), (t_hbm, t_ref), (w2_hbm, w2),
        (w1_hbm, w1), (back_hbm, back_ref),
    )
    loads = [pltpu.make_async_copy(a, b, sems.at[n]) for n, (a, b) in enumerate(pairs)]
    for load in loads:
        load.start()
    loads[0].wait()

    def before(p):
        block_of(src_hbm, src_ref, src_sems, p).wait()
        pltpu.make_async_copy(square_hbm.at[p], square_ref.at[p], square_sems.at[p]).start()
        pltpu.make_async_copy(slope_hbm.at[p], slope_ref.at[p], slope_sems.at[p]).start()

    plane_forward(src_ref, work_ref, twiddle_ref, before)
    for load in loads[1:]:
        load.wait()

    sends = []
    spectral = load_group(work_ref, 0, t_ref)
    for g in range(GROUPS):
        following = load_group(work_ref, g + 1, t_ref) if g + 1 < GROUPS else None
        pltpu.make_async_copy(square_hbm.at[g], square_ref.at[g], square_sems.at[g]).wait()
        grad_two = spectral * square_ref[g]
        two_ref[g] = grad_two
        sends.append(pltpu.make_async_copy(two_ref.at[g], two_hbm.at[g], two_sems.at[g]))
        sends[-1].start()
        pltpu.make_async_copy(slope_hbm.at[g], slope_ref.at[g], slope_sems.at[g]).wait()
        grad_one = product(w2, grad_two) * slope_ref[g]
        store_group(part_ref, g, product(w1, grad_one), back_ref)
        spectral = following
    plane_backward(
        part_ref, out_ref, twiddle_ref, lambda p: block_of(out_ref, out_hbm, out_sems, p).start()
    )
    for send in sends:
        send.wait()
    for p in range(8):
        block_of(out_ref, out_hbm, out_sems, p).wait()


def spread(value):
    gap = jnp.zeros((128 - BS, value.shape[1]), value.dtype)
    return jnp.concatenate([value[:BS], gap, value[BS:], gap], axis=0)


def rest_kernel(
    spec_ref, outer_ref, two_ref, slope_ref, w2, w1, twiddle_ref, back_ref,
    out_ref, plane_hbm,
    t1_ref, s1_ref, t2_ref, s2_ref, part_ref, plane_ref, sends,
):
    lanes = ((1,), (1,))
    g = pl.program_id(0)

    @pl.when(g == 0)
    def _():
        for ref in (t1_ref, s1_ref, t2_ref, s2_ref):
            ref[...] = jnp.zeros(ref.shape, f32)

    grad_two = two_ref[0]
    two = spread(grad_two)
    t2_ref[...] += dot3(split(outer_ref[0]), split(two), lanes)
    s2_ref[...] += two
    grad_one = product(w2, grad_two) * slope_ref[0]
    one = spread(grad_one)
    t1_ref[...] += dot3(split(spec_ref[0]), split(one), lanes)
    s1_ref[...] += one
    store_group(part_ref, g, product(w1, grad_one), back_ref)

    def send(p):
        span = pl.ds(p * 8, 8)
        rows = pl.ds(0, 2 * SECOND)
        return pltpu.make_async_copy(plane_ref.at[span], plane_hbm.at[span, rows], sends.at[p])

    @pl.when(g == GROUPS - 1)
    def _():
        plane_backward(part_ref, plane_ref, twiddle_ref, lambda p: send(p).start())
        norm = 1.0 / math.sqrt(4 * NX * NY * KZ)
        ones = jnp.ones((8, WIDE), bf16)
        row = lax.broadcasted_iota(jnp.int32, (8, 128), 0)
        out_ref[4 * BS :] = jnp.zeros((ROWS - 4 * BS, 128), f32)
        biases = jnp.zeros((8, 128), f32)
        for n, (table_ref, total_ref) in enumerate(((t1_ref, s1_ref), (t2_ref, s2_ref))):
            table = table_ref[...]
            real = table[:BS, :128] + table[BS:, 128:]
            imag = table[:BS, 128:] - table[BS:, :128]
            out_ref[2 * n * BS : (2 * n + 1) * BS] = real * norm
            out_ref[(2 * n + 1) * BS : (2 * n + 2) * BS] = imag * norm
            high, low = split(total_ref[...])
            sums = dot(ones, high, lanes) + dot(ones, low, lanes)
            for q in range(2):
                biases = jnp.where(row == 2 * n + q, sums[:, q * 128 : (q + 1) * 128], biases)
        out_ref[4 * BS : 4 * BS + 8] = biases * norm
        for p in range(8):
            send(p).wait()


def field_kernel(
    first_hbm, second_hbm, cotangent_hbm, table_hbm, out_hbm,
    first_ref, second_ref, cotangent_ref, table_ref, out_ref, work_ref,
    first_sems, second_sems, sems, out_sems,
):
    loads = []
    for k in range(KZ):
        span = pl.ds(0, 2 * SECOND)
        loads.append(
            (
                pltpu.make_async_copy(first_hbm.at[:, k], first_ref.at[:, k], first_sems.at[k]),
                pltpu.make_async_copy(
                    second_hbm.at[:, k, span], second_ref.at[:, k], second_sems.at[k]
                ),
            )
        )
    pairs = ((table_hbm, table_ref), (cotangent_hbm, cotangent_ref))
    others = [pltpu.make_async_copy(a, b, sems.at[n]) for n, (a, b) in enumerate(pairs)]
    for load in loads:
        load[0].start()
        load[1].start()
    for load in others:
        load.start()
    for k in range(KZ):
        loads[k][0].wait()
        loads[k][1].wait()
        parts = []
        for b in range(NB):
            left = swap(first_ref[b, k, :FIRST], first_ref[b, k, FIRST:])
            right = swap(second_ref[b, k, :SECOND], second_ref[b, k, SECOND:])
            parts.extend([left[0], right[0], left[1], right[1]])
        values = jnp.concatenate(parts, axis=0).T
        work_ref[2 * k : 2 * k + 2] = values.reshape(2, CELLS, C)
    for load in others:
        load.wait()
    sends = []
    for g in range(8):
        values = product(table_ref, work_ref[:, g * 8 : (g + 1) * 8, :].reshape(256, C))
        span = slice(g * 256, (g + 1) * 256)
        out_ref[span, :] = (cotangent_ref[span, :].astype(f32) + values).astype(bf16)
        rows = pl.ds(g * 256, 256)
        sends.append(pltpu.make_async_copy(out_ref.at[rows], out_hbm.at[rows], out_sems.at[g]))
        sends[-1].start()
    for send in sends:
        send.wait()


def gather_kernel(core_ref, low_ref, *refs):
    sources, (one_ref, bias_one_ref, two_ref, bias_two_ref, all_ref) = refs[:4], refs[4:]
    core = core_ref[0, 0]
    low = low_ref[0, 0]
    for n, source in enumerate(sources):
        place = (core + n // 2) % 2 * 2 + (low + n % 2) % 2
        start = pl.multiple_of(place * (ROWS // 4), ROWS // 4)
        all_ref[:, pl.ds(start, ROWS // 4), :] = source[...].reshape(NB, ROWS // 4, 128)
    for b in range(NB):
        for q in range(2):
            one_ref[q, b] = all_ref[b, q * BS : (q + 1) * BS, :BS]
            two_ref[q, b] = all_ref[b, (2 + q) * BS : (3 + q) * BS, :BS]
            bias_one_ref[q, b : b + 1] = all_ref[b, 4 * BS + q : 4 * BS + q + 1, :BS]
            bias_two_ref[q, b : b + 1] = all_ref[b, 4 * BS + 2 + q : 4 * BS + 3 + q, :BS]


def gathered(sources):
    dp = lax.axis_index("dp")
    bits = [(dp % 2).reshape(1, 1).astype(jnp.int32), (dp // 2).reshape(1, 1).astype(jnp.int32)]
    weight = jax.ShapeDtypeStruct((2, NB, BS, BS), f32)
    bias = jax.ShapeDtypeStruct((2, NB, BS), f32)
    return pl.pallas_call(
        gather_kernel,
        out_shape=(weight, bias, weight, bias),
        in_specs=[pl.BlockSpec(memory_space=pltpu.SMEM)] * 2 + vmem(4),
        out_specs=tuple(vmem(4)),
        scratch_shapes=[pltpu.VMEM((NB, ROWS, 128), f32)],
        compiler_params=pltpu.CompilerParams(vmem_limit_bytes=16 * 1024 * 1024),
        cost_estimate=pl.CostEstimate(flops=0, bytes_accessed=2_000_000, transcendentals=0),
    )(*bits, *sources)


def vmem(n):
    return [pl.BlockSpec(memory_space=pltpu.VMEM)] * n


def free(n):
    return [pl.BlockSpec(memory_space=pl.ANY)] * n


def held(*values):
    return [pltpu.VMEM(v.shape, v.dtype) for v in values]


def sems(*counts):
    return [pltpu.SemaphoreType.DMA((n,)) for n in counts]


def call(kernel, out_shape, args, scratch, flops, moved, place=vmem):
    outs = len(out_shape) if isinstance(out_shape, tuple) else 1
    return pl.pallas_call(
        kernel,
        out_shape=out_shape,
        in_specs=place(len(args)),
        out_specs=tuple(place(outs)) if isinstance(out_shape, tuple) else place(1)[0],
        scratch_shapes=scratch,
        compiler_params=BIG,
        cost_estimate=pl.CostEstimate(flops=flops, bytes_accessed=moved, transcendentals=0),
    )(*args)


def depth_forward(field, tables):
    args = (field.reshape(2048, C), tables)
    out = jax.ShapeDtypeStruct((NB, KZ, 2 * HALF, 128), f32)
    scratch = [*held(*args, out), pltpu.VMEM((2 * KZ, CELLS, C), f32), *sems(9, KZ)]
    return call(depth_kernel, out, args, scratch, 800_000_000, 5_000_000, free).reshape(SPECTRAL)


def backward(cot_spec, twiddle, plane_fwd, plane_bwd, first, second, slope, square):
    args = (cot_spec, twiddle, plane_fwd, plane_bwd, first, second, slope, square)
    outs = (GROUPED, jax.ShapeDtypeStruct((64, 2 * FIRST, 128), f32))
    scratch = [
        *held(*args, *outs),
        pltpu.VMEM(SPECTRAL, f32),
        pltpu.VMEM((64, 2 * FIRST, 128), f32),
        *sems(8, 5, *[GROUPS] * 3, 8),
    ]
    return call(backward_kernel, outs, args, scratch, 10_000_000_000, 20_000_000, free)


def by_group(n):
    return [pl.BlockSpec((1, 2 * BS, WIDE), lambda g: (g, 0, 0))] * n


def rest(spec, outer, grad_two, slope, second, first, twiddle, plane_bwd):
    return pl.pallas_call(
        rest_kernel,
        grid=(GROUPS,),
        out_shape=(
            jax.ShapeDtypeStruct((ROWS, 128), f32),
            jax.ShapeDtypeStruct((64, 2 * SECOND + 8, 128), f32),
        ),
        in_specs=by_group(4) + vmem(4),
        out_specs=(pl.BlockSpec((ROWS, 128), lambda g: (0, 0)), *free(1)),
        scratch_shapes=[
            *[pltpu.VMEM((2 * BS, 256), f32), pltpu.VMEM((256, WIDE), f32)] * 2,
            *[pltpu.VMEM((64, 2 * SECOND, 128), f32)] * 2,
            *sems(8),
        ],
        compiler_params=BIG,
        cost_estimate=pl.CostEstimate(
            flops=8_000_000_000, bytes_accessed=16_000_000, transcendentals=0
        ),
    )(spec, outer, grad_two, slope, second, first, twiddle, plane_bwd)


def field(first, second, cotangent, tables):
    args = (
        first.reshape(NB, KZ, 2 * FIRST, 128),
        second.reshape(NB, KZ, 2 * SECOND + 8, 128),
        cotangent.reshape(2048, C),
        tables,
    )
    out = jax.ShapeDtypeStruct((2048, C), bf16)
    scratch = [
        *held(args[0], jax.ShapeDtypeStruct((NB, KZ, 2 * SECOND, 128), f32), *args[2:], out),
        pltpu.VMEM((2 * KZ, CELLS, C), f32),
        *sems(KZ, KZ, 2, 8),
    ]
    return call(field_kernel, out, args, scratch, 1_200_000_000, 7_000_000, free)


def rows_of(weight, start, stop):
    return weight.reshape(4, HALF, 2 * BS)[:, start:stop].reshape(-1, 2 * BS)


def mixing(weight):
    real = weight[0].T
    imag = weight[1].T
    return jnp.concatenate(
        [jnp.concatenate([real, -imag], axis=1), jnp.concatenate([imag, real], axis=1)], axis=0
    )


def stacked(value):
    high = lax.reduce_precision(value, 8, 7)
    return thrice((high.astype(bf16), (value - high).astype(bf16)), 1)


def keep_half(value, axis, flip, bit):
    half = value.shape[0] // 2
    size = lax.axis_size(axis)
    mine = lax.dynamic_slice_in_dim(value, bit * half, half, 0)
    other = lax.dynamic_slice_in_dim(value, (1 - bit) * half, half, 0)
    return mine + lax.ppermute(other, axis, [(n, n ^ flip) for n in range(size)])


def owned_rows(rows):
    dp = lax.axis_index("dp")
    px = lax.axis_index("px")
    py = lax.axis_index("py")
    rows = keep_half(rows, "dp", 1, dp % 2)
    rows = keep_half(rows, "dp", 2, dp // 2)
    rows = keep_half(rows, "px", 1, px % 2)
    pieces = rows.reshape(8, -1, 128)
    total = lax.dynamic_index_in_dim(pieces, py, 0, keepdims=False)
    for offset in range(1, 8):
        piece = lax.dynamic_index_in_dim(pieces, (py + offset) % 8, 0, keepdims=False)
        total = total + lax.ppermute(piece, "py", [(n, (n + offset) % 8) for n in range(8)])
    return total


def partner(value, flip):
    return lax.ppermute(value, "dp", [(n, n ^ flip) for n in range(4)])


def exchange(value):
    return lax.all_to_all(value, ("px", "py"), split_axis=0, concat_axis=0, tiled=True)


def shards(state_field, cotangent, first_weight, first_bias, second_weight, second_bias):
    depth_fwd, depth_bwd = depth_tables()
    plane_fwd, plane_bwd = plane_tables()
    twiddle = twiddle_table()
    owner = lax.axis_index("px") * 8 + lax.axis_index("py")
    block = owner // KZ
    doubling = jnp.where(owner % KZ == 0, 1.0, 2.0).astype(f32).reshape(1, 1)

    first = mixing(lax.dynamic_index_in_dim(first_weight, block, 1, keepdims=False))
    second = mixing(lax.dynamic_index_in_dim(second_weight, block, 1, keepdims=False))
    bias_one = lax.dynamic_index_in_dim(first_bias, block, 1, keepdims=False).reshape(2 * BS, 1)
    bias_two = lax.dynamic_index_in_dim(second_bias, block, 1, keepdims=False).reshape(2 * BS, 1)

    state_spec = exchange(depth_forward(state_field, depth_fwd))
    cot_spec = exchange(depth_forward(cotangent, depth_fwd))
    spec, outer, slope, square = pl.pallas_call(
        forward_kernel,
        out_shape=(GROUPED,) * 4,
        in_specs=[pl.BlockSpec(memory_space=pltpu.SMEM)] + vmem(7),
        out_specs=tuple(vmem(4)),
        scratch_shapes=[pltpu.VMEM(SPECTRAL, f32)],
        compiler_params=BIG,
        cost_estimate=pl.CostEstimate(
            flops=8_000_000_000, bytes_accessed=16_000_000, transcendentals=1_500_000
        ),
    )(doubling, state_spec, twiddle, plane_fwd, stacked(first), bias_one, stacked(second), bias_two)

    second_back = stacked(second.T)
    grad_two, plane = backward(
        cot_spec,
        twiddle,
        plane_fwd,
        plane_bwd,
        stacked(rows_of(first.T, 0, FIRST)),
        second_back,
        slope,
        square,
    )
    first_part = exchange(plane)
    rows, plane = rest(
        spec, outer, grad_two, slope, second_back, stacked(rows_of(first.T, FIRST, HALF)), twiddle, plane_bwd
    )
    rows = owned_rows(rows)
    plane = lax.dynamic_update_slice(
        plane, jnp.broadcast_to(rows[None], (64, *rows.shape)), (0, 2 * SECOND, 0)
    )
    first_part, plane = lax.optimization_barrier((first_part, plane))
    second_part = exchange(plane)
    mine = second_part[:, 2 * SECOND :]
    across = partner(mine, 1)
    beside = partner(mine, 2)
    state_grad = field(first_part, second_part, cotangent, depth_bwd).reshape(1, 8, 8, NZ, C)
    state_grad, across, beside = lax.optimization_barrier((state_grad, across, beside))
    sums = gathered((mine, beside, across, partner(beside, 1)))
    return (state_grad, *sums)


def solution(mesh):
    in_specs = (
        P("dp", "px", "py", None, None),
        P("dp", "px", "py", None, None),
        P(),
        P(),
        P(),
        P(),
    )
    out_specs = (P("dp", "px", "py", None, None), P(), P(), P(), P())
    return jax.shard_map(shards, mesh=mesh, in_specs=in_specs, out_specs=out_specs, check_vma=False)
```

```python
import math

import jax
import jax.numpy as jnp
import ml_dtypes
import numpy as np
from jax import lax
from jax.experimental import pallas as pl
from jax.experimental.pallas import tpu as pltpu
from jax.sharding import PartitionSpec as P

NX = 64
NY = 64
NZ = 32
NB = 4
BS = 96
KZ = 16
C = 384
HALF = BS // 2
FIRST = 40
BATCH = 4
SECOND = HALF - FIRST
CELLS = 64
STEP = 8
GROUPS = 64 // STEP
WIDE = STEP * 64
ROWS = 512
SHRINK = 0.25
f32 = jnp.float32
bf16 = jnp.bfloat16
BIG = pltpu.CompilerParams(vmem_limit_bytes=62 * 1024 * 1024)
SPECTRAL = (64, 2 * HALF, 128)
GROUPED = jax.ShapeDtypeStruct((GROUPS, 2 * BS, WIDE), f32)


def np_split(table):
    high = table.astype(np.float32).astype(ml_dtypes.bfloat16)
    low = (table - high.astype(np.float64)).astype(np.float32).astype(ml_dtypes.bfloat16)
    return high, low


def depth_tables():
    k = np.arange(KZ)[:, None]
    z = np.arange(NZ)[None, :]
    angle = 2.0 * np.pi * (k * z % NZ) / NZ
    scale = 1.0 / math.sqrt(NX * NY * NZ)
    pair = np.stack([np.cos(angle), -np.sin(angle)], axis=1) * scale
    eye = np.eye(8)
    forward = np.einsum("kqz,ab->kqabz", pair, eye).reshape(256, 256)
    scheme = ((0, 1), (0, 1, 0))
    return [
        np.concatenate([np_split(table)[n] for n in order], axis=1)
        for table, order in zip((forward, forward.T.copy()), scheme)
    ]


def plane_tables():
    j = np.arange(8)
    eight = np.exp(-2j * np.pi * np.outer(j, j) / 8.0)
    both = np.einsum("xk,yl->xykl", eight, eight).reshape(64, 64)
    real = np.zeros((2, 64, 2, 64))
    real[0, :, 0] = both.real
    real[0, :, 1] = both.imag
    real[1, :, 0] = -both.imag
    real[1, :, 1] = both.real
    forward = np.einsum("qxpf,cd->qcxpdf", real, np.eye(2)).reshape(256, 256)
    tables = np_split(forward), np_split(forward.T.copy())
    return [np.concatenate([high, high, low], axis=0) for high, low in tables]


def twiddle_table():
    k2 = np.arange(8)
    j = np.arange(8)
    one = np.exp(-2j * np.pi * np.outer(k2, j) / 64.0)
    both = np.einsum("kx,ly->klxy", one, one).reshape(64, 64)
    both = np.tile(both, (1, 2))
    return np.stack([both.real, both.imag], axis=1).astype(np.float32)


def split(value):
    high = value.astype(bf16)
    low = (value - high.astype(f32)).astype(bf16)
    return high, low


def dot(left, right, dims=((1,), (0,))):
    return lax.dot_general(left, right, (dims, ((), ())), preferred_element_type=f32)


def thrice(pair, axis):
    high, low = pair
    return jnp.concatenate([high, low, high], axis=axis)


def paired(pair, axis):
    high, low = pair
    return jnp.concatenate([high, high, low], axis=axis)


def dot3(left, right, dims=((1,), (0,))):
    return dot(thrice(left, 1), paired(right, dims[1][0]), dims)


def product(weight_ref, value):
    return dot(weight_ref[...], paired(split(value), 0))


def swap(upper, lower):
    lane = lax.broadcasted_iota(jnp.int32, upper.shape, 1)
    first = jnp.where(lane < 64, upper, pltpu.roll(lower, 64, 1))
    second = jnp.where(lane < 64, pltpu.roll(upper, 64, 1), lower)
    return first, second


def fft(re, im, sign):
    n = len(re)
    if n == 1:
        return re, im
    even_re, even_im = fft(re[0::2], im[0::2], sign)
    odd_re, odd_im = fft(re[1::2], im[1::2], sign)
    out_re = [None] * n
    out_im = [None] * n
    root = math.sqrt(0.5)
    for k in range(n // 2):
        a, b = odd_re[k], odd_im[k]
        turn = k * (8 // n)
        if turn == 1:
            a, b = (a - sign * b) * root, (b + sign * a) * root
        elif turn == 2:
            a, b = -sign * b, sign * a
        elif turn == 3:
            a, b = (-a - sign * b) * root, (-b + sign * a) * root
        out_re[k], out_im[k] = even_re[k] + a, even_im[k] + b
        out_re[k + n // 2], out_im[k + n // 2] = even_re[k] - a, even_im[k] - b
    return out_re, out_im


def read(ref, index, tile):
    half = ref.shape[1] // 2
    rows = slice(tile * 8, tile * 8 + 8), slice(half + tile * 8, half + tile * 8 + 8)
    return ref[index, rows[0], :], ref[index, rows[1], :]


def write(ref, index, tile, re, im):
    half = ref.shape[1] // 2
    ref[index, tile * 8 : tile * 8 + 8, :] = re
    ref[index, half + tile * 8 : half + tile * 8 + 8, :] = im


def senders(src_ref, dst_ref, sign, before, after):
    def body(p, carry):
        before(p)
        for tile in range(src_ref.shape[1] // 16):
            re, im = zip(*[read(src_ref, p * 8 + n, tile) for n in range(8)])
            re, im = fft(re, im, sign)
            for n in range(8):
                write(dst_ref, p * 8 + n, tile, re[n], im[n])
        after(p)
        return carry

    lax.fori_loop(0, 8, body, 0)


def turned(a, b, twiddle_ref, index, sign):
    c = twiddle_ref[index, 0:1, :]
    s = twiddle_ref[index, 1:2, :] * sign
    return a * c - b * s, a * s + b * c


def plane_forward(src_ref, work_ref, twiddle_ref, before):
    senders(src_ref, work_ref, -1.0, before, lambda p: None)

    def body(p, carry):
        for tile in range(HALF // 8):
            re, im = zip(*[read(work_ref, n * 8 + p, tile) for n in range(8)])
            re, im = fft(re, im, -1.0)
            for n in range(8):
                write(work_ref, n * 8 + p, tile, *turned(re[n], im[n], twiddle_ref, n * 8 + p, 1.0))
        return carry

    lax.fori_loop(0, 8, body, 0)


def plane_backward(work_ref, out_ref, twiddle_ref, after):
    def body(p, carry):
        for tile in range(work_ref.shape[1] // 16):
            pairs = [
                turned(*read(work_ref, n * 8 + p, tile), twiddle_ref, n * 8 + p, -1.0)
                for n in range(8)
            ]
            re, im = fft(*zip(*pairs), 1.0)
            for n in range(8):
                write(work_ref, n * 8 + p, tile, re[n], im[n])
        return carry

    lax.fori_loop(0, 8, body, 0)
    senders(work_ref, out_ref, 1.0, lambda p: None, after)


def load_group(work_ref, group, table_ref):
    rows = [
        jnp.concatenate(
            [work_ref[group * STEP + n, :HALF], work_ref[group * STEP + n, HALF:]], axis=1
        )
        for n in range(STEP)
    ]
    values = dot(thrice(split(jnp.concatenate(rows, axis=0)), 1), table_ref[...])
    pairs = []
    for pair in range(STEP // 2):
        part = []
        for q in range(2):
            lanes = slice(q * 128, (q + 1) * 128)
            upper = values[2 * pair * HALF : (2 * pair + 1) * HALF, lanes]
            lower = values[(2 * pair + 1) * HALF : (2 * pair + 2) * HALF, lanes]
            part.extend(swap(upper, lower))
        pairs.append(jnp.concatenate(part, axis=0))
    return jnp.concatenate(pairs, axis=1)


def store_group(work_ref, group, spectral, table_ref):
    count = spectral.shape[0] // 4
    rows = []
    for pair in range(STEP // 2):
        part = spectral[:, pair * 128 : (pair + 1) * 128]
        parts = [
            swap(
                part[2 * q * count : (2 * q + 1) * count],
                part[(2 * q + 1) * count : (2 * q + 2) * count],
            )
            for q in range(2)
        ]
        for n in range(2):
            rows.append(jnp.concatenate([parts[0][n], parts[1][n]], axis=1))
    values = dot(thrice(split(jnp.concatenate(rows, axis=0)), 1), table_ref[...])
    for n in range(STEP):
        for q in range(2):
            work_ref[group * STEP + n, q * count : (q + 1) * count] = values[
                n * count : (n + 1) * count, q * 128 : (q + 1) * 128
            ]


def depth_kernel(field_hbm, both_hbm, out_hbm, field_ref, both_ref, out_ref, work_ref, sems, out_sems):
    table = pltpu.make_async_copy(both_hbm, both_ref, sems.at[8])
    table.start()
    copies = []
    for g in range(8):
        span = pl.ds(g * 256, 256)
        copies.append(pltpu.make_async_copy(field_hbm.at[span], field_ref.at[span], sems.at[g]))
        copies[-1].start()
    table.wait()
    for g in range(8):
        if g % BATCH == 0:
            for copy in copies[g : g + BATCH]:
                copy.wait()
        rows = field_ref[g * 256 : (g + 1) * 256, :]
        values = dot(both_ref[...], jnp.concatenate([rows, rows], axis=0))
        work_ref[:, g * 8 : (g + 1) * 8, :] = values.reshape(2 * KZ, 8, C)
    sends = []
    for k in range(KZ):
        values = work_ref[2 * k : 2 * k + 2].reshape(2 * CELLS, C).T
        for b in range(NB):
            upper = values[b * BS : b * BS + HALF]
            lower = values[b * BS + HALF : (b + 1) * BS]
            out_ref[b, k, :HALF], out_ref[b, k, HALF:] = swap(upper, lower)
        sends.append(pltpu.make_async_copy(out_ref.at[:, k], out_hbm.at[:, k], out_sems.at[k]))
        if k % BATCH == BATCH - 1:
            for send in sends[-BATCH:]:
                send.start()
    for send in sends:
        send.wait()


def forward_kernel(
    doubling_ref, src_ref, twiddle_ref, t_ref, w1, b1, w2, b2,
    spec_ref, outer_ref, slope_ref, square_ref, work_ref,
):
    plane_forward(src_ref, work_ref, twiddle_ref, lambda p: None)
    root = math.sqrt(2.0 / math.pi)

    def body(g, carry):
        spectral = load_group(work_ref, g, t_ref)
        spec_ref[g] = spectral
        pre = product(w1, spectral) + b1[...]
        pre_sq = pre * pre
        t = jnp.tanh(root * (pre + 0.044715 * (pre * pre_sq)))
        outer = 0.5 * pre * (1.0 + t)
        outer_ref[g] = outer
        slope_ref[g] = 0.5 * (1.0 + t) + 0.5 * pre * (1.0 - t * t) * (
            root * (1.0 + 3.0 * 0.044715 * pre_sq)
        )
        pre_two = product(w2, outer) + b2[...]
        t2 = jnp.tanh(pre_two * (1.0 / SHRINK))
        square_ref[g] = t2 * t2 * doubling_ref[0, 0]
        return carry

    lax.fori_loop(0, GROUPS, body, 0)


def block_of(hbm, ref, sems, p):
    span = pl.ds(p * 8, 8)
    return pltpu.make_async_copy(hbm.at[span], ref.at[span], sems.at[p])


def backward_kernel(
    src_hbm, twiddle_hbm, t_hbm, back_hbm, w1_hbm, w2_hbm, slope_hbm, square_hbm,
    two_hbm, out_hbm,
    src_ref, twiddle_ref, t_ref, back_ref, w1, w2, slope_ref, square_ref,
    two_ref, out_ref, work_ref, part_ref, src_sems, sems, square_sems, slope_sems,
    two_sems, out_sems,
):
    for p in range(8):
        block_of(src_hbm, src_ref, src_sems, p).start()
    pairs = (
        (twiddle_hbm, twiddle_ref), (t_hbm, t_ref), (w2_hbm, w2),
        (w1_hbm, w1), (back_hbm, back_ref),
    )
    loads = [pltpu.make_async_copy(a, b, sems.at[n]) for n, (a, b) in enumerate(pairs)]
    for load in loads:
        load.start()
    loads[0].wait()

    def before(p):
        block_of(src_hbm, src_ref, src_sems, p).wait()
        pltpu.make_async_copy(square_hbm.at[p], square_ref.at[p], square_sems.at[p]).start()
        pltpu.make_async_copy(slope_hbm.at[p], slope_ref.at[p], slope_sems.at[p]).start()

    plane_forward(src_ref, work_ref, twiddle_ref, before)
    for load in loads[1:]:
        load.wait()

    sends = []
    spectral = load_group(work_ref, 0, t_ref)
    for g in range(GROUPS):
        following = load_group(work_ref, g + 1, t_ref) if g + 1 < GROUPS else None
        for n in range(g, g + BATCH) if g % BATCH == 0 else ():
            pltpu.make_async_copy(square_hbm.at[n], square_ref.at[n], square_sems.at[n]).wait()
            pltpu.make_async_copy(slope_hbm.at[n], slope_ref.at[n], slope_sems.at[n]).wait()
        grad_two = spectral * square_ref[g]
        two_ref[g] = grad_two
        sends.append(pltpu.make_async_copy(two_ref.at[g], two_hbm.at[g], two_sems.at[g]))
        if g % BATCH == BATCH - 1:
            for send in sends[-BATCH:]:
                send.start()
        grad_one = product(w2, grad_two) * slope_ref[g]
        store_group(part_ref, g, product(w1, grad_one), back_ref)
        spectral = following
    plane_backward(
        part_ref, out_ref, twiddle_ref, lambda p: block_of(out_ref, out_hbm, out_sems, p).start()
    )
    for send in sends:
        send.wait()
    for p in range(8):
        block_of(out_ref, out_hbm, out_sems, p).wait()


def spread(value):
    gap = jnp.zeros((128 - BS, value.shape[1]), value.dtype)
    return jnp.concatenate([value[:BS], gap, value[BS:], gap], axis=0)


def rest_kernel(
    spec_ref, outer_ref, two_ref, slope_ref, w2, w1, twiddle_ref, back_ref,
    out_ref, plane_hbm,
    t1_ref, s1_ref, t2_ref, s2_ref, part_ref, plane_ref, sends,
):
    lanes = ((1,), (1,))
    g = pl.program_id(0)

    @pl.when(g == 0)
    def _():
        for ref in (t1_ref, s1_ref, t2_ref, s2_ref):
            ref[...] = jnp.zeros(ref.shape, f32)

    grad_two = two_ref[0]
    two = spread(grad_two)
    t2_ref[...] += dot3(split(outer_ref[0]), split(two), lanes)
    s2_ref[...] += two
    grad_one = product(w2, grad_two) * slope_ref[0]
    one = spread(grad_one)
    t1_ref[...] += dot3(split(spec_ref[0]), split(one), lanes)
    s1_ref[...] += one
    store_group(part_ref, g, product(w1, grad_one), back_ref)

    def send(p):
        span = pl.ds(p * 8, 8)
        rows = pl.ds(0, 2 * SECOND)
        return pltpu.make_async_copy(plane_ref.at[span], plane_hbm.at[span, rows], sends.at[p])

    @pl.when(g == GROUPS - 1)
    def _():
        plane_backward(part_ref, plane_ref, twiddle_ref, lambda p: send(p).start())
        norm = 1.0 / math.sqrt(4 * NX * NY * KZ)
        ones = jnp.ones((8, WIDE), bf16)
        row = lax.broadcasted_iota(jnp.int32, (8, 128), 0)
        out_ref[4 * BS :] = jnp.zeros((ROWS - 4 * BS, 128), f32)
        biases = jnp.zeros((8, 128), f32)
        for n, (table_ref, total_ref) in enumerate(((t1_ref, s1_ref), (t2_ref, s2_ref))):
            table = table_ref[...]
            real = table[:BS, :128] + table[BS:, 128:]
            imag = table[:BS, 128:] - table[BS:, :128]
            out_ref[2 * n * BS : (2 * n + 1) * BS] = real * norm
            out_ref[(2 * n + 1) * BS : (2 * n + 2) * BS] = imag * norm
            high, low = split(total_ref[...])
            sums = dot(ones, high, lanes) + dot(ones, low, lanes)
            for q in range(2):
                biases = jnp.where(row == 2 * n + q, sums[:, q * 128 : (q + 1) * 128], biases)
        out_ref[4 * BS : 4 * BS + 8] = biases * norm
        for p in range(8):
            send(p).wait()


def field_kernel(
    first_hbm, second_hbm, cotangent_hbm, table_hbm, out_hbm,
    first_ref, second_ref, cotangent_ref, table_ref, out_ref, work_ref,
    first_sems, second_sems, sems, out_sems,
):
    loads = []
    for k in range(KZ):
        span = pl.ds(0, 2 * SECOND)
        loads.append(
            (
                pltpu.make_async_copy(first_hbm.at[:, k], first_ref.at[:, k], first_sems.at[k]),
                pltpu.make_async_copy(
                    second_hbm.at[:, k, span], second_ref.at[:, k], second_sems.at[k]
                ),
            )
        )
    pairs = ((table_hbm, table_ref), (cotangent_hbm, cotangent_ref))
    others = [pltpu.make_async_copy(a, b, sems.at[n]) for n, (a, b) in enumerate(pairs)]
    for load in loads:
        load[0].start()
        load[1].start()
    for load in others:
        load.start()
    for k in range(KZ):
        for load in loads[k : k + BATCH] if k % BATCH == 0 else ():
            load[0].wait()
            load[1].wait()
        parts = []
        for b in range(NB):
            left = swap(first_ref[b, k, :FIRST], first_ref[b, k, FIRST:])
            right = swap(second_ref[b, k, :SECOND], second_ref[b, k, SECOND:])
            parts.extend([left[0], right[0], left[1], right[1]])
        values = jnp.concatenate(parts, axis=0).T
        work_ref[2 * k : 2 * k + 2] = values.reshape(2, CELLS, C)
    for load in others:
        load.wait()
    sends = []
    for g in range(8):
        values = product(table_ref, work_ref[:, g * 8 : (g + 1) * 8, :].reshape(256, C))
        span = slice(g * 256, (g + 1) * 256)
        out_ref[span, :] = (cotangent_ref[span, :].astype(f32) + values).astype(bf16)
        rows = pl.ds(g * 256, 256)
        sends.append(pltpu.make_async_copy(out_ref.at[rows], out_hbm.at[rows], out_sems.at[g]))
        if g % BATCH == BATCH - 1:
            for send in sends[-BATCH:]:
                send.start()
    for send in sends:
        send.wait()


def gather_kernel(core_ref, low_ref, *refs):
    sources, (one_ref, bias_one_ref, two_ref, bias_two_ref, all_ref) = refs[:4], refs[4:]
    core = core_ref[0, 0]
    low = low_ref[0, 0]
    for n, source in enumerate(sources):
        place = (core + n // 2) % 2 * 2 + (low + n % 2) % 2
        start = pl.multiple_of(place * (ROWS // 4), ROWS // 4)
        all_ref[:, pl.ds(start, ROWS // 4), :] = source[...].reshape(NB, ROWS // 4, 128)
    for b in range(NB):
        for q in range(2):
            one_ref[q, b] = all_ref[b, q * BS : (q + 1) * BS, :BS]
            two_ref[q, b] = all_ref[b, (2 + q) * BS : (3 + q) * BS, :BS]
            bias_one_ref[q, b : b + 1] = all_ref[b, 4 * BS + q : 4 * BS + q + 1, :BS]
            bias_two_ref[q, b : b + 1] = all_ref[b, 4 * BS + 2 + q : 4 * BS + 3 + q, :BS]


def gathered(sources):
    dp = lax.axis_index("dp")
    bits = [(dp % 2).reshape(1, 1).astype(jnp.int32), (dp // 2).reshape(1, 1).astype(jnp.int32)]
    weight = jax.ShapeDtypeStruct((2, NB, BS, BS), f32)
    bias = jax.ShapeDtypeStruct((2, NB, BS), f32)
    return pl.pallas_call(
        gather_kernel,
        out_shape=(weight, bias, weight, bias),
        in_specs=[pl.BlockSpec(memory_space=pltpu.SMEM)] * 2 + vmem(4),
        out_specs=tuple(vmem(4)),
        scratch_shapes=[pltpu.VMEM((NB, ROWS, 128), f32)],
        compiler_params=pltpu.CompilerParams(vmem_limit_bytes=16 * 1024 * 1024),
        cost_estimate=pl.CostEstimate(flops=0, bytes_accessed=2_000_000, transcendentals=0),
    )(*bits, *sources)


def vmem(n):
    return [pl.BlockSpec(memory_space=pltpu.VMEM)] * n


def free(n):
    return [pl.BlockSpec(memory_space=pl.ANY)] * n


def held(*values):
    return [pltpu.VMEM(v.shape, v.dtype) for v in values]


def sems(*counts):
    return [pltpu.SemaphoreType.DMA((n,)) for n in counts]


def call(kernel, out_shape, args, scratch, flops, moved, place=vmem):
    outs = len(out_shape) if isinstance(out_shape, tuple) else 1
    return pl.pallas_call(
        kernel,
        out_shape=out_shape,
        in_specs=place(len(args)),
        out_specs=tuple(place(outs)) if isinstance(out_shape, tuple) else place(1)[0],
        scratch_shapes=scratch,
        compiler_params=BIG,
        cost_estimate=pl.CostEstimate(flops=flops, bytes_accessed=moved, transcendentals=0),
    )(*args)


def depth_forward(field, tables):
    args = (field.reshape(2048, C), tables)
    out = jax.ShapeDtypeStruct((NB, KZ, 2 * HALF, 128), f32)
    scratch = [*held(*args, out), pltpu.VMEM((2 * KZ, CELLS, C), f32), *sems(9, KZ)]
    return call(depth_kernel, out, args, scratch, 800_000_000, 5_000_000, free).reshape(SPECTRAL)


def backward(cot_spec, twiddle, plane_fwd, plane_bwd, first, second, slope, square):
    args = (cot_spec, twiddle, plane_fwd, plane_bwd, first, second, slope, square)
    outs = (GROUPED, jax.ShapeDtypeStruct((64, 2 * FIRST, 128), f32))
    scratch = [
        *held(*args, *outs),
        pltpu.VMEM(SPECTRAL, f32),
        pltpu.VMEM((64, 2 * FIRST, 128), f32),
        *sems(8, 5, *[GROUPS] * 3, 8),
    ]
    return call(backward_kernel, outs, args, scratch, 10_000_000_000, 20_000_000, free)


def by_group(n):
    return [pl.BlockSpec((1, 2 * BS, WIDE), lambda g: (g, 0, 0))] * n


def rest(spec, outer, grad_two, slope, second, first, twiddle, plane_bwd):
    return pl.pallas_call(
        rest_kernel,
        grid=(GROUPS,),
        out_shape=(
            jax.ShapeDtypeStruct((ROWS, 128), f32),
            jax.ShapeDtypeStruct((64, 2 * SECOND + 8, 128), f32),
        ),
        in_specs=by_group(4) + vmem(4),
        out_specs=(pl.BlockSpec((ROWS, 128), lambda g: (0, 0)), *free(1)),
        scratch_shapes=[
            *[pltpu.VMEM((2 * BS, 256), f32), pltpu.VMEM((256, WIDE), f32)] * 2,
            *[pltpu.VMEM((64, 2 * SECOND, 128), f32)] * 2,
            *sems(8),
        ],
        compiler_params=BIG,
        cost_estimate=pl.CostEstimate(
            flops=8_000_000_000, bytes_accessed=16_000_000, transcendentals=0
        ),
    )(spec, outer, grad_two, slope, second, first, twiddle, plane_bwd)


def field(first, second, cotangent, tables):
    args = (
        first.reshape(NB, KZ, 2 * FIRST, 128),
        second.reshape(NB, KZ, 2 * SECOND + 8, 128),
        cotangent.reshape(2048, C),
        tables,
    )
    out = jax.ShapeDtypeStruct((2048, C), bf16)
    scratch = [
        *held(args[0], jax.ShapeDtypeStruct((NB, KZ, 2 * SECOND, 128), f32), *args[2:], out),
        pltpu.VMEM((2 * KZ, CELLS, C), f32),
        *sems(KZ, KZ, 2, 8),
    ]
    return call(field_kernel, out, args, scratch, 1_200_000_000, 7_000_000, free)


def rows_of(weight, start, stop):
    return weight.reshape(4, HALF, 2 * BS)[:, start:stop].reshape(-1, 2 * BS)


def mixing(weight):
    real = weight[0].T
    imag = weight[1].T
    return jnp.concatenate(
        [jnp.concatenate([real, -imag], axis=1), jnp.concatenate([imag, real], axis=1)], axis=0
    )


def stacked(value):
    high = lax.reduce_precision(value, 8, 7)
    return thrice((high.astype(bf16), (value - high).astype(bf16)), 1)


def keep_half(value, axis, flip, bit):
    half = value.shape[0] // 2
    size = lax.axis_size(axis)
    mine = lax.dynamic_slice_in_dim(value, bit * half, half, 0)
    other = lax.dynamic_slice_in_dim(value, (1 - bit) * half, half, 0)
    return mine + lax.ppermute(other, axis, [(n, n ^ flip) for n in range(size)])


def owned_rows(rows):
    dp = lax.axis_index("dp")
    px = lax.axis_index("px")
    py = lax.axis_index("py")
    rows = keep_half(rows, "dp", 1, dp % 2)
    rows = keep_half(rows, "dp", 2, dp // 2)
    rows = keep_half(rows, "px", 1, px % 2)
    pieces = rows.reshape(8, -1, 128)
    total = lax.dynamic_index_in_dim(pieces, py, 0, keepdims=False)
    for offset in range(1, 8):
        piece = lax.dynamic_index_in_dim(pieces, (py + offset) % 8, 0, keepdims=False)
        total = total + lax.ppermute(piece, "py", [(n, (n + offset) % 8) for n in range(8)])
    return total


def partner(value, flip):
    return lax.ppermute(value, "dp", [(n, n ^ flip) for n in range(4)])


def exchange(value):
    return lax.all_to_all(value, ("px", "py"), split_axis=0, concat_axis=0, tiled=True)


def shards(state_field, cotangent, first_weight, first_bias, second_weight, second_bias):
    depth_fwd, depth_bwd = depth_tables()
    plane_fwd, plane_bwd = plane_tables()
    twiddle = twiddle_table()
    owner = lax.axis_index("px") * 8 + lax.axis_index("py")
    block = owner // KZ
    doubling = jnp.where(owner % KZ == 0, 1.0, 2.0).astype(f32).reshape(1, 1)

    first = mixing(lax.dynamic_index_in_dim(first_weight, block, 1, keepdims=False))
    second = mixing(lax.dynamic_index_in_dim(second_weight, block, 1, keepdims=False))
    bias_one = lax.dynamic_index_in_dim(first_bias, block, 1, keepdims=False).reshape(2 * BS, 1)
    bias_two = lax.dynamic_index_in_dim(second_bias, block, 1, keepdims=False).reshape(2 * BS, 1)

    state_spec = exchange(depth_forward(state_field, depth_fwd))
    cot_spec = exchange(depth_forward(cotangent, depth_fwd))
    spec, outer, slope, square = pl.pallas_call(
        forward_kernel,
        out_shape=(GROUPED,) * 4,
        in_specs=[pl.BlockSpec(memory_space=pltpu.SMEM)] + vmem(7),
        out_specs=tuple(vmem(4)),
        scratch_shapes=[pltpu.VMEM(SPECTRAL, f32)],
        compiler_params=BIG,
        cost_estimate=pl.CostEstimate(
            flops=8_000_000_000, bytes_accessed=16_000_000, transcendentals=1_500_000
        ),
    )(doubling, state_spec, twiddle, plane_fwd, stacked(first), bias_one, stacked(second), bias_two)

    second_back = stacked(second.T)
    grad_two, plane = backward(
        cot_spec,
        twiddle,
        plane_fwd,
        plane_bwd,
        stacked(rows_of(first.T, 0, FIRST)),
        second_back,
        slope,
        square,
    )
    first_part = exchange(plane)
    rows, plane = rest(
        spec, outer, grad_two, slope, second_back, stacked(rows_of(first.T, FIRST, HALF)), twiddle, plane_bwd
    )
    rows = owned_rows(rows)
    plane = lax.dynamic_update_slice(
        plane, jnp.broadcast_to(rows[None], (64, *rows.shape)), (0, 2 * SECOND, 0)
    )
    first_part, plane = lax.optimization_barrier((first_part, plane))
    second_part = exchange(plane)
    mine = second_part[:, 2 * SECOND :]
    across = partner(mine, 1)
    beside = partner(mine, 2)
    state_grad = field(first_part, second_part, cotangent, depth_bwd).reshape(1, 8, 8, NZ, C)
    state_grad, across, beside = lax.optimization_barrier((state_grad, across, beside))
    sums = gathered((mine, beside, across, partner(beside, 1)))
    return (state_grad, *sums)


def solution(mesh):
    in_specs = (
        P("dp", "px", "py", None, None),
        P("dp", "px", "py", None, None),
        P(),
        P(),
        P(),
        P(),
    )
    out_specs = (P("dp", "px", "py", None, None), P(), P(), P(), P())
    return jax.shard_map(shards, mesh=mesh, in_specs=in_specs, out_specs=out_specs, check_vma=False)
```

```python
import math

import jax
import jax.numpy as jnp
import ml_dtypes
import numpy as np
from jax import lax
from jax.experimental import pallas as pl
from jax.experimental.pallas import tpu as pltpu
from jax.sharding import PartitionSpec as P

NX = 64
NY = 64
NZ = 32
NB = 4
BS = 96
KZ = 16
C = 384
HALF = BS // 2
FIRST = 32
BATCH = 4
SECOND = HALF - FIRST
CELLS = 64
STEP = 8
GROUPS = 64 // STEP
WIDE = STEP * 64
ROWS = 512
SHRINK = 0.25
f32 = jnp.float32
bf16 = jnp.bfloat16
BIG = pltpu.CompilerParams(vmem_limit_bytes=62 * 1024 * 1024)
SPECTRAL = (64, 2 * HALF, 128)
GROUPED = jax.ShapeDtypeStruct((GROUPS, 2 * BS, WIDE), f32)


def np_split(table):
    high = table.astype(np.float32).astype(ml_dtypes.bfloat16)
    low = (table - high.astype(np.float64)).astype(np.float32).astype(ml_dtypes.bfloat16)
    return high, low


def depth_tables():
    k = np.arange(KZ)[:, None]
    z = np.arange(NZ)[None, :]
    angle = 2.0 * np.pi * (k * z % NZ) / NZ
    scale = 1.0 / math.sqrt(NX * NY * NZ)
    pair = np.stack([np.cos(angle), -np.sin(angle)], axis=1) * scale
    eye = np.eye(8)
    forward = np.einsum("kqz,ab->kqabz", pair, eye).reshape(256, 256)
    scheme = ((0, 1), (0, 1, 0))
    return [
        np.concatenate([np_split(table)[n] for n in order], axis=1)
        for table, order in zip((forward, forward.T.copy()), scheme)
    ]


def plane_tables():
    j = np.arange(8)
    eight = np.exp(-2j * np.pi * np.outer(j, j) / 8.0)
    both = np.einsum("xk,yl->xykl", eight, eight).reshape(64, 64)
    real = np.zeros((2, 64, 2, 64))
    real[0, :, 0] = both.real
    real[0, :, 1] = both.imag
    real[1, :, 0] = -both.imag
    real[1, :, 1] = both.real
    forward = np.einsum("qxpf,cd->qcxpdf", real, np.eye(2)).reshape(256, 256)
    tables = np_split(forward), np_split(forward.T.copy())
    return [np.concatenate([high, high, low], axis=0) for high, low in tables]


def twiddle_table():
    k2 = np.arange(8)
    j = np.arange(8)
    one = np.exp(-2j * np.pi * np.outer(k2, j) / 64.0)
    both = np.einsum("kx,ly->klxy", one, one).reshape(64, 64)
    both = np.tile(both, (1, 2))
    return np.stack([both.real, both.imag], axis=1).astype(np.float32)


def split(value):
    high = value.astype(bf16)
    low = (value - high.astype(f32)).astype(bf16)
    return high, low


def dot(left, right, dims=((1,), (0,))):
    return lax.dot_general(left, right, (dims, ((), ())), preferred_element_type=f32)


def thrice(pair, axis):
    high, low = pair
    return jnp.concatenate([high, low, high], axis=axis)


def paired(pair, axis):
    high, low = pair
    return jnp.concatenate([high, high, low], axis=axis)


def dot3(left, right, dims=((1,), (0,))):
    return dot(thrice(left, 1), paired(right, dims[1][0]), dims)


def product(weight_ref, value):
    return dot(weight_ref[...], paired(split(value), 0))


def swap(upper, lower):
    lane = lax.broadcasted_iota(jnp.int32, upper.shape, 1)
    first = jnp.where(lane < 64, upper, pltpu.roll(lower, 64, 1))
    second = jnp.where(lane < 64, pltpu.roll(upper, 64, 1), lower)
    return first, second


def fft(re, im, sign):
    n = len(re)
    if n == 1:
        return re, im
    even_re, even_im = fft(re[0::2], im[0::2], sign)
    odd_re, odd_im = fft(re[1::2], im[1::2], sign)
    out_re = [None] * n
    out_im = [None] * n
    root = math.sqrt(0.5)
    for k in range(n // 2):
        a, b = odd_re[k], odd_im[k]
        turn = k * (8 // n)
        if turn == 1:
            a, b = (a - sign * b) * root, (b + sign * a) * root
        elif turn == 2:
            a, b = -sign * b, sign * a
        elif turn == 3:
            a, b = (-a - sign * b) * root, (-b + sign * a) * root
        out_re[k], out_im[k] = even_re[k] + a, even_im[k] + b
        out_re[k + n // 2], out_im[k + n // 2] = even_re[k] - a, even_im[k] - b
    return out_re, out_im


def read(ref, index, tile):
    half = ref.shape[1] // 2
    rows = slice(tile * 8, tile * 8 + 8), slice(half + tile * 8, half + tile * 8 + 8)
    return ref[index, rows[0], :], ref[index, rows[1], :]


def write(ref, index, tile, re, im):
    half = ref.shape[1] // 2
    ref[index, tile * 8 : tile * 8 + 8, :] = re
    ref[index, half + tile * 8 : half + tile * 8 + 8, :] = im


def senders(src_ref, dst_ref, sign, before, after):
    def body(p, carry):
        before(p)
        for tile in range(src_ref.shape[1] // 16):
            re, im = zip(*[read(src_ref, p * 8 + n, tile) for n in range(8)])
            re, im = fft(re, im, sign)
            for n in range(8):
                write(dst_ref, p * 8 + n, tile, re[n], im[n])
        after(p)
        return carry

    lax.fori_loop(0, 8, body, 0)


def turned(a, b, twiddle_ref, index, sign):
    c = twiddle_ref[index, 0:1, :]
    s = twiddle_ref[index, 1:2, :] * sign
    return a * c - b * s, a * s + b * c


def plane_forward(src_ref, work_ref, twiddle_ref, before):
    senders(src_ref, work_ref, -1.0, before, lambda p: None)

    def body(p, carry):
        for tile in range(HALF // 8):
            re, im = zip(*[read(work_ref, n * 8 + p, tile) for n in range(8)])
            re, im = fft(re, im, -1.0)
            for n in range(8):
                write(work_ref, n * 8 + p, tile, *turned(re[n], im[n], twiddle_ref, n * 8 + p, 1.0))
        return carry

    lax.fori_loop(0, 8, body, 0)


def plane_backward(work_ref, out_ref, twiddle_ref, after):
    def body(p, carry):
        for tile in range(work_ref.shape[1] // 16):
            pairs = [
                turned(*read(work_ref, n * 8 + p, tile), twiddle_ref, n * 8 + p, -1.0)
                for n in range(8)
            ]
            re, im = fft(*zip(*pairs), 1.0)
            for n in range(8):
                write(work_ref, n * 8 + p, tile, re[n], im[n])
        return carry

    lax.fori_loop(0, 8, body, 0)
    senders(work_ref, out_ref, 1.0, lambda p: None, after)


def load_group(work_ref, group, table_ref):
    rows = [
        jnp.concatenate(
            [work_ref[group * STEP + n, :HALF], work_ref[group * STEP + n, HALF:]], axis=1
        )
        for n in range(STEP)
    ]
    values = dot(thrice(split(jnp.concatenate(rows, axis=0)), 1), table_ref[...])
    pairs = []
    for pair in range(STEP // 2):
        part = []
        for q in range(2):
            lanes = slice(q * 128, (q + 1) * 128)
            upper = values[2 * pair * HALF : (2 * pair + 1) * HALF, lanes]
            lower = values[(2 * pair + 1) * HALF : (2 * pair + 2) * HALF, lanes]
            part.extend(swap(upper, lower))
        pairs.append(jnp.concatenate(part, axis=0))
    return jnp.concatenate(pairs, axis=1)


def store_group(work_ref, group, spectral, table_ref):
    count = spectral.shape[0] // 4
    rows = []
    for pair in range(STEP // 2):
        part = spectral[:, pair * 128 : (pair + 1) * 128]
        parts = [
            swap(
                part[2 * q * count : (2 * q + 1) * count],
                part[(2 * q + 1) * count : (2 * q + 2) * count],
            )
            for q in range(2)
        ]
        for n in range(2):
            rows.append(jnp.concatenate([parts[0][n], parts[1][n]], axis=1))
    values = dot(thrice(split(jnp.concatenate(rows, axis=0)), 1), table_ref[...])
    for n in range(STEP):
        for q in range(2):
            work_ref[group * STEP + n, q * count : (q + 1) * count] = values[
                n * count : (n + 1) * count, q * 128 : (q + 1) * 128
            ]


def depth_kernel(field_hbm, both_hbm, out_hbm, field_ref, both_ref, out_ref, work_ref, sems, out_sems):
    table = pltpu.make_async_copy(both_hbm, both_ref, sems.at[8])
    table.start()
    copies = []
    for g in range(8):
        span = pl.ds(g * 256, 256)
        copies.append(pltpu.make_async_copy(field_hbm.at[span], field_ref.at[span], sems.at[g]))
        copies[-1].start()
    table.wait()
    for g in range(8):
        if g % BATCH == 0:
            for copy in copies[g : g + BATCH]:
                copy.wait()
        rows = field_ref[g * 256 : (g + 1) * 256, :]
        values = dot(both_ref[...], jnp.concatenate([rows, rows], axis=0))
        work_ref[:, g * 8 : (g + 1) * 8, :] = values.reshape(2 * KZ, 8, C)
    sends = []
    for k in range(KZ):
        values = work_ref[2 * k : 2 * k + 2].reshape(2 * CELLS, C).T
        for b in range(NB):
            upper = values[b * BS : b * BS + HALF]
            lower = values[b * BS + HALF : (b + 1) * BS]
            out_ref[b, k, :HALF], out_ref[b, k, HALF:] = swap(upper, lower)
        sends.append(pltpu.make_async_copy(out_ref.at[:, k], out_hbm.at[:, k], out_sems.at[k]))
        if k % BATCH == BATCH - 1:
            for send in sends[-BATCH:]:
                send.start()
    for send in sends:
        send.wait()


def forward_kernel(
    doubling_ref, src_ref, twiddle_ref, t_ref, w1, b1, w2, b2,
    spec_ref, outer_ref, slope_ref, square_ref, work_ref,
):
    plane_forward(src_ref, work_ref, twiddle_ref, lambda p: None)
    root = math.sqrt(2.0 / math.pi)

    def body(g, carry):
        spectral = load_group(work_ref, g, t_ref)
        spec_ref[g] = spectral
        pre = product(w1, spectral) + b1[...]
        pre_sq = pre * pre
        t = jnp.tanh(root * (pre + 0.044715 * (pre * pre_sq)))
        outer = 0.5 * pre * (1.0 + t)
        outer_ref[g] = outer
        slope_ref[g] = 0.5 * (1.0 + t) + 0.5 * pre * (1.0 - t * t) * (
            root * (1.0 + 3.0 * 0.044715 * pre_sq)
        )
        pre_two = product(w2, outer) + b2[...]
        t2 = jnp.tanh(pre_two * (1.0 / SHRINK))
        square_ref[g] = t2 * t2 * doubling_ref[0, 0]
        return carry

    lax.fori_loop(0, GROUPS, body, 0)


def block_of(hbm, ref, sems, p):
    span = pl.ds(p * 8, 8)
    return pltpu.make_async_copy(hbm.at[span], ref.at[span], sems.at[p])


def backward_kernel(
    src_hbm, twiddle_hbm, t_hbm, back_hbm, w1_hbm, w2_hbm, slope_hbm, square_hbm,
    two_hbm, out_hbm,
    src_ref, twiddle_ref, t_ref, back_ref, w1, w2, slope_ref, square_ref,
    two_ref, out_ref, work_ref, part_ref, src_sems, sems, square_sems, slope_sems,
    two_sems, out_sems,
):
    for p in range(8):
        block_of(src_hbm, src_ref, src_sems, p).start()
    pairs = (
        (twiddle_hbm, twiddle_ref), (t_hbm, t_ref), (w2_hbm, w2),
        (w1_hbm, w1), (back_hbm, back_ref),
    )
    loads = [pltpu.make_async_copy(a, b, sems.at[n]) for n, (a, b) in enumerate(pairs)]
    for load in loads:
        load.start()
    loads[0].wait()

    def before(p):
        block_of(src_hbm, src_ref, src_sems, p).wait()
        pltpu.make_async_copy(square_hbm.at[p], square_ref.at[p], square_sems.at[p]).start()
        pltpu.make_async_copy(slope_hbm.at[p], slope_ref.at[p], slope_sems.at[p]).start()

    plane_forward(src_ref, work_ref, twiddle_ref, before)
    for load in loads[1:]:
        load.wait()

    sends = []
    spectral = load_group(work_ref, 0, t_ref)
    for g in range(GROUPS):
        following = load_group(work_ref, g + 1, t_ref) if g + 1 < GROUPS else None
        for n in range(g, g + BATCH) if g % BATCH == 0 else ():
            pltpu.make_async_copy(square_hbm.at[n], square_ref.at[n], square_sems.at[n]).wait()
            pltpu.make_async_copy(slope_hbm.at[n], slope_ref.at[n], slope_sems.at[n]).wait()
        grad_two = spectral * square_ref[g]
        two_ref[g] = grad_two
        sends.append(pltpu.make_async_copy(two_ref.at[g], two_hbm.at[g], two_sems.at[g]))
        if g % BATCH == BATCH - 1:
            for send in sends[-BATCH:]:
                send.start()
        grad_one = product(w2, grad_two) * slope_ref[g]
        store_group(part_ref, g, product(w1, grad_one), back_ref)
        spectral = following
    plane_backward(
        part_ref, out_ref, twiddle_ref, lambda p: block_of(out_ref, out_hbm, out_sems, p).start()
    )
    for send in sends:
        send.wait()
    for p in range(8):
        block_of(out_ref, out_hbm, out_sems, p).wait()


def spread(value):
    gap = jnp.zeros((128 - BS, value.shape[1]), value.dtype)
    return jnp.concatenate([value[:BS], gap, value[BS:], gap], axis=0)


def rest_kernel(
    spec_ref, outer_ref, two_ref, slope_ref, w2, w1, twiddle_ref, back_ref,
    out_ref, plane_hbm,
    t1_ref, s1_ref, t2_ref, s2_ref, part_ref, plane_ref, sends,
):
    lanes = ((1,), (1,))
    g = pl.program_id(0)

    @pl.when(g == 0)
    def _():
        for ref in (t1_ref, s1_ref, t2_ref, s2_ref):
            ref[...] = jnp.zeros(ref.shape, f32)

    grad_two = two_ref[0]
    two = spread(grad_two)
    t2_ref[...] += dot3(split(outer_ref[0]), split(two), lanes)
    s2_ref[...] += two
    grad_one = product(w2, grad_two) * slope_ref[0]
    one = spread(grad_one)
    t1_ref[...] += dot3(split(spec_ref[0]), split(one), lanes)
    s1_ref[...] += one
    store_group(part_ref, g, product(w1, grad_one), back_ref)

    def send(p):
        span = pl.ds(p * 8, 8)
        rows = pl.ds(0, 2 * SECOND)
        return pltpu.make_async_copy(plane_ref.at[span], plane_hbm.at[span, rows], sends.at[p])

    @pl.when(g == GROUPS - 1)
    def _():
        plane_backward(part_ref, plane_ref, twiddle_ref, lambda p: send(p).start())
        norm = 1.0 / math.sqrt(4 * NX * NY * KZ)
        ones = jnp.ones((8, WIDE), bf16)
        row = lax.broadcasted_iota(jnp.int32, (8, 128), 0)
        out_ref[4 * BS :] = jnp.zeros((ROWS - 4 * BS, 128), f32)
        biases = jnp.zeros((8, 128), f32)
        for n, (table_ref, total_ref) in enumerate(((t1_ref, s1_ref), (t2_ref, s2_ref))):
            table = table_ref[...]
            real = table[:BS, :128] + table[BS:, 128:]
            imag = table[:BS, 128:] - table[BS:, :128]
            out_ref[2 * n * BS : (2 * n + 1) * BS] = real * norm
            out_ref[(2 * n + 1) * BS : (2 * n + 2) * BS] = imag * norm
            high, low = split(total_ref[...])
            sums = dot(ones, high, lanes) + dot(ones, low, lanes)
            for q in range(2):
                biases = jnp.where(row == 2 * n + q, sums[:, q * 128 : (q + 1) * 128], biases)
        out_ref[4 * BS : 4 * BS + 8] = biases * norm
        for p in range(8):
            send(p).wait()


def field_kernel(
    first_hbm, second_hbm, cotangent_hbm, table_hbm, out_hbm,
    first_ref, second_ref, cotangent_ref, table_ref, out_ref, work_ref,
    first_sems, second_sems, sems, out_sems,
):
    loads = []
    for k in range(KZ):
        span = pl.ds(0, 2 * SECOND)
        loads.append(
            (
                pltpu.make_async_copy(first_hbm.at[:, k], first_ref.at[:, k], first_sems.at[k]),
                pltpu.make_async_copy(
                    second_hbm.at[:, k, span], second_ref.at[:, k], second_sems.at[k]
                ),
            )
        )
    pairs = ((table_hbm, table_ref), (cotangent_hbm, cotangent_ref))
    others = [pltpu.make_async_copy(a, b, sems.at[n]) for n, (a, b) in enumerate(pairs)]
    for load in loads:
        load[0].start()
        load[1].start()
    for load in others:
        load.start()
    for k in range(KZ):
        for load in loads[k : k + BATCH] if k % BATCH == 0 else ():
            load[0].wait()
            load[1].wait()
        parts = []
        for b in range(NB):
            left = swap(first_ref[b, k, :FIRST], first_ref[b, k, FIRST:])
            right = swap(second_ref[b, k, :SECOND], second_ref[b, k, SECOND:])
            parts.extend([left[0], right[0], left[1], right[1]])
        values = jnp.concatenate(parts, axis=0).T
        work_ref[2 * k : 2 * k + 2] = values.reshape(2, CELLS, C)
    for load in others:
        load.wait()
    sends = []
    for g in range(8):
        values = product(table_ref, work_ref[:, g * 8 : (g + 1) * 8, :].reshape(256, C))
        span = slice(g * 256, (g + 1) * 256)
        out_ref[span, :] = (cotangent_ref[span, :].astype(f32) + values).astype(bf16)
        rows = pl.ds(g * 256, 256)
        sends.append(pltpu.make_async_copy(out_ref.at[rows], out_hbm.at[rows], out_sems.at[g]))
        if g % BATCH == BATCH - 1:
            for send in sends[-BATCH:]:
                send.start()
    for send in sends:
        send.wait()


def gather_kernel(core_ref, low_ref, *refs):
    sources, (one_ref, bias_one_ref, two_ref, bias_two_ref, all_ref) = refs[:4], refs[4:]
    core = core_ref[0, 0]
    low = low_ref[0, 0]
    for n, source in enumerate(sources):
        place = (core + n // 2) % 2 * 2 + (low + n % 2) % 2
        start = pl.multiple_of(place * (ROWS // 4), ROWS // 4)
        all_ref[:, pl.ds(start, ROWS // 4), :] = source[...].reshape(NB, ROWS // 4, 128)
    for b in range(NB):
        for q in range(2):
            one_ref[q, b] = all_ref[b, q * BS : (q + 1) * BS, :BS]
            two_ref[q, b] = all_ref[b, (2 + q) * BS : (3 + q) * BS, :BS]
            bias_one_ref[q, b : b + 1] = all_ref[b, 4 * BS + q : 4 * BS + q + 1, :BS]
            bias_two_ref[q, b : b + 1] = all_ref[b, 4 * BS + 2 + q : 4 * BS + 3 + q, :BS]


def gathered(sources):
    dp = lax.axis_index("dp")
    bits = [(dp % 2).reshape(1, 1).astype(jnp.int32), (dp // 2).reshape(1, 1).astype(jnp.int32)]
    weight = jax.ShapeDtypeStruct((2, NB, BS, BS), f32)
    bias = jax.ShapeDtypeStruct((2, NB, BS), f32)
    return pl.pallas_call(
        gather_kernel,
        out_shape=(weight, bias, weight, bias),
        in_specs=[pl.BlockSpec(memory_space=pltpu.SMEM)] * 2 + vmem(4),
        out_specs=tuple(vmem(4)),
        scratch_shapes=[pltpu.VMEM((NB, ROWS, 128), f32)],
        compiler_params=pltpu.CompilerParams(vmem_limit_bytes=16 * 1024 * 1024),
        cost_estimate=pl.CostEstimate(flops=0, bytes_accessed=2_000_000, transcendentals=0),
    )(*bits, *sources)


def vmem(n):
    return [pl.BlockSpec(memory_space=pltpu.VMEM)] * n


def free(n):
    return [pl.BlockSpec(memory_space=pl.ANY)] * n


def held(*values):
    return [pltpu.VMEM(v.shape, v.dtype) for v in values]


def sems(*counts):
    return [pltpu.SemaphoreType.DMA((n,)) for n in counts]


def call(kernel, out_shape, args, scratch, flops, moved, place=vmem):
    outs = len(out_shape) if isinstance(out_shape, tuple) else 1
    return pl.pallas_call(
        kernel,
        out_shape=out_shape,
        in_specs=place(len(args)),
        out_specs=tuple(place(outs)) if isinstance(out_shape, tuple) else place(1)[0],
        scratch_shapes=scratch,
        compiler_params=BIG,
        cost_estimate=pl.CostEstimate(flops=flops, bytes_accessed=moved, transcendentals=0),
    )(*args)


def depth_forward(field, tables):
    args = (field.reshape(2048, C), tables)
    out = jax.ShapeDtypeStruct((NB, KZ, 2 * HALF, 128), f32)
    scratch = [*held(*args, out), pltpu.VMEM((2 * KZ, CELLS, C), f32), *sems(9, KZ)]
    return call(depth_kernel, out, args, scratch, 800_000_000, 5_000_000, free).reshape(SPECTRAL)


def backward(cot_spec, twiddle, plane_fwd, plane_bwd, first, second, slope, square):
    args = (cot_spec, twiddle, plane_fwd, plane_bwd, first, second, slope, square)
    outs = (GROUPED, jax.ShapeDtypeStruct((64, 2 * FIRST, 128), f32))
    scratch = [
        *held(*args, *outs),
        pltpu.VMEM(SPECTRAL, f32),
        pltpu.VMEM((64, 2 * FIRST, 128), f32),
        *sems(8, 5, *[GROUPS] * 3, 8),
    ]
    return call(backward_kernel, outs, args, scratch, 10_000_000_000, 20_000_000, free)


def by_group(n):
    return [pl.BlockSpec((1, 2 * BS, WIDE), lambda g: (g, 0, 0))] * n


def rest(spec, outer, grad_two, slope, second, first, twiddle, plane_bwd):
    return pl.pallas_call(
        rest_kernel,
        grid=(GROUPS,),
        out_shape=(
            jax.ShapeDtypeStruct((ROWS, 128), f32),
            jax.ShapeDtypeStruct((64, 2 * SECOND + 8, 128), f32),
        ),
        in_specs=by_group(4) + vmem(4),
        out_specs=(pl.BlockSpec((ROWS, 128), lambda g: (0, 0)), *free(1)),
        scratch_shapes=[
            *[pltpu.VMEM((2 * BS, 256), f32), pltpu.VMEM((256, WIDE), f32)] * 2,
            *[pltpu.VMEM((64, 2 * SECOND, 128), f32)] * 2,
            *sems(8),
        ],
        compiler_params=BIG,
        cost_estimate=pl.CostEstimate(
            flops=8_000_000_000, bytes_accessed=16_000_000, transcendentals=0
        ),
    )(spec, outer, grad_two, slope, second, first, twiddle, plane_bwd)


def field(first, second, cotangent, tables):
    args = (
        first.reshape(NB, KZ, 2 * FIRST, 128),
        second.reshape(NB, KZ, 2 * SECOND + 8, 128),
        cotangent.reshape(2048, C),
        tables,
    )
    out = jax.ShapeDtypeStruct((2048, C), bf16)
    scratch = [
        *held(args[0], jax.ShapeDtypeStruct((NB, KZ, 2 * SECOND, 128), f32), *args[2:], out),
        pltpu.VMEM((2 * KZ, CELLS, C), f32),
        *sems(KZ, KZ, 2, 8),
    ]
    return call(field_kernel, out, args, scratch, 1_200_000_000, 7_000_000, free)


def rows_of(weight, start, stop):
    return weight.reshape(4, HALF, 2 * BS)[:, start:stop].reshape(-1, 2 * BS)


def mixing(weight):
    real = weight[0].T
    imag = weight[1].T
    return jnp.concatenate(
        [jnp.concatenate([real, -imag], axis=1), jnp.concatenate([imag, real], axis=1)], axis=0
    )


def stacked(value):
    high = lax.reduce_precision(value, 8, 7)
    return thrice((high.astype(bf16), (value - high).astype(bf16)), 1)


def keep_half(value, axis, flip, bit):
    half = value.shape[0] // 2
    size = lax.axis_size(axis)
    mine = lax.dynamic_slice_in_dim(value, bit * half, half, 0)
    other = lax.dynamic_slice_in_dim(value, (1 - bit) * half, half, 0)
    return mine + lax.ppermute(other, axis, [(n, n ^ flip) for n in range(size)])


def owned_rows(rows):
    dp = lax.axis_index("dp")
    px = lax.axis_index("px")
    py = lax.axis_index("py")
    rows = keep_half(rows, "dp", 1, dp % 2)
    rows = keep_half(rows, "dp", 2, dp // 2)
    rows = keep_half(rows, "px", 1, px % 2)
    pieces = rows.reshape(8, -1, 128)
    total = lax.dynamic_index_in_dim(pieces, py, 0, keepdims=False)
    for offset in range(1, 8):
        piece = lax.dynamic_index_in_dim(pieces, (py + offset) % 8, 0, keepdims=False)
        total = total + lax.ppermute(piece, "py", [(n, (n + offset) % 8) for n in range(8)])
    return total


def partner(value, flip):
    return lax.ppermute(value, "dp", [(n, n ^ flip) for n in range(4)])


def exchange(value):
    return lax.all_to_all(value, ("px", "py"), split_axis=0, concat_axis=0, tiled=True)


def shards(state_field, cotangent, first_weight, first_bias, second_weight, second_bias):
    depth_fwd, depth_bwd = depth_tables()
    plane_fwd, plane_bwd = plane_tables()
    twiddle = twiddle_table()
    owner = lax.axis_index("px") * 8 + lax.axis_index("py")
    block = owner // KZ
    doubling = jnp.where(owner % KZ == 0, 1.0, 2.0).astype(f32).reshape(1, 1)

    first = mixing(lax.dynamic_index_in_dim(first_weight, block, 1, keepdims=False))
    second = mixing(lax.dynamic_index_in_dim(second_weight, block, 1, keepdims=False))
    bias_one = lax.dynamic_index_in_dim(first_bias, block, 1, keepdims=False).reshape(2 * BS, 1)
    bias_two = lax.dynamic_index_in_dim(second_bias, block, 1, keepdims=False).reshape(2 * BS, 1)

    state_spec = exchange(depth_forward(state_field, depth_fwd))
    cot_spec = exchange(depth_forward(cotangent, depth_fwd))
    spec, outer, slope, square = pl.pallas_call(
        forward_kernel,
        out_shape=(GROUPED,) * 4,
        in_specs=[pl.BlockSpec(memory_space=pltpu.SMEM)] + vmem(7),
        out_specs=tuple(vmem(4)),
        scratch_shapes=[pltpu.VMEM(SPECTRAL, f32)],
        compiler_params=BIG,
        cost_estimate=pl.CostEstimate(
            flops=8_000_000_000, bytes_accessed=16_000_000, transcendentals=1_500_000
        ),
    )(doubling, state_spec, twiddle, plane_fwd, stacked(first), bias_one, stacked(second), bias_two)

    second_back = stacked(second.T)
    grad_two, plane = backward(
        cot_spec,
        twiddle,
        plane_fwd,
        plane_bwd,
        stacked(rows_of(first.T, 0, FIRST)),
        second_back,
        slope,
        square,
    )
    first_part = exchange(plane)
    rows, plane = rest(
        spec, outer, grad_two, slope, second_back, stacked(rows_of(first.T, FIRST, HALF)), twiddle, plane_bwd
    )
    rows = owned_rows(rows)
    plane = lax.dynamic_update_slice(
        plane, jnp.broadcast_to(rows[None], (64, *rows.shape)), (0, 2 * SECOND, 0)
    )
    first_part, plane = lax.optimization_barrier((first_part, plane))
    second_part = exchange(plane)
    mine = second_part[:, 2 * SECOND :]
    across = partner(mine, 1)
    beside = partner(mine, 2)
    state_grad = field(first_part, second_part, cotangent, depth_bwd).reshape(1, 8, 8, NZ, C)
    state_grad, across, beside = lax.optimization_barrier((state_grad, across, beside))
    sums = gathered((mine, beside, across, partner(beside, 1)))
    return (state_grad, *sums)


def solution(mesh):
    in_specs = (
        P("dp", "px", "py", None, None),
        P("dp", "px", "py", None, None),
        P(),
        P(),
        P(),
        P(),
    )
    out_specs = (P("dp", "px", "py", None, None), P(), P(), P(), P())
    return jax.shard_map(shards, mesh=mesh, in_specs=in_specs, out_specs=out_specs, check_vma=False)
```

```python
import math

import jax
import jax.numpy as jnp
import ml_dtypes
import numpy as np
from jax import lax
from jax.experimental import pallas as pl
from jax.experimental.pallas import tpu as pltpu
from jax.sharding import PartitionSpec as P

NX = 64
NY = 64
NZ = 32
NB = 4
BS = 96
KZ = 16
C = 384
HALF = BS // 2
FIRST = 40
BATCH = 4
SECOND = HALF - FIRST
CELLS = 64
STEP = 8
GROUPS = 64 // STEP
WIDE = STEP * 64
ROWS = 512
SHRINK = 0.25
f32 = jnp.float32
bf16 = jnp.bfloat16
BIG = pltpu.CompilerParams(vmem_limit_bytes=62 * 1024 * 1024)
SPECTRAL = (64, 2 * HALF, 128)
GROUPED = jax.ShapeDtypeStruct((GROUPS, 2 * BS, WIDE), f32)


def np_split(table):
    high = table.astype(np.float32).astype(ml_dtypes.bfloat16)
    low = (table - high.astype(np.float64)).astype(np.float32).astype(ml_dtypes.bfloat16)
    return high, low


def depth_tables():
    k = np.arange(KZ)[:, None]
    z = np.arange(NZ)[None, :]
    angle = 2.0 * np.pi * (k * z % NZ) / NZ
    scale = 1.0 / math.sqrt(NX * NY * NZ)
    pair = np.stack([np.cos(angle), -np.sin(angle)], axis=1) * scale
    eye = np.eye(8)
    forward = np.einsum("kqz,ab->kqabz", pair, eye).reshape(256, 256)
    scheme = ((0, 1), (0, 1, 0))
    return [
        np.concatenate([np_split(table)[n] for n in order], axis=1)
        for table, order in zip((forward, forward.T.copy()), scheme)
    ]


def plane_tables():
    j = np.arange(8)
    eight = np.exp(-2j * np.pi * np.outer(j, j) / 8.0)
    both = np.einsum("xk,yl->xykl", eight, eight).reshape(64, 64)
    real = np.zeros((2, 64, 2, 64))
    real[0, :, 0] = both.real
    real[0, :, 1] = both.imag
    real[1, :, 0] = -both.imag
    real[1, :, 1] = both.real
    forward = np.einsum("qxpf,cd->qcxpdf", real, np.eye(2)).reshape(256, 256)
    tables = np_split(forward), np_split(forward.T.copy())
    return [np.concatenate([high, high, low], axis=0) for high, low in tables]


def twiddle_table():
    k2 = np.arange(8)
    j = np.arange(8)
    one = np.exp(-2j * np.pi * np.outer(k2, j) / 64.0)
    both = np.einsum("kx,ly->klxy", one, one).reshape(64, 64)
    both = np.tile(both, (1, 2))
    return np.stack([both.real, both.imag], axis=1).astype(np.float32)


def split(value):
    high = value.astype(bf16)
    low = (value - high.astype(f32)).astype(bf16)
    return high, low


def dot(left, right, dims=((1,), (0,))):
    return lax.dot_general(left, right, (dims, ((), ())), preferred_element_type=f32)


def thrice(pair, axis):
    high, low = pair
    return jnp.concatenate([high, low, high], axis=axis)


def paired(pair, axis):
    high, low = pair
    return jnp.concatenate([high, high, low], axis=axis)


def dot3(left, right, dims=((1,), (0,))):
    return dot(thrice(left, 1), paired(right, dims[1][0]), dims)


def product(weight_ref, value):
    return dot(weight_ref[...], paired(split(value), 0))


def swap(upper, lower):
    lane = lax.broadcasted_iota(jnp.int32, upper.shape, 1)
    first = jnp.where(lane < 64, upper, pltpu.roll(lower, 64, 1))
    second = jnp.where(lane < 64, pltpu.roll(upper, 64, 1), lower)
    return first, second


def fft(re, im, sign):
    n = len(re)
    if n == 1:
        return re, im
    even_re, even_im = fft(re[0::2], im[0::2], sign)
    odd_re, odd_im = fft(re[1::2], im[1::2], sign)
    out_re = [None] * n
    out_im = [None] * n
    root = math.sqrt(0.5)
    for k in range(n // 2):
        a, b = odd_re[k], odd_im[k]
        turn = k * (8 // n)
        if turn == 1:
            a, b = (a - sign * b) * root, (b + sign * a) * root
        elif turn == 2:
            a, b = -sign * b, sign * a
        elif turn == 3:
            a, b = (-a - sign * b) * root, (-b + sign * a) * root
        out_re[k], out_im[k] = even_re[k] + a, even_im[k] + b
        out_re[k + n // 2], out_im[k + n // 2] = even_re[k] - a, even_im[k] - b
    return out_re, out_im


def read(ref, index, tile):
    half = ref.shape[1] // 2
    rows = slice(tile * 8, tile * 8 + 8), slice(half + tile * 8, half + tile * 8 + 8)
    return ref[index, rows[0], :], ref[index, rows[1], :]


def write(ref, index, tile, re, im):
    half = ref.shape[1] // 2
    ref[index, tile * 8 : tile * 8 + 8, :] = re
    ref[index, half + tile * 8 : half + tile * 8 + 8, :] = im


def senders(src_ref, dst_ref, sign, before, after):
    def body(p, carry):
        before(p)
        for tile in range(src_ref.shape[1] // 16):
            re, im = zip(*[read(src_ref, p * 8 + n, tile) for n in range(8)])
            re, im = fft(re, im, sign)
            for n in range(8):
                write(dst_ref, p * 8 + n, tile, re[n], im[n])
        after(p)
        return carry

    lax.fori_loop(0, 8, body, 0)


def turned(a, b, twiddle_ref, index, sign):
    c = twiddle_ref[index, 0:1, :]
    s = twiddle_ref[index, 1:2, :] * sign
    return a * c - b * s, a * s + b * c


def plane_forward(src_ref, work_ref, twiddle_ref, before):
    senders(src_ref, work_ref, -1.0, before, lambda p: None)

    def body(p, carry):
        for tile in range(HALF // 8):
            re, im = zip(*[read(work_ref, n * 8 + p, tile) for n in range(8)])
            re, im = fft(re, im, -1.0)
            for n in range(8):
                write(work_ref, n * 8 + p, tile, *turned(re[n], im[n], twiddle_ref, n * 8 + p, 1.0))
        return carry

    lax.fori_loop(0, 8, body, 0)


def plane_backward(work_ref, out_ref, twiddle_ref, after):
    def body(p, carry):
        for tile in range(work_ref.shape[1] // 16):
            pairs = [
                turned(*read(work_ref, n * 8 + p, tile), twiddle_ref, n * 8 + p, -1.0)
                for n in range(8)
            ]
            re, im = fft(*zip(*pairs), 1.0)
            for n in range(8):
                write(work_ref, n * 8 + p, tile, re[n], im[n])
        return carry

    lax.fori_loop(0, 8, body, 0)
    senders(work_ref, out_ref, 1.0, lambda p: None, after)


def load_group(work_ref, group, table_ref):
    rows = [
        jnp.concatenate(
            [work_ref[group * STEP + n, :HALF], work_ref[group * STEP + n, HALF:]], axis=1
        )
        for n in range(STEP)
    ]
    values = dot(thrice(split(jnp.concatenate(rows, axis=0)), 1), table_ref[...])
    pairs = []
    for pair in range(STEP // 2):
        part = []
        for q in range(2):
            lanes = slice(q * 128, (q + 1) * 128)
            upper = values[2 * pair * HALF : (2 * pair + 1) * HALF, lanes]
            lower = values[(2 * pair + 1) * HALF : (2 * pair + 2) * HALF, lanes]
            part.extend(swap(upper, lower))
        pairs.append(jnp.concatenate(part, axis=0))
    return jnp.concatenate(pairs, axis=1)


def store_group(work_ref, group, spectral, table_ref):
    count = spectral.shape[0] // 4
    rows = []
    for pair in range(STEP // 2):
        part = spectral[:, pair * 128 : (pair + 1) * 128]
        parts = [
            swap(
                part[2 * q * count : (2 * q + 1) * count],
                part[(2 * q + 1) * count : (2 * q + 2) * count],
            )
            for q in range(2)
        ]
        for n in range(2):
            rows.append(jnp.concatenate([parts[0][n], parts[1][n]], axis=1))
    values = dot(thrice(split(jnp.concatenate(rows, axis=0)), 1), table_ref[...])
    for n in range(STEP):
        for q in range(2):
            work_ref[group * STEP + n, q * count : (q + 1) * count] = values[
                n * count : (n + 1) * count, q * 128 : (q + 1) * 128
            ]


def depth_kernel(field_hbm, both_hbm, out_hbm, field_ref, both_ref, out_ref, work_ref, sems, out_sems):
    table = pltpu.make_async_copy(both_hbm, both_ref, sems.at[8])
    table.start()
    copies = []
    for g in range(8):
        span = pl.ds(g * 256, 256)
        copies.append(pltpu.make_async_copy(field_hbm.at[span], field_ref.at[span], sems.at[g]))
        copies[-1].start()
    table.wait()
    for g in range(8):
        if g % BATCH == 0:
            for copy in copies[g : g + BATCH]:
                copy.wait()
        rows = field_ref[g * 256 : (g + 1) * 256, :]
        values = dot(both_ref[...], jnp.concatenate([rows, rows], axis=0))
        work_ref[:, g * 8 : (g + 1) * 8, :] = values.reshape(2 * KZ, 8, C)
    sends = []
    for k in range(KZ):
        values = work_ref[2 * k : 2 * k + 2].reshape(2 * CELLS, C).T
        for b in range(NB):
            upper = values[b * BS : b * BS + HALF]
            lower = values[b * BS + HALF : (b + 1) * BS]
            out_ref[b, k, :HALF], out_ref[b, k, HALF:] = swap(upper, lower)
        sends.append(pltpu.make_async_copy(out_ref.at[:, k], out_hbm.at[:, k], out_sems.at[k]))
        if k % BATCH == BATCH - 1:
            for send in sends[-BATCH:]:
                send.start()
    for send in sends:
        send.wait()


def forward_kernel(
    doubling_ref, src_ref, twiddle_ref, t_ref, w1, b1, w2, b2,
    spec_ref, outer_ref, slope_ref, square_ref, work_ref,
):
    plane_forward(src_ref, work_ref, twiddle_ref, lambda p: None)
    root = math.sqrt(2.0 / math.pi)

    def body(g, carry):
        spectral = load_group(work_ref, g, t_ref)
        spec_ref[g] = spectral
        pre = product(w1, spectral) + b1[...]
        pre_sq = pre * pre
        t = jnp.tanh(root * (pre + 0.044715 * (pre * pre_sq)))
        outer = 0.5 * pre * (1.0 + t)
        outer_ref[g] = outer
        slope_ref[g] = 0.5 * (1.0 + t) + 0.5 * pre * (1.0 - t * t) * (
            root * (1.0 + 3.0 * 0.044715 * pre_sq)
        )
        pre_two = product(w2, outer) + b2[...]
        t2 = jnp.tanh(pre_two * (1.0 / SHRINK))
        square_ref[g] = t2 * t2 * doubling_ref[0, 0]
        return carry

    lax.fori_loop(0, GROUPS, body, 0)


def block_of(hbm, ref, sems, p):
    span = pl.ds(p * 8, 8)
    return pltpu.make_async_copy(hbm.at[span], ref.at[span], sems.at[p])


def backward_kernel(
    src_hbm, twiddle_hbm, t_hbm, back_hbm, w1_hbm, w2_hbm, slope_hbm, square_hbm,
    two_hbm, out_hbm,
    src_ref, twiddle_ref, t_ref, back_ref, w1, w2, slope_ref, square_ref,
    two_ref, out_ref, work_ref, part_ref, src_sems, sems, square_sems, slope_sems,
    two_sems, out_sems,
):
    pairs = (
        (twiddle_hbm, twiddle_ref), (t_hbm, t_ref), (w2_hbm, w2),
        (w1_hbm, w1), (back_hbm, back_ref),
    )
    loads = [pltpu.make_async_copy(a, b, sems.at[n]) for n, (a, b) in enumerate(pairs)]
    loads[0].start()
    for p in range(8):
        block_of(src_hbm, src_ref, src_sems, p).start()
    for load in loads[1:]:
        load.start()
    loads[0].wait()

    def before(p):
        block_of(src_hbm, src_ref, src_sems, p).wait()
        pltpu.make_async_copy(square_hbm.at[p], square_ref.at[p], square_sems.at[p]).start()
        pltpu.make_async_copy(slope_hbm.at[p], slope_ref.at[p], slope_sems.at[p]).start()

    plane_forward(src_ref, work_ref, twiddle_ref, before)
    for load in loads[1:]:
        load.wait()

    sends = []
    spectral = load_group(work_ref, 0, t_ref)
    for g in range(GROUPS):
        following = load_group(work_ref, g + 1, t_ref) if g + 1 < GROUPS else None
        for n in range(g, g + BATCH) if g % BATCH == 0 else ():
            pltpu.make_async_copy(square_hbm.at[n], square_ref.at[n], square_sems.at[n]).wait()
            pltpu.make_async_copy(slope_hbm.at[n], slope_ref.at[n], slope_sems.at[n]).wait()
        grad_two = spectral * square_ref[g]
        two_ref[g] = grad_two
        sends.append(pltpu.make_async_copy(two_ref.at[g], two_hbm.at[g], two_sems.at[g]))
        if g % BATCH == BATCH - 1:
            for send in sends[-BATCH:]:
                send.start()
        grad_one = product(w2, grad_two) * slope_ref[g]
        store_group(part_ref, g, product(w1, grad_one), back_ref)
        spectral = following
    plane_backward(
        part_ref, out_ref, twiddle_ref, lambda p: block_of(out_ref, out_hbm, out_sems, p).start()
    )
    for send in sends:
        send.wait()
    for p in range(8):
        block_of(out_ref, out_hbm, out_sems, p).wait()


def spread(value):
    gap = jnp.zeros((128 - BS, value.shape[1]), value.dtype)
    return jnp.concatenate([value[:BS], gap, value[BS:], gap], axis=0)


def rest_kernel(
    spec_ref, outer_ref, two_ref, slope_ref, w2, w1, twiddle_ref, back_ref,
    out_ref, plane_hbm,
    t1_ref, s1_ref, t2_ref, s2_ref, part_ref, plane_ref, sends,
):
    lanes = ((1,), (1,))
    g = pl.program_id(0)

    @pl.when(g == 0)
    def _():
        for ref in (t1_ref, s1_ref, t2_ref, s2_ref):
            ref[...] = jnp.zeros(ref.shape, f32)

    grad_two = two_ref[0]
    two = spread(grad_two)
    t2_ref[...] += dot3(split(outer_ref[0]), split(two), lanes)
    s2_ref[...] += two
    grad_one = product(w2, grad_two) * slope_ref[0]
    one = spread(grad_one)
    t1_ref[...] += dot3(split(spec_ref[0]), split(one), lanes)
    s1_ref[...] += one
    store_group(part_ref, g, product(w1, grad_one), back_ref)

    def send(p):
        span = pl.ds(p * 8, 8)
        rows = pl.ds(0, 2 * SECOND)
        return pltpu.make_async_copy(plane_ref.at[span], plane_hbm.at[span, rows], sends.at[p])

    @pl.when(g == GROUPS - 1)
    def _():
        plane_backward(part_ref, plane_ref, twiddle_ref, lambda p: send(p).start())
        norm = 1.0 / math.sqrt(4 * NX * NY * KZ)
        ones = jnp.ones((8, WIDE), bf16)
        row = lax.broadcasted_iota(jnp.int32, (8, 128), 0)
        out_ref[4 * BS :] = jnp.zeros((ROWS - 4 * BS, 128), f32)
        biases = jnp.zeros((8, 128), f32)
        for n, (table_ref, total_ref) in enumerate(((t1_ref, s1_ref), (t2_ref, s2_ref))):
            table = table_ref[...]
            real = table[:BS, :128] + table[BS:, 128:]
            imag = table[:BS, 128:] - table[BS:, :128]
            out_ref[2 * n * BS : (2 * n + 1) * BS] = real * norm
            out_ref[(2 * n + 1) * BS : (2 * n + 2) * BS] = imag * norm
            high, low = split(total_ref[...])
            sums = dot(ones, high, lanes) + dot(ones, low, lanes)
            for q in range(2):
                biases = jnp.where(row == 2 * n + q, sums[:, q * 128 : (q + 1) * 128], biases)
        out_ref[4 * BS : 4 * BS + 8] = biases * norm
        for p in range(8):
            send(p).wait()


def field_kernel(
    first_hbm, second_hbm, cotangent_hbm, table_hbm, out_hbm,
    first_ref, second_ref, cotangent_ref, table_ref, out_ref, work_ref,
    first_sems, second_sems, sems, out_sems,
):
    loads = []
    for k in range(KZ):
        span = pl.ds(0, 2 * SECOND)
        loads.append(
            (
                pltpu.make_async_copy(first_hbm.at[:, k], first_ref.at[:, k], first_sems.at[k]),
                pltpu.make_async_copy(
                    second_hbm.at[:, k, span], second_ref.at[:, k], second_sems.at[k]
                ),
            )
        )
    pairs = ((table_hbm, table_ref), (cotangent_hbm, cotangent_ref))
    others = [pltpu.make_async_copy(a, b, sems.at[n]) for n, (a, b) in enumerate(pairs)]
    for load in loads:
        load[0].start()
        load[1].start()
    for load in others:
        load.start()
    for k in range(KZ):
        for load in loads[k : k + BATCH] if k % BATCH == 0 else ():
            load[0].wait()
            load[1].wait()
        parts = []
        for b in range(NB):
            left = swap(first_ref[b, k, :FIRST], first_ref[b, k, FIRST:])
            right = swap(second_ref[b, k, :SECOND], second_ref[b, k, SECOND:])
            parts.extend([left[0], right[0], left[1], right[1]])
        values = jnp.concatenate(parts, axis=0).T
        work_ref[2 * k : 2 * k + 2] = values.reshape(2, CELLS, C)
    for load in others:
        load.wait()
    sends = []
    for g in range(8):
        values = product(table_ref, work_ref[:, g * 8 : (g + 1) * 8, :].reshape(256, C))
        span = slice(g * 256, (g + 1) * 256)
        out_ref[span, :] = (cotangent_ref[span, :].astype(f32) + values).astype(bf16)
        rows = pl.ds(g * 256, 256)
        sends.append(pltpu.make_async_copy(out_ref.at[rows], out_hbm.at[rows], out_sems.at[g]))
        if g % BATCH == BATCH - 1:
            for send in sends[-BATCH:]:
                send.start()
    for send in sends:
        send.wait()


def gather_kernel(core_ref, low_ref, *refs):
    sources, (one_ref, bias_one_ref, two_ref, bias_two_ref, all_ref) = refs[:4], refs[4:]
    core = core_ref[0, 0]
    low = low_ref[0, 0]
    for n, source in enumerate(sources):
        place = (core + n // 2) % 2 * 2 + (low + n % 2) % 2
        start = pl.multiple_of(place * (ROWS // 4), ROWS // 4)
        all_ref[:, pl.ds(start, ROWS // 4), :] = source[...].reshape(NB, ROWS // 4, 128)
    for b in range(NB):
        for q in range(2):
            one_ref[q, b] = all_ref[b, q * BS : (q + 1) * BS, :BS]
            two_ref[q, b] = all_ref[b, (2 + q) * BS : (3 + q) * BS, :BS]
            bias_one_ref[q, b : b + 1] = all_ref[b, 4 * BS + q : 4 * BS + q + 1, :BS]
            bias_two_ref[q, b : b + 1] = all_ref[b, 4 * BS + 2 + q : 4 * BS + 3 + q, :BS]


def gathered(sources):
    dp = lax.axis_index("dp")
    bits = [(dp % 2).reshape(1, 1).astype(jnp.int32), (dp // 2).reshape(1, 1).astype(jnp.int32)]
    weight = jax.ShapeDtypeStruct((2, NB, BS, BS), f32)
    bias = jax.ShapeDtypeStruct((2, NB, BS), f32)
    return pl.pallas_call(
        gather_kernel,
        out_shape=(weight, bias, weight, bias),
        in_specs=[pl.BlockSpec(memory_space=pltpu.SMEM)] * 2 + vmem(4),
        out_specs=tuple(vmem(4)),
        scratch_shapes=[pltpu.VMEM((NB, ROWS, 128), f32)],
        compiler_params=pltpu.CompilerParams(vmem_limit_bytes=16 * 1024 * 1024),
        cost_estimate=pl.CostEstimate(flops=0, bytes_accessed=2_000_000, transcendentals=0),
    )(*bits, *sources)


def vmem(n):
    return [pl.BlockSpec(memory_space=pltpu.VMEM)] * n


def free(n):
    return [pl.BlockSpec(memory_space=pl.ANY)] * n


def held(*values):
    return [pltpu.VMEM(v.shape, v.dtype) for v in values]


def sems(*counts):
    return [pltpu.SemaphoreType.DMA((n,)) for n in counts]


def call(kernel, out_shape, args, scratch, flops, moved, place=vmem):
    outs = len(out_shape) if isinstance(out_shape, tuple) else 1
    return pl.pallas_call(
        kernel,
        out_shape=out_shape,
        in_specs=place(len(args)),
        out_specs=tuple(place(outs)) if isinstance(out_shape, tuple) else place(1)[0],
        scratch_shapes=scratch,
        compiler_params=BIG,
        cost_estimate=pl.CostEstimate(flops=flops, bytes_accessed=moved, transcendentals=0),
    )(*args)


def depth_forward(field, tables):
    args = (field.reshape(2048, C), tables)
    out = jax.ShapeDtypeStruct((NB, KZ, 2 * HALF, 128), f32)
    scratch = [*held(*args, out), pltpu.VMEM((2 * KZ, CELLS, C), f32), *sems(9, KZ)]
    return call(depth_kernel, out, args, scratch, 800_000_000, 5_000_000, free).reshape(SPECTRAL)


def backward(cot_spec, twiddle, plane_fwd, plane_bwd, first, second, slope, square):
    args = (cot_spec, twiddle, plane_fwd, plane_bwd, first, second, slope, square)
    outs = (GROUPED, jax.ShapeDtypeStruct((64, 2 * FIRST, 128), f32))
    scratch = [
        *held(*args, *outs),
        pltpu.VMEM(SPECTRAL, f32),
        pltpu.VMEM((64, 2 * FIRST, 128), f32),
        *sems(8, 5, *[GROUPS] * 3, 8),
    ]
    return call(backward_kernel, outs, args, scratch, 10_000_000_000, 20_000_000, free)


def by_group(n):
    return [pl.BlockSpec((1, 2 * BS, WIDE), lambda g: (g, 0, 0))] * n


def rest(spec, outer, grad_two, slope, second, first, twiddle, plane_bwd):
    return pl.pallas_call(
        rest_kernel,
        grid=(GROUPS,),
        out_shape=(
            jax.ShapeDtypeStruct((ROWS, 128), f32),
            jax.ShapeDtypeStruct((64, 2 * SECOND + 8, 128), f32),
        ),
        in_specs=by_group(4) + vmem(4),
        out_specs=(pl.BlockSpec((ROWS, 128), lambda g: (0, 0)), *free(1)),
        scratch_shapes=[
            *[pltpu.VMEM((2 * BS, 256), f32), pltpu.VMEM((256, WIDE), f32)] * 2,
            *[pltpu.VMEM((64, 2 * SECOND, 128), f32)] * 2,
            *sems(8),
        ],
        compiler_params=BIG,
        cost_estimate=pl.CostEstimate(
            flops=8_000_000_000, bytes_accessed=16_000_000, transcendentals=0
        ),
    )(spec, outer, grad_two, slope, second, first, twiddle, plane_bwd)


def field(first, second, cotangent, tables):
    args = (
        first.reshape(NB, KZ, 2 * FIRST, 128),
        second.reshape(NB, KZ, 2 * SECOND + 8, 128),
        cotangent.reshape(2048, C),
        tables,
    )
    out = jax.ShapeDtypeStruct((2048, C), bf16)
    scratch = [
        *held(args[0], jax.ShapeDtypeStruct((NB, KZ, 2 * SECOND, 128), f32), *args[2:], out),
        pltpu.VMEM((2 * KZ, CELLS, C), f32),
        *sems(KZ, KZ, 2, 8),
    ]
    return call(field_kernel, out, args, scratch, 1_200_000_000, 7_000_000, free)


def rows_of(weight, start, stop):
    return weight.reshape(4, HALF, 2 * BS)[:, start:stop].reshape(-1, 2 * BS)


def mixing(weight):
    real = weight[0].T
    imag = weight[1].T
    return jnp.concatenate(
        [jnp.concatenate([real, -imag], axis=1), jnp.concatenate([imag, real], axis=1)], axis=0
    )


def stacked(value):
    high = lax.reduce_precision(value, 8, 7)
    return thrice((high.astype(bf16), (value - high).astype(bf16)), 1)


def keep_half(value, axis, flip, bit):
    half = value.shape[0] // 2
    size = lax.axis_size(axis)
    mine = lax.dynamic_slice_in_dim(value, bit * half, half, 0)
    other = lax.dynamic_slice_in_dim(value, (1 - bit) * half, half, 0)
    return mine + lax.ppermute(other, axis, [(n, n ^ flip) for n in range(size)])


def owned_rows(rows):
    dp = lax.axis_index("dp")
    px = lax.axis_index("px")
    py = lax.axis_index("py")
    rows = keep_half(rows, "dp", 1, dp % 2)
    rows = keep_half(rows, "dp", 2, dp // 2)
    rows = keep_half(rows, "px", 1, px % 2)
    pieces = rows.reshape(8, -1, 128)
    total = lax.dynamic_index_in_dim(pieces, py, 0, keepdims=False)
    for offset in range(1, 8):
        piece = lax.dynamic_index_in_dim(pieces, (py + offset) % 8, 0, keepdims=False)
        total = total + lax.ppermute(piece, "py", [(n, (n + offset) % 8) for n in range(8)])
    return total


def partner(value, flip):
    return lax.ppermute(value, "dp", [(n, n ^ flip) for n in range(4)])


def exchange(value):
    return lax.all_to_all(value, ("px", "py"), split_axis=0, concat_axis=0, tiled=True)


def shards(state_field, cotangent, first_weight, first_bias, second_weight, second_bias):
    depth_fwd, depth_bwd = depth_tables()
    plane_fwd, plane_bwd = plane_tables()
    twiddle = twiddle_table()
    owner = lax.axis_index("px") * 8 + lax.axis_index("py")
    block = owner // KZ
    doubling = jnp.where(owner % KZ == 0, 1.0, 2.0).astype(f32).reshape(1, 1)

    first = mixing(lax.dynamic_index_in_dim(first_weight, block, 1, keepdims=False))
    second = mixing(lax.dynamic_index_in_dim(second_weight, block, 1, keepdims=False))
    bias_one = lax.dynamic_index_in_dim(first_bias, block, 1, keepdims=False).reshape(2 * BS, 1)
    bias_two = lax.dynamic_index_in_dim(second_bias, block, 1, keepdims=False).reshape(2 * BS, 1)

    state_spec = exchange(depth_forward(state_field, depth_fwd))
    cot_spec = exchange(depth_forward(cotangent, depth_fwd))
    spec, outer, slope, square = pl.pallas_call(
        forward_kernel,
        out_shape=(GROUPED,) * 4,
        in_specs=[pl.BlockSpec(memory_space=pltpu.SMEM)] + vmem(7),
        out_specs=tuple(vmem(4)),
        scratch_shapes=[pltpu.VMEM(SPECTRAL, f32)],
        compiler_params=BIG,
        cost_estimate=pl.CostEstimate(
            flops=8_000_000_000, bytes_accessed=16_000_000, transcendentals=1_500_000
        ),
    )(doubling, state_spec, twiddle, plane_fwd, stacked(first), bias_one, stacked(second), bias_two)

    second_back = stacked(second.T)
    grad_two, plane = backward(
        cot_spec,
        twiddle,
        plane_fwd,
        plane_bwd,
        stacked(rows_of(first.T, 0, FIRST)),
        second_back,
        slope,
        square,
    )
    first_part = exchange(plane)
    rows, plane = rest(
        spec, outer, grad_two, slope, second_back, stacked(rows_of(first.T, FIRST, HALF)), twiddle, plane_bwd
    )
    rows = owned_rows(rows)
    plane = lax.dynamic_update_slice(
        plane, jnp.broadcast_to(rows[None], (64, *rows.shape)), (0, 2 * SECOND, 0)
    )
    first_part, plane = lax.optimization_barrier((first_part, plane))
    second_part = exchange(plane)
    mine = second_part[:, 2 * SECOND :]
    across = partner(mine, 1)
    beside = partner(mine, 2)
    state_grad = field(first_part, second_part, cotangent, depth_bwd).reshape(1, 8, 8, NZ, C)
    state_grad, across, beside = lax.optimization_barrier((state_grad, across, beside))
    sums = gathered((mine, beside, across, partner(beside, 1)))
    return (state_grad, *sums)


def solution(mesh):
    in_specs = (
        P("dp", "px", "py", None, None),
        P("dp", "px", "py", None, None),
        P(),
        P(),
        P(),
        P(),
    )
    out_specs = (P("dp", "px", "py", None, None), P(), P(), P(), P())
    return jax.shard_map(shards, mesh=mesh, in_specs=in_specs, out_specs=out_specs, check_vma=False)
```
